512 devices in a mesh: freq: 64 (over x, y, core), rcv: 8 (over z).
Axes of the slice: x: 4, y: 8, z: 8, core: 2. Of those that a mesh axis runs over, the one named last changes fastest.
Arguments:
- focus_start: bfloat16 [16, 2048, 1024], P(None, ('rcv', 'freq')), may hold values from -6 to 6
- onset: int32 [16, 2048], P(None, ('rcv', 'freq')), may hold values from 128 to 383
- bins: int32 [64], replicated, may hold values from 0 to 63, each once
- refl_real: bfloat16 [64, 2048, 2048], P('freq', 'rcv'), may hold values from -0.09375 to 0.09375
- refl_imag: bfloat16 [64, 2048, 2048], P('freq', 'rcv'), may hold values from -0.09375 to 0.09375
Outputs:
- focus_plus: bfloat16 [16, 2048, 1024], P(None, ('rcv', 'freq'))
- focus_minus: bfloat16 [16, 2048, 1024], P(None, ('rcv', 'freq'))
The draws below stay inside these ranges and needn't reach their ends.
Inputs may be any that keep to these rules, and one draw needn't show every extreme that they name: `bins`: each value 0 to 63 appears once.
All inputs are finite; a program needn't handle non-finite values.
Results may differ from the reference program's by a relative error of at most 0.022.
Values may be sent and summed in bfloat16 or wider, within the bound.
No kernel may reach another device: no remote copies, remote signals or barrier semaphores. Data moves between devices by JAX's collectives and lax.ppermute only.
A program may use at most 64 MiB of HBM per device.

```python
import math
import jax
import jax.numpy as jnp
from jax import lax

NR = 2048
NT = 1024
FLO = 8
ITERS = 2
P_SIZE = 16
F = 64


def touch_ends(result, stream_key, smallest, largest):
    shape = result.shape
    spot = [jax.random.randint(jax.random.fold_in(stream_key, axis), (), 0, shape[axis]) for axis in range(len(shape))]
    result = result.at[tuple(spot)].set(smallest)
    longest = shape.index(max(shape))
    spot[longest] = (spot[longest] + 1) % shape[longest]
    return result.at[tuple(spot)].set(largest)


def shard_levels(stream_key, dims, shards, smallest, high):
    gain, own = 1.0, jax.random.fold_in(stream_key, 6)
    for dim, parts in shards:
        steps = jnp.exp(jax.random.uniform(jax.random.fold_in(own, dim), (parts,), jnp.float32, smallest / len(shards), high / len(shards)))
        gain = gain * jnp.repeat(steps, dims[dim] // parts).reshape([-1 if axis == dim else 1 for axis in range(len(dims))])
    return gain


def gaussian(stream_key, dims, deviation, reach, split=(), held_as=jnp.bfloat16):
    entries = deviation * jax.random.normal(stream_key, dims, jnp.float32)
    if split:
        entries = entries * shard_levels(stream_key, dims, split, -0.22, 0.18)
    return jnp.clip(entries, -reach, reach).astype(held_as)


def setup_inputs(seed: int = 0) -> dict:
    splits = jax.random.split(jax.random.key(seed), 6)
    focus_start = gaussian(splits[0], (P_SIZE, NR, NT), 1.0, 6.0, ((1, 512),))
    onset = touch_ends(jax.random.randint(splits[1], (P_SIZE, NR), NT // 8, 3 * NT // 8), jax.random.fold_in(splits[1], 1), NT // 8, (3 * NT // 8) - 1).astype(jnp.int32)
    bins = jax.random.permutation(splits[2], F).astype(jnp.int32)
    refl_real = gaussian(splits[3], (F, NR, NR), (2 * NR) ** -0.5, 0.09375, ((0, 64), (1, 8)))
    refl_imag = gaussian(splits[4], (F, NR, NR), (2 * NR) ** -0.5, 0.09375, ((0, 64), (1, 8)))
    return {"focus_start": focus_start, "onset": onset, "bins": bins, "refl_real": refl_real, "refl_imag": refl_imag}


def make_tables(bins, nsamp, nfreq):
    times = jnp.arange(nsamp, dtype=jnp.int32)
    waves = (FLO + bins).astype(jnp.int32)
    phase = times[:, None] * waves[None, :] % nsamp
    angle = phase.astype(jnp.float32) * jnp.float32(2.0 * math.pi / nsamp)
    forward = jnp.concatenate([jnp.cos(angle), -jnp.sin(angle)], axis=1) * jnp.float32(1.0 / math.sqrt(nsamp))
    inverse = jnp.concatenate([jnp.cos(angle).T, -jnp.sin(angle).T], axis=0) * jnp.float32(math.sqrt(2.0 / nfreq))
    return (forward.astype(jnp.bfloat16), inverse.astype(jnp.bfloat16))

def window_apply(values, onset):
    nsamp = values.shape[2]
    times = lax.broadcasted_iota(jnp.int32, (1, 1, nsamp), 2)
    keep = (times < onset[:, :, None]) | (times >= nsamp - onset[:, :, None])
    return jnp.where(keep, values, jnp.zeros_like(values))

def reference(focus_start, onset, bins, refl_real, refl_imag):
    forward, inverse = make_tables(bins, NT, F)

    def spectrum(traces):
        return jnp.dot(traces.reshape(P_SIZE * NR, NT), forward, preferred_element_type=jnp.float32).astype(jnp.bfloat16).reshape(P_SIZE, NR, 2 * F)

    def trace(spec):
        return jnp.dot(spec.reshape(P_SIZE * NR, 2 * F), inverse, preferred_element_type=jnp.float32).reshape(P_SIZE, NR, NT)

    def apply(spec, conjugate):
        real_part = jnp.transpose(spec[:, :, :F], (2, 0, 1))
        imag_part = jnp.transpose(spec[:, :, F:], (2, 0, 1))

        def one(items):
            rr, ri, xr, xi = items
            if conjugate:
                out_re = jnp.dot(xr, rr, preferred_element_type=jnp.float32) + jnp.dot(xi, ri, preferred_element_type=jnp.float32)
                out_im = jnp.dot(xi, rr, preferred_element_type=jnp.float32) - jnp.dot(xr, ri, preferred_element_type=jnp.float32)
            else:
                out_re = jnp.dot(xr, rr.T, preferred_element_type=jnp.float32) - jnp.dot(xi, ri.T, preferred_element_type=jnp.float32)
                out_im = jnp.dot(xi, rr.T, preferred_element_type=jnp.float32) + jnp.dot(xr, ri.T, preferred_element_type=jnp.float32)
            return (out_re.astype(jnp.bfloat16), out_im.astype(jnp.bfloat16))
        out_re, out_im = lax.map(one, (refl_real, refl_imag, real_part, imag_part))
        return jnp.concatenate([jnp.transpose(out_re, (1, 2, 0)), jnp.transpose(out_im, (1, 2, 0))], axis=2)
    focus_plus = focus_start
    focus_minus = focus_start
    for step in range(ITERS):
        focus_minus = window_apply(trace(apply(spectrum(focus_plus), False)), onset).astype(jnp.bfloat16)
        update = window_apply(trace(apply(spectrum(focus_minus), True)), onset)
        focus_plus = (focus_start.astype(jnp.float32) + update).astype(jnp.bfloat16)
    return (focus_plus, focus_minus)
```

```python
import math

import jax
import jax.numpy as jnp
import numpy as np
from jax import lax
from jax.sharding import Mesh
from jax.sharding import PartitionSpec as P

FLO = 8
ITERS = 2
NX, NY, NC, NZ = 4, 8, 2, 8
BF = jnp.bfloat16
F32 = jnp.float32
ONSET_MID = 256


def base_tables(nsamp, nfreq):
    waves = FLO + np.arange(nfreq)
    phase = (np.arange(nsamp)[None, :] * waves[:, None]) % nsamp
    angle = phase.astype(np.float32) * np.float32(2.0 * math.pi / nsamp)
    rows = np.concatenate([np.cos(angle), -np.sin(angle)], axis=0)
    return (
        (rows * np.float32(1.0 / math.sqrt(nsamp))).astype(BF),
        (rows * np.float32(math.sqrt(2.0 / nfreq))).astype(BF),
    )


def pick(slab_bins, nfreq):
    want = jnp.stack([slab_bins, slab_bins + nfreq], axis=1).reshape(1, -1)
    have = lax.broadcasted_iota(jnp.int32, (2 * nfreq, want.shape[1]), 0)
    return (have == want).astype(BF)


def dot(a, b, dims):
    return lax.dot_general(a, b, (dims, ((), ())), preferred_element_type=F32)


def exchange(values, axes):
    return lax.all_to_all(values, axes, 0, 0, tiled=True)


def shards(focus_start, onset, bins, refl_real, refl_imag):
    points, own, nsamp = focus_start.shape
    nfreq = bins.shape[0]
    rows, cols = refl_real.shape[1:]
    mat_re, mat_im = refl_real[0], refl_imag[0]
    ngrp = NX * NC
    sub = points // ngrp
    base_fwd, base_inv = base_tables(nsamp, nfreq)
    grid_bins = bins.reshape(NX, NY, NC)
    zi, yi = lax.axis_index("z"), lax.axis_index("y")

    fwd_start = dot(pick(grid_bins.transpose(1, 2, 0).reshape(-1), nfreq), base_fwd, ((0,), (0,))).astype(BF)
    order = pick(grid_bins.transpose(1, 0, 2).reshape(-1), nfreq)
    inv = dot(base_inv, order, ((0,), (0,))).astype(BF)
    mine = lax.dynamic_index_in_dim(grid_bins, yi, 1, keepdims=False).reshape(-1)
    fwd_mine = dot(pick(mine, nfreq), base_fwd, ((0,), (0,))).astype(BF)

    spec = dot(fwd_start, focus_start, ((1,), (2,))).astype(BF)
    spec = spec.reshape(NY * NC, NX * 2, points * own)
    marks = (onset - ONSET_MID).astype(BF).reshape(NX, NC, sub * own)
    marks = jnp.broadcast_to(marks.transpose(1, 0, 2)[None], (NY, NC, NX, sub * own))
    marks = marks.reshape(NY * NC, 1, NX * sub * own)
    marks = jnp.pad(marks, ((0, 0), (0, 0), (0, points * own - NX * sub * own)))
    got = exchange(jnp.concatenate([spec, marks], axis=1), ("y", "c"))
    half = NY * NC * own
    send = got[:, : NX * 2].reshape(NY * NC, NX, 2, ngrp, sub, own)
    send = send.transpose(1, 3, 2, 4, 0, 5).reshape(NX, 2 * points, half)
    marks = got[:, NX * 2, : NX * sub * own].reshape(NY * NC, NX, sub, own).transpose(1, 2, 0, 3).reshape(NX, sub, half)
    send = jnp.concatenate([send, marks], axis=1)[:, None]
    send = jnp.broadcast_to(send, (NX, NZ, 2 * points + sub, half))
    got = exchange(send.reshape(NX * NZ, 2 * points + sub, half), ("x", "z"))
    got = got.reshape(NX, NZ, 2 * points + sub, half)
    src0 = got[:, :, : 2 * points].transpose(2, 1, 0, 3).reshape(2 * points, cols)
    marks = lax.dynamic_index_in_dim(got[:, :, 2 * points :], zi, 1, keepdims=False)
    marks = marks.transpose(1, 0, 2).reshape(1, sub * rows).astype(jnp.int32) + ONSET_MID
    times = lax.broadcasted_iota(jnp.int32, (nsamp, 1), 0)
    keep = (times < marks) | (times >= nsamp - marks)

    def convolve(src):
        a = dot(src, mat_re, ((1,), (1,))).reshape(ngrp, 2, sub, rows)
        b = dot(src, mat_im, ((1,), (1,))).reshape(ngrp, 2, sub, rows)
        out = jnp.stack([a[:, 0] - b[:, 1], a[:, 1] + b[:, 0]], axis=1)
        return out.astype(BF)

    def correlate(src):
        turned = jnp.stack([src[:, 1], -src[:, 0]], axis=1).reshape(2 * points, rows)
        src = src.reshape(2 * points, rows)
        out = dot(src, mat_re, ((1,), (0,))) + dot(turned, mat_im, ((1,), (0,)))
        return out.astype(BF)

    def windowed(spectra):
        trace = dot(inv, spectra, ((1,), (0,)))
        trace = jnp.where(keep, trace, 0.0).astype(BF)
        return dot(fwd_mine, trace, ((1,), (0,))).astype(BF)

    def own_trace(spectra):
        flat = spectra.transpose(0, 2, 1, 3, 4).reshape(2 * nfreq, points * own)
        trace = dot(flat, inv, ((0,), (1,))).reshape(points, own, nsamp)
        when = lax.broadcasted_iota(jnp.int32, (1, 1, nsamp), 2)
        inside = (when < onset[:, :, None]) | (when >= nsamp - onset[:, :, None])
        return jnp.where(inside, trace, 0.0)

    src = src0
    for step in range(ITERS):
        last = step == ITERS - 1
        out = convolve(src)
        send = out.reshape(1, NX, NC, 2, sub * rows)
        send = jnp.broadcast_to(send, (NY, NX, NC, 2, sub * rows)).reshape(nfreq, 2 * sub * rows // 128, 128)
        if last:
            tail = out.reshape(2 * points, NX, NY, NC, own).transpose(2, 1, 3, 0, 4)
            send = jnp.concatenate([send, tail.reshape(nfreq, 2 * points * own // 128, 128)], axis=1)
        got = exchange(send, ("y", "x", "c"))
        if last:
            tail = got[:, 2 * sub * rows // 128 :].reshape(nfreq, ngrp, 2, sub, own)
            focus_minus = own_trace(tail).astype(BF)
            got = got[:, : 2 * sub * rows // 128]
        back = windowed(got.reshape(2 * nfreq, sub * rows))
        got = exchange(back.reshape(ngrp, 2, sub * rows), ("x", "c"))
        part = correlate(got.reshape(ngrp, 2, sub, rows))
        if not last:
            send = part.reshape(ngrp, 2 * sub, NZ, rows).transpose(0, 2, 1, 3)
            got = exchange(send.reshape(ngrp * NZ, 2 * sub, rows), ("x", "c", "z"))
            total = got.reshape(ngrp, NZ, 2, sub * rows).astype(F32).sum(axis=1).astype(BF)
            send = jnp.broadcast_to(total[None], (NY, ngrp, 2, sub * rows))
            got = exchange(send, "y")
            back = windowed(got.reshape(2 * nfreq, sub * rows))
            send = jnp.broadcast_to(back.reshape(ngrp, 1, 2, sub * rows), (ngrp, NZ, 2, sub * rows))
            got = exchange(send.reshape(ngrp * NZ, 2, sub * rows), ("x", "c", "z"))
            more = got.reshape(ngrp, NZ, 2 * sub, rows).transpose(0, 2, 1, 3).reshape(2 * points, cols)
            src = (src0.astype(F32) + more.astype(F32)).astype(BF)
    send = part.reshape(2 * points, NZ, NX, half).transpose(2, 1, 0, 3).reshape(NX * NZ, 2 * points, half)
    got = exchange(send, ("x", "z")).reshape(NX, NZ, 2 * points, half)
    total = got.astype(F32).sum(axis=1).astype(BF)
    send = total.reshape(NX, 2 * points, NY * NC, own).transpose(2, 0, 1, 3)
    got = exchange(send.reshape(NY * NC, NX, 2 * points * own), ("y", "c"))
    got = got.reshape(NY, NC, NX, ngrp, 2, sub, own).transpose(0, 2, 1, 3, 4, 5, 6)
    update = own_trace(got.reshape(nfreq, ngrp, 2, sub, own))
    focus_plus = (focus_start.astype(F32) + update).astype(BF)
    return (focus_plus, focus_minus)


def solution(mesh):
    fine = Mesh(mesh.devices.reshape(NX, NY, NC, NZ), ("x", "y", "c", "z"))
    receivers = ("z", "x", "y", "c")
    slabs = ("x", "y", "c")
    return jax.shard_map(
        shards,
        mesh=fine,
        in_specs=(
            P(None, receivers, None),
            P(None, receivers),
            P(),
            P(slabs, "z", None),
            P(slabs, "z", None),
        ),
        out_specs=(P(None, receivers, None), P(None, receivers, None)),
        check_vma=False,
    )
```

```python
import math

import jax
import jax.numpy as jnp
import numpy as np
from jax import lax
from jax.experimental import pallas as pl
from jax.experimental.pallas import tpu as pltpu
from jax.sharding import Mesh
from jax.sharding import PartitionSpec as P

FLO = 8
ITERS = 2
NX, NY, NC, NZ = 4, 8, 2, 8
NA, NG, NI = NY * NC, NX * NC, 4
NF, POINTS, NT = 64, 16, 1024
BLOCK, COLS = 256, 2048
LO, HI = 384, 640
KEPT = NT - (HI - LO)
ONSET_MID = 256
LANES = 128
BF, F32, I32 = jnp.bfloat16, jnp.float32, jnp.int32
VMEM_LIMIT = 8 * 1024 * 1024


def base_tables():
    phase = (np.arange(NT)[None, :] * (FLO + np.arange(NF))[:, None]) % NT
    angle = phase.astype(np.float32) * np.float32(2.0 * math.pi / NT)
    rows = np.concatenate([np.cos(angle), -np.sin(angle)], axis=0)
    forward = (rows * np.float32(1.0 / math.sqrt(NT))).astype(BF)
    inverse = (rows * np.float32(math.sqrt(2.0 / NF))).astype(BF)
    inverse = np.concatenate([inverse[:, :LO], inverse[:, HI:]], axis=1)
    return forward, np.ascontiguousarray(inverse.T)


def iota(shape, dim):
    return lax.broadcasted_iota(I32, shape, dim)


def grid(rows, cols):
    return iota((rows, cols), 0), iota((rows, cols), 1)


def hot(mask):
    return jnp.where(mask, jnp.float32(1), jnp.float32(0)).astype(BF)


def nn(a, b):
    return lax.dot_general(a, b, (((1,), (0,)), ((), ())), preferred_element_type=F32)


def nt(a, b):
    return lax.dot_general(a, b, (((1,), (1,)), ((), ())), preferred_element_type=F32)


def slab_of_bin(bins):
    k, _ = grid(NF, NF)
    return hot(k == bins)


def start_kernel(bins, onset, focus, base, out, flat):
    for p in range(POINTS):
        flat[NI * p : NI * (p + 1), :] = focus[p].astype(F32)
    rows = flat[...].astype(BF)
    none = jnp.zeros_like(rows)
    spec = nt(base[:NF], jnp.concatenate([rows, none], axis=0))
    spec = spec + nt(base[NF:], jnp.concatenate([none, rows], axis=0))
    m, j = grid(8 * NA, NF)
    place = hot(((m & 7) < NX) & (j == (m & 7) * NA + (m >> 3)))
    order = nt(place, slab_of_bin(bins[...])).astype(BF)
    sent = nn(order, spec.astype(BF))
    lane = iota((POINTS, LANES), 1)
    marks = jnp.zeros((POINTS, LANES), F32)
    for i in range(NI):
        marks = marks + jnp.where((lane & 63) == i, (onset[:, i : i + 1] - ONSET_MID).astype(F32), 0.0)
    m, p = grid(8 * NA, POINTS)
    group = ((m & 7) - NX) * NC + ((m >> 3) & 1)
    for h in range(2):
        mine = hot(((m & 7) >= NX) & (p == group + NG * h))
        sent = sent + nn(mine, jnp.where((lane >> 6) == h, marks, 0.0).astype(BF))
    out[...] = sent.reshape(NA, 8, LANES).astype(BF)


def tables_kernel(where, bins, forward, inverse, fwd, inv):
    holds = slab_of_bin(bins[...])
    j, f = grid(NF, NF)
    order = nn(holds, hot(j == ((f >> 1) & 3) * NA + (f >> 3) * NC + (f & 1))).astype(BF)
    r64, c128 = grid(NF, LANES)
    r128, c64 = grid(LANES, NF)
    both = jnp.zeros((LANES, LANES), F32)
    for part in range(2):
        wide = nn(order, hot(c128 == r64 + NF * part)).astype(BF)
        both = both + nn(hot(r128 == c64 + NF * part), wide)
    inv[...] = nn(inverse[...], both.astype(BF)).astype(BF)
    m, j = grid(2 * NG, NF)
    mine = hot(j == ((m & 7) >> 1) * NA + where[0] * NC + (m & 1))
    mine = nt(mine, holds).astype(BF)
    m, k = grid(2 * NG, LANES)
    wide = nn(mine, hot((c128 & 63) == r64))
    wide = jnp.where((k >> 6) == (m >> 3), wide, 0.0).astype(BF)
    fwd[:, :LO] = nn(wide, forward[:, :LO]).astype(BF)
    fwd[:, LO:] = nn(wide, forward[:, HI:]).astype(BF)


def middle_kernel(got, out, rows):
    rows[...] = got[...].astype(F32).reshape(8 * NA, LANES)
    line = jnp.concatenate([rows[pl.ds(e, NA, stride=8), :] for e in range(8)], axis=1).astype(BF)
    m, a = grid(NA * NI, NA)
    spread = nn(hot((m >> 2) == a), line)
    m, lane = grid(NA * NI, LANES)
    stacked = []
    for e in range(8):
        piece = spread[:, LANES * e : LANES * (e + 1)]
        for part in range(2):
            fits = ((lane & 3) == (m & 3)) & ((lane >> 6) == part)
            stacked.append(jnp.where(fits, piece, 0.0))
    stacked = jnp.concatenate(stacked, axis=0).astype(BF)
    p, lane = grid(POINTS, LANES)
    turned = nt(hot(((lane >> 2) & 15) == p), stacked)
    for x in range(NX):
        spec = turned[:, LANES * x : LANES * (x + 1)]
        mark = turned[:8, LANES * (NX + x) : LANES * (NX + x + 1)]
        message = jnp.concatenate([spec, mark], axis=0).astype(BF)
        for z in range(NZ):
            out[x, z] = message


def swap(a, b):
    lane = iota(a.shape, 1)
    low = lane < LANES // 2
    return (
        jnp.where(low, a, pltpu.roll(b, LANES // 2, 1)),
        jnp.where(low, pltpu.roll(a, LANES // 2, 1), b),
    )


def convolve(src, mat_re, mat_im, out, turn):
    a = nt(src, mat_re[...])
    b = nt(src, mat_im[...])
    parts = (a[:POINTS] - b[POINTS:], a[POINTS:] + b[:POINTS])
    for part in range(2):
        for h in range(2):
            for half in range(2):
                q = 4 * part + 2 * h + half
                turn[pl.ds(q, NG, stride=8), :] = parts[part][NG * h : NG * (h + 1), LANES * half : LANES * (half + 1)]
    message = turn[...].reshape(NG, 8, LANES).astype(BF)
    for y in range(NY):
        out[y] = message


def first_conv_kernel(where, got, mat_re, mat_im, out, src, marks, turn):
    for z in range(NZ):
        for half in range(2):
            a = got[2 * half, z].astype(F32)[:POINTS]
            b = got[2 * half + 1, z].astype(F32)[:POINTS]
            at = LANES * (2 * z + half)
            re, im = swap(a, b)
            src[:POINTS, at : at + LANES] = re.astype(BF)
            src[POINTS:, at : at + LANES] = im.astype(BF)
    for half in range(2):
        a = got[2 * half, where[1]].astype(F32)[POINTS:]
        b = got[2 * half + 1, where[1]].astype(F32)[POINTS:]
        for h, row in enumerate(swap(a, b)):
            at = LANES * (2 * h + half)
            marks[:, at : at + LANES] = row.astype(I32) + ONSET_MID
    convolve(src[...], mat_re, mat_im, out, turn)


def next_conv_kernel(got, first, mat_re, mat_im, out, rows, src, turn):
    rows[...] = got[...].astype(F32).reshape(NG * NZ * 8, LANES)
    for part in range(2):
        for z in range(NZ):
            for half in range(2):
                more = [rows[pl.ds(8 * z + 4 * part + 2 * h + half, NG, stride=8 * NZ), :] for h in range(2)]
                more = jnp.concatenate(more, axis=0)
                at = LANES * (2 * z + half)
                old = first[POINTS * part : POINTS * (part + 1), at : at + LANES].astype(F32)
                src[POINTS * part : POINTS * (part + 1), at : at + LANES] = (old + more).astype(BF)
    convolve(src[...], mat_re, mat_im, out, turn)


def window_traces(got, inv, fwd, marks, rows, turn):
    rows[...] = got[...].astype(F32).reshape(NF * 8, LANES)
    spectra = []
    for n in range(4):
        parts = [rows[pl.ds(4 * part + n, NF, stride=8), :] for part in range(2)]
        spectra.append(jnp.concatenate(parts, axis=0))
    spectra = jnp.concatenate(spectra, axis=1).astype(BF)
    trace = nn(inv[...], spectra)
    t = iota((KEPT, 1), 0)
    t = jnp.where(t < LO, t, t + (HI - LO))
    mark = marks[:1, :]
    trace = jnp.where((t < mark) | (t >= NT - mark), trace, 0.0).astype(BF)
    spec = nn(fwd[...], trace)
    for part in range(2):
        for n in range(4):
            turn[pl.ds(4 * part + n, NG, stride=8), :] = spec[NG * part : NG * (part + 1), LANES * n : LANES * (n + 1)]
    return spectra, turn[...].reshape(NG, 8, LANES)


def time_kernel(got, inv, fwd, marks, out, rows, turn):
    out[...] = window_traces(got, inv, fwd, marks, rows, turn)[1].astype(BF)


def time_copies_kernel(got, inv, fwd, marks, out, rows, turn):
    message = window_traces(got, inv, fwd, marks, rows, turn)[1].astype(BF)
    for z in range(NZ):
        out[:, z] = message


def last_time_kernel(where, got, inv, fwd, marks, out, rows, turn):
    spectra, message = window_traces(got, inv, fwd, marks, rows, turn)
    m, n = grid(8 * NG, 2 * BLOCK)
    own = ((m >> 2) & 1) * BLOCK + (m >> 4) * 64 + where[0] * 8 + ((m >> 3) & 1) * 4 + (m & 3)
    own = nt(hot(n == own), spectra).reshape(NG, 8, LANES)
    out[...] = jnp.concatenate([message, own], axis=1).astype(BF)


def correlate(got, mat_re, mat_im, rows, height):
    rows[...] = got[...].astype(F32).reshape(NG * height, LANES)
    parts = []
    for part in range(2):
        halves = []
        for half in range(2):
            both = [rows[pl.ds(4 * part + 2 * h + half, NG, stride=height), :] for h in range(2)]
            halves.append(jnp.concatenate(both, axis=0))
        parts.append(jnp.concatenate(halves, axis=1))
    straight = jnp.concatenate(parts, axis=0).astype(BF)
    turned = jnp.concatenate([parts[1], -parts[0]], axis=0).astype(BF)
    for z in range(NZ):
        at = slice(BLOCK * z, BLOCK * (z + 1))
        yield z, nn(straight, mat_re[:, at]) + nn(turned, mat_im[:, at])


def corr_kernel(got, mat_re, mat_im, out, rows, turn):
    for z, block in correlate(got, mat_re, mat_im, rows, 8):
        for part in range(2):
            for h in range(2):
                for half in range(2):
                    q = 4 * part + 2 * h + half
                    at = POINTS * part + NG * h
                    turn[pl.ds(8 * z + q, NG, stride=8 * NZ), :] = block[at : at + NG, LANES * half : LANES * (half + 1)]
    out[...] = turn[...].reshape(NG * NZ, 8, LANES).astype(BF)


def last_corr_kernel(got, mat_re, mat_im, out, rows):
    for z, block in correlate(got, mat_re, mat_im, rows, 16):
        for half in range(2):
            at = slice(LANES * half, LANES * (half + 1))
            a, b = swap(block[:POINTS, at], block[POINTS:, at])
            out[2 * half, z] = a.astype(BF)
            out[2 * half + 1, z] = b.astype(BF)


def sum_kernel(got, out):
    total = got[...].astype(F32).reshape(NG, NZ, 8, LANES).sum(axis=1)
    total = total.reshape(NG * 8, LANES).astype(BF)
    for y in range(NY):
        out[y] = total


def last_sum_kernel(got, out):
    total = got[...].astype(F32).sum(axis=1).astype(BF)
    p, lane = grid(POINTS, LANES)
    spread = hot(((lane >> 2) & 15) == p)
    m, lane = grid(LANES, LANES)
    fits = ((lane & 3) == (m & 3)) & ((lane >> 6) == (m >> 6))
    sent = jnp.zeros((8 * NA, LANES), F32)
    for x in range(NX):
        turned = nn(total[x].astype(F32).T.astype(BF), spread)
        turned = jnp.where(fits, turned, 0.0).astype(BF)
        pick = hot(((m & 7) == x) & ((m >> 3) == ((lane >> 2) & 15)))
        sent = sent + nn(pick, turned)
    out[...] = sent.reshape(NA, 8, LANES).astype(BF)


def keep_own(trace, onset, p):
    t = iota((NI, KEPT), 1)
    t = jnp.where(t < LO, t, t + (HI - LO))
    mark = onset[:, p : p + 1]
    return jnp.where((t < mark) | (t >= NT - mark), trace, 0.0)


def minus_kernel(got, inv, onset, out):
    own = got[...].astype(F32)[:, 8:].reshape(8 * NG, LANES).astype(BF)
    trace = nt(own, inv[...])
    for p in range(POINTS):
        at = 8 * (p % NG) + NI * (p // NG)
        kept = keep_own(trace[at : at + NI], onset, p).astype(BF)
        out[p, :, :LO] = kept[:, :LO]
        out[p, :, LO:HI] = jnp.zeros((NI, HI - LO), BF)
        out[p, :, HI:] = kept[:, LO:]


def plus_kernel(got, inv, onset, focus, out):
    rows = got[...].astype(F32).reshape(8 * NA, LANES).T.astype(BF)
    m, k = grid(8 * NA, LANES)
    arrival = ((m >> 4) << 3) + ((m & 7) << 1) + ((m >> 3) & 1)
    spectra = jnp.zeros((POINTS * NI, LANES), F32)
    for part in range(2):
        place = hot(((m & 7) < NX) & (k == arrival + NF * part))
        spectra = spectra + nn(rows[NF * part : NF * (part + 1)], place)
    trace = nt(spectra.astype(BF), inv[...])
    for p in range(POINTS):
        kept = keep_own(trace[NI * p : NI * (p + 1)], onset, p)
        start = focus[p]
        out[p, :, :LO] = (start[:, :LO].astype(F32) + kept[:, :LO]).astype(BF)
        out[p, :, LO:HI] = start[:, LO:HI]
        out[p, :, HI:] = (start[:, HI:].astype(F32) + kept[:, LO:]).astype(BF)


def call(kernel, outs, scratch=(), scalars=0):
    single = not isinstance(outs, list)
    shapes = [jax.ShapeDtypeStruct(shape, dtype) for shape, dtype in ([outs] if single else outs)]

    def run(*args):
        specs = [pl.BlockSpec(memory_space=pltpu.SMEM if n < scalars else pltpu.VMEM) for n in range(len(args))]
        got = pl.pallas_call(
            kernel,
            out_shape=shapes,
            in_specs=specs,
            out_specs=[pl.BlockSpec(memory_space=pltpu.VMEM)] * len(shapes),
            scratch_shapes=[pltpu.VMEM(shape, dtype) for shape, dtype in scratch],
            compiler_params=pltpu.CompilerParams(vmem_limit_bytes=VMEM_LIMIT),
        )(*args)
        return got[0] if single else got

    return run


def exchange(values, axes):
    return lax.all_to_all(values, axes, 0, 0, tiled=True)


def shards(focus_start, onset, bins, refl_real, refl_imag):
    mats = (refl_real[0], refl_imag[0])
    where = jnp.stack([lax.axis_index("y"), lax.axis_index("z")]).astype(I32)
    bins = bins.reshape(1, NF)
    onset_turned = onset.T
    forward, inverse = base_tables()
    full = ((8 * NF, LANES), F32)
    small = ((8 * NG, LANES), F32)

    send = call(start_kernel, ((NA, 8, LANES), BF), [((POINTS * NI, NT), F32)])(bins, onset, focus_start, forward)
    got = exchange(send, ("y", "c"))
    fwd, inv = call(tables_kernel, [((2 * NG, KEPT), BF), ((KEPT, LANES), BF)], scalars=1)(where, bins, forward, inverse)
    send = call(middle_kernel, ((NX, NZ, POINTS + 8, LANES), BF), [((8 * NA, LANES), F32)])(got)
    got = exchange(send.reshape(NX * NZ, POINTS + 8, LANES), ("x", "z")).reshape(NX, NZ, POINTS + 8, LANES)
    outs = [((NY, NG, 8, LANES), BF), ((2 * POINTS, COLS), BF), ((8, 2 * BLOCK), I32)]
    send, first, marks = call(first_conv_kernel, outs, [small], scalars=1)(where, got, *mats)
    for step in range(ITERS):
        got = exchange(send.reshape(NF, 8, LANES), ("y", "x", "c"))
        if step == ITERS - 1:
            send = call(last_time_kernel, ((NG, 16, LANES), BF), [full, small], scalars=1)(where, got, inv, fwd, marks)
            got = exchange(send, ("x", "c"))
            focus_minus = call(minus_kernel, ((POINTS, NI, NT), BF))(got, inv, onset_turned)
            break
        send = call(time_kernel, ((NG, 8, LANES), BF), [full, small])(got, inv, fwd, marks)
        got = exchange(send, ("x", "c"))
        send = call(corr_kernel, ((NG * NZ, 8, LANES), BF), [small, full])(got, *mats)
        got = exchange(send, ("x", "c", "z"))
        send = call(sum_kernel, ((NY, NG * 8, LANES), BF))(got)
        got = exchange(send, "y")
        send = call(time_copies_kernel, ((NG, NZ, 8, LANES), BF), [full, small])(got, inv, fwd, marks)
        got = exchange(send.reshape(NG * NZ, 8, LANES), ("x", "c", "z"))
        scratch = [full, ((2 * POINTS, COLS), BF), small]
        send = call(next_conv_kernel, ((NY, NG, 8, LANES), BF), scratch)(got, first, *mats)
    send = call(last_corr_kernel, ((NX, NZ, POINTS, LANES), BF), [((16 * NG, LANES), F32)])(got, *mats)
    got = exchange(send.reshape(NX * NZ, POINTS, LANES), ("x", "z")).reshape(NX, NZ, POINTS, LANES)
    send = call(last_sum_kernel, ((NA, 8, LANES), BF))(got)
    got = exchange(send, ("y", "c"))
    focus_plus = call(plus_kernel, ((POINTS, NI, NT), BF))(got, inv, onset_turned, focus_start)
    return (focus_plus, focus_minus)


def solution(mesh):
    fine = Mesh(mesh.devices.reshape(NX, NY, NC, NZ), ("x", "y", "c", "z"))
    receivers = ("z", "x", "y", "c")
    slabs = ("x", "y", "c")
    return jax.shard_map(
        shards,
        mesh=fine,
        in_specs=(
            P(None, receivers, None),
            P(None, receivers),
            P(),
            P(slabs, "z", None),
            P(slabs, "z", None),
        ),
        out_specs=(P(None, receivers, None), P(None, receivers, None)),
        check_vma=False,
    )
```

```python
import math

import jax
import jax.numpy as jnp
import numpy as np
from jax import lax
from jax.experimental import pallas as pl
from jax.experimental.pallas import tpu as pltpu
from jax.sharding import Mesh
from jax.sharding import PartitionSpec as P

FLO = 8
ITERS = 2
NX, NY, NC, NZ = 4, 8, 2, 8
NA, NG, NI = NY * NC, NX * NC, 4
NF, POINTS, NT = 64, 16, 1024
BLOCK, COLS = 256, 2048
LANES = 128
SPANS = ((128, 384), (640, 896), (0, 128), (896, 1024))
CUT = 512
KEPT = 768
ONSET_MID = 256
BF, F32, I32 = jnp.bfloat16, jnp.float32, jnp.int32
VMEM_LIMIT = 8 * 1024 * 1024


def base_tables():
    phase = (np.arange(NT)[None, :] * (FLO + np.arange(NF))[:, None]) % NT
    angle = phase.astype(np.float32) * np.float32(2.0 * math.pi / NT)
    rows = np.concatenate([np.cos(angle), -np.sin(angle)], axis=0)
    forward = (rows * np.float32(1.0 / math.sqrt(NT))).astype(BF)
    inverse = (rows * np.float32(math.sqrt(2.0 / NF))).astype(BF)
    inverse = np.concatenate([inverse[:, a:b] for a, b in SPANS], axis=1)
    wide = np.concatenate([forward[:NF], forward[NF:]], axis=1)
    return forward, wide, np.ascontiguousarray(inverse.T)


def iota(shape, dim):
    return lax.broadcasted_iota(I32, shape, dim)


def grid(rows, cols):
    return iota((rows, cols), 0), iota((rows, cols), 1)


def hot(mask):
    return jnp.where(mask, jnp.float32(1), jnp.float32(0)).astype(BF)


def nn(a, b):
    return lax.dot_general(a, b, (((1,), (0,)), ((), ())), preferred_element_type=F32)


def nt(a, b):
    return lax.dot_general(a, b, (((1,), (1,)), ((), ())), preferred_element_type=F32)


def two_terms(value):
    high = value.astype(BF)
    return high, (value - high.astype(F32)).astype(BF)


def slab_of_bin(bins):
    row, _ = grid(NF, NF)
    return hot(row == bins)


def fetch(pairs, sems):
    copies = [pltpu.make_async_copy(src, dst, sems.at[n]) for n, (src, dst) in enumerate(pairs)]
    for copy in copies:
        copy.start()
    return copies


def start_kernel(bins_in, onset_in, focus_in, base_in, out, bins, onset, focus, base, flat, sems):
    copies = fetch([(bins_in, bins), (onset_in, onset), (focus_in, focus), (base_in, base)], sems)
    copies[0].wait()
    m, j = grid(8 * NA, NF)
    place = hot(((m & 7) < NX) & (j == ((m & 7) << 4) + (m >> 3)))
    order = nt(place, slab_of_bin(bins[...])).astype(BF)
    copies[1].wait()
    p, lane = grid(POINTS, LANES)
    spread = hot((((lane >> 2) & 15) == p) & ((lane >> 6) == (p >> 3)))
    marks = nn((onset[...] - ONSET_MID).astype(F32).astype(BF), spread)
    i, lane = grid(NI, LANES)
    marks = jnp.where((lane & 3) == i, marks, 0.0).sum(axis=0, keepdims=True)
    copies[2].wait()
    for p in range(POINTS):
        flat[NI * p : NI * (p + 1), :] = focus[p].astype(F32)
    rows = flat[...].astype(BF)
    none = jnp.zeros_like(rows)
    copies[3].wait()
    spec = nt(base[:, :NT], jnp.concatenate([rows, none], axis=0))
    spec = spec + nt(base[:, NT:], jnp.concatenate([none, rows], axis=0))
    sent = nn(order, spec.astype(BF))
    sent = jnp.where((iota((8 * NA, LANES), 0) & 7) == NX, marks, sent)
    out[...] = sent.reshape(NA, 8, LANES).astype(BF)


def tables_kernel(
    where, bins_in, forward_in, inverse_in, re_in, im_in, inv, own_inv, turned_inv, fwd, own_fwd, fixed, own_fixed, re, im,
    bins, forward, inverse, sems,
):
    pairs = [(bins_in, bins), (forward_in, forward), (inverse_in, inverse), (re_in, re), (im_in, im)]
    copies = fetch(pairs, sems)
    for copy in copies[:3]:
        copy.wait()
    x, y, c = where[0], where[1], where[2]
    holds = slab_of_bin(bins[...])
    j, k = grid(NF, LANES)
    arrival = hot(j == ((k >> 5) << 4) + (k & 15))
    order = nn(holds, arrival)
    _, k = grid(NF, LANES)
    part = (k >> 4) & 1
    order = jnp.concatenate([jnp.where(part == 0, order, 0.0), jnp.where(part == 1, order, 0.0)], axis=0)
    table = nn(inverse[...], order.astype(BF)).astype(BF)
    inv[...] = table
    k, n = grid(LANES, 2 * NA)
    mine = hot(k == 2 * NA * x + n)
    own_inv[...] = nn(table[:CUT], mine).astype(BF)
    k, n = grid(LANES, LANES)
    turn = hot(k == ((n >> 4) << 4) + ((n & 7) << 1) + ((n >> 3) & 1))
    turned_inv[...] = nn(table[:CUT], turn).astype(BF)
    m, j = grid(2 * NG, NF)
    slabs = hot(j == (((m & 7) >> 1) << 4) + (y << 1) + (m & 1))
    slabs = nt(slabs, holds)
    m, _ = grid(2 * NG, NF)
    pick = jnp.concatenate([jnp.where(m < NG, slabs, 0.0), jnp.where(m < NG, 0.0, slabs)], axis=1)
    picked = nn(pick.astype(BF), forward[...]).astype(BF)
    picked = jnp.concatenate([picked[:, a:b] for a, b in SPANS], axis=1)
    m, n = grid(2 * NX, 2 * NG)
    mine_rows = hot(n == ((m >> 2) << 3) + ((m & 3) << 1) + c)
    ours = nn(mine_rows, picked).astype(BF)
    fwd[...] = picked[:, :CUT]
    own_fwd[...] = ours[:, :CUT]
    all_fixed = nn(picked[:, CUT:], table[CUT:])
    for n, term in enumerate(two_terms(all_fixed)):
        fixed[n] = nn(term, mine).astype(BF)
    for n, term in enumerate(two_terms(nn(ours[:, CUT:], table[CUT:]))):
        own_fixed[n] = nn(term, turn).astype(BF)
    copies[3].wait()
    copies[4].wait()


def middle_kernel(got, out, rows):
    rows[...] = got[...].astype(F32).reshape(8 * NA, LANES)
    line = jnp.concatenate([rows[pl.ds(e, NA, stride=8), :] for e in range(NX + 1)], axis=1).astype(BF)
    m, a = grid(NA * NI, NA)
    spread = nn(hot((m >> 2) == a), line)
    m, lane = grid(NA * NI, LANES)
    stacked = []
    for e in range(NX + 1):
        piece = spread[:, LANES * e : LANES * (e + 1)]
        for part in range(2):
            fits = ((lane & 3) == (m & 3)) & ((lane >> 6) == part)
            stacked.append(jnp.where(fits, piece, 0.0))
    stacked = jnp.concatenate(stacked, axis=0).astype(BF)
    p, lane = grid(POINTS, LANES)
    turned = nt(hot(((lane >> 2) & 15) == p), stacked)
    marks = turned[:8, LANES * NX :] + turned[8:, LANES * NX :]
    for x in range(NX):
        message = jnp.concatenate([turned[:, LANES * x : LANES * (x + 1)], marks], axis=0).astype(BF)
        for z in range(NZ):
            out[x, z] = message


def swap(a, b):
    low = iota(a.shape, 1) < LANES // 2
    return (
        jnp.where(low, a, pltpu.roll(b, LANES // 2, 1)),
        jnp.where(low, pltpu.roll(a, LANES // 2, 1), b),
    )


def convolve(src, mat_re, mat_im, out):
    a = nt(src, mat_re[...])
    b = nt(src, mat_im[...])
    parts = (a[:POINTS] - b[POINTS:], a[POINTS:] + b[:POINTS])
    for c in range(NC):
        at = slice(8 * c, 8 * (c + 1))
        slabs = [part[at, LANES * half : LANES * (half + 1)] for part in parts for half in range(2)]
        message = jnp.concatenate(slabs, axis=0).astype(BF)
        for y in range(NY):
            out[y, c] = message


def first_conv_kernel(where, got, mat_re, mat_im, out, src, marks, rows):
    height = POINTS + 8
    rows[...] = got[...].astype(F32).reshape(NX * NZ * height, LANES)
    for z in range(NZ):
        for half in range(2):
            a = rows[pl.ds((2 * half * NZ + z) * height, POINTS), :]
            b = rows[pl.ds(((2 * half + 1) * NZ + z) * height, POINTS), :]
            at = LANES * (2 * z + half)
            re, im = swap(a, b)
            src[:POINTS, at : at + LANES] = re.astype(BF)
            src[POINTS:, at : at + LANES] = im.astype(BF)
    for half in range(2):
        at = (2 * half * NZ + where[3]) * height + POINTS
        a = rows[pl.ds(pl.multiple_of(at, 8), 8), :]
        b = rows[pl.ds(pl.multiple_of(at + NZ * height, 8), 8), :]
        for h, block in enumerate(swap(a, b)):
            marks[8 * h : 8 * (h + 1), LANES * half : LANES * (half + 1)] = block.astype(I32) + ONSET_MID
    convolve(src[...], mat_re, mat_im, out)


def next_conv_kernel(got, first, mat_re, mat_im, out, rows, more):
    rows[...] = got[...].astype(F32).reshape(NX * NZ * 16, LANES)
    for x in range(NX):
        for z in range(NZ):
            for part in range(2):
                for half in range(2):
                    at = (x * NZ + z) * 16 + (2 * part + half) * 4
                    lanes = slice(LANES * (2 * z + half), LANES * (2 * z + half + 1))
                    more[POINTS * part + 4 * x : POINTS * part + 4 * (x + 1), lanes] = rows[at : at + 4, :]
    src = (first[...].astype(F32) + more[...]).astype(BF)
    convolve(src, mat_re, mat_im, out)


def window(spectra, marks, inv, fwd, fixed):
    t = iota((BLOCK, 1), 0)
    front = jnp.where(t + SPANS[0][0] < marks, nn(inv[:BLOCK], spectra), 0.0).astype(BF)
    back = jnp.where(t + SPANS[1][0] >= NT - marks, nn(inv[BLOCK:], spectra), 0.0).astype(BF)
    spec = nn(fwd[:, :BLOCK], front) + nn(fwd[:, BLOCK:], back)
    return spec + nn(fixed[0], spectra) + nn(fixed[1], spectra)


def points_window(marks, first, count, every, inv, fwd, fixed):
    mark = jnp.concatenate([marks[pl.ds(first + p, 1), :] for p in range(count)], axis=1)
    spec = window(jnp.concatenate(every, axis=1), mark, inv, fwd, fixed)
    return [spec[:, BLOCK * p : BLOCK * (p + 1)] for p in range(count)]


def window_slabs(where, got, inv, fwd, fixed, marks, rows, turn):
    rows[...] = got[...].astype(F32).reshape(NA * 32, LANES)
    every = []
    for p in range(8):
        parts = []
        for part in range(2):
            halves = [rows[pl.ds(16 * part + 8 * half + p, NA, stride=32), :] for half in range(2)]
            parts.append(jnp.concatenate(halves, axis=1))
        every.append(jnp.concatenate(parts, axis=0).astype(BF))
    for p, spec in enumerate(points_window(marks, 8 * where[2], 8, every, inv, fwd, fixed)):
        for part in range(2):
            for half in range(2):
                at = 16 * part + 8 * half + p
                slab = spec[NG * part : NG * (part + 1), LANES * half : LANES * (half + 1)]
                turn[pl.ds(at, NG, stride=32), :] = slab
    return every, turn[...].reshape(NG, 32, LANES)


def time_kernel(where, got, inv, fwd, fixed, marks, out, rows, turn):
    out[...] = window_slabs(where, got, inv, fwd, fixed, marks, rows, turn)[1].astype(BF)


def last_time_kernel(where, got, inv, fwd, fixed, marks, out, rows, turn, tail):
    every, message = window_slabs(where, got, inv, fwd, fixed, marks, rows, turn)
    m, r = grid(NG * NI, BLOCK)
    own = hot(r == ((m >> 3) << 6) + (where[1] << 3) + (((m >> 2) & 1) << 2) + (m & 3))
    taken = [nt(own, spectra) for spectra in every]
    taken = jnp.concatenate(taken, axis=0).astype(BF)
    n, k = grid(2 * NA, LANES)
    taken = nn(taken, hot(k == 2 * NA * where[0] + n))
    for p in range(8):
        for g in range(NG):
            at = NG * NI * p + NI * g
            tail[32 * g + NI * p : 32 * g + NI * (p + 1), :] = taken[at : at + NI]
    own = tail[...].reshape(NG, 32, LANES)
    out[...] = jnp.concatenate([message, own], axis=1).astype(BF)


def time_copies_kernel(where, got, inv, fwd, fixed, marks, out, rows, turn):
    rows[...] = got[...].astype(F32).reshape(NF * 16, LANES)
    every = []
    for p in range(4):
        parts = []
        for x in range(NX):
            for part in range(2):
                at = [16 * x + 8 * part + 4 * half + p for half in range(2)]
                halves = [rows[pl.ds(n, NA, stride=16 * NX), :] for n in at]
                parts.append(jnp.concatenate(halves, axis=1))
        every.append(jnp.concatenate(parts, axis=0).astype(BF))
    for p, spec in enumerate(points_window(marks, 4 * where[0], 4, every, inv, fwd, fixed)):
        for part in range(2):
            for half in range(2):
                slab = spec[NX * part : NX * (part + 1), LANES * half : LANES * (half + 1)]
                turn[pl.ds(8 * part + 4 * half + p, NX, stride=16), :] = slab
    message = turn[...].reshape(NX, 16, LANES).astype(BF)
    for z in range(NZ):
        out[:, z] = message


def correlate(got, mat_re, mat_im):
    parts = []
    for part in range(2):
        halves = []
        for half in range(2):
            at = 8 * (2 * part + half)
            both = [sum(got[NC * x + c].astype(F32)[at : at + 8] for x in range(NX)) for c in range(NC)]
            halves.append(jnp.concatenate(both, axis=0))
        parts.append(jnp.concatenate(halves, axis=1))
    straight = jnp.concatenate(parts, axis=0).astype(BF)
    turned = jnp.concatenate([parts[1], -parts[0]], axis=0).astype(BF)
    for z in range(NZ):
        at = slice(BLOCK * z, BLOCK * (z + 1))
        yield z, nn(straight, mat_re[:, at]) + nn(turned, mat_im[:, at])


def corr_kernel(got, mat_re, mat_im, out, turn):
    for z, block in correlate(got, mat_re, mat_im):
        for x in range(NX):
            for part in range(2):
                for half in range(2):
                    at = (x * NZ + z) * 16 + (2 * part + half) * 4
                    row = POINTS * part + 4 * x
                    turn[at : at + 4, :] = block[row : row + 4, LANES * half : LANES * (half + 1)]
    out[...] = turn[...].reshape(NX * NZ, 16, LANES).astype(BF)


def last_corr_kernel(got, mat_re, mat_im, out):
    for z, block in correlate(got, mat_re, mat_im):
        for half in range(2):
            at = slice(LANES * half, LANES * (half + 1))
            a, b = swap(block[:POINTS, at], block[POINTS:, at])
            out[2 * half, z] = a.astype(BF)
            out[2 * half + 1, z] = b.astype(BF)


def sum_kernel(got, out):
    total = got[...].astype(F32).reshape(NX, NZ, 16, LANES).sum(axis=1)
    total = total.reshape(NX * 16, LANES).astype(BF)
    for y in range(NY):
        out[y] = total


def last_sum_kernel(got, out):
    total = got[...].astype(F32).sum(axis=1)
    turned = jnp.concatenate([total[x].T for x in range(NX)], axis=0).astype(BF)
    p, lane = grid(POINTS, LANES)
    turned = nn(turned, hot(((lane >> 2) & 15) == p))
    m, lane = grid(NX * LANES, LANES)
    turned = jnp.where(((lane & 3) == (m & 3)) & ((lane >> 6) == ((m >> 6) & 1)), turned, 0.0).astype(BF)
    m, n = grid(8 * NA, NX * LANES)
    sent = nn(hot(((m & 7) == (n >> 7)) & ((m >> 3) == ((n >> 2) & 15))), turned)
    out[...] = sent.reshape(NA, 8, LANES).astype(BF)


def keep_own(trace, onset, p):
    t = iota((NI, BLOCK), 1)
    mark = onset[:, p : p + 1]
    front = jnp.where(t + SPANS[0][0] < mark, trace[:, :BLOCK], 0.0)
    back = jnp.where(t + SPANS[1][0] >= NT - mark, trace[:, BLOCK:CUT], 0.0)
    return front, back, trace[:, CUT : CUT + LANES], trace[:, CUT + LANES :]


def minus_kernel(got, inv, onset, out):
    own = [sum(got[NC * x + c].astype(F32)[32:] for x in range(NX)) for c in range(NC)]
    own = jnp.concatenate(own, axis=0).astype(BF)
    trace = nt(own, inv[...])
    for p in range(POINTS):
        for (a, b), piece in zip(SPANS, keep_own(trace[NI * p : NI * (p + 1)], onset, p)):
            out[p, :, a:b] = piece.astype(BF)
        out[p, :, 384:640] = jnp.zeros((NI, BLOCK), BF)


def plus_kernel(got, inv, onset, focus, out):
    rows = got[...].astype(F32).reshape(8 * NA, LANES).T.astype(BF)
    m, k = grid(8 * NA, LANES)
    spectra = jnp.zeros((POINTS * NI, LANES), F32)
    for part in range(2):
        place = hot(((m & 7) < NX) & (k == ((m & 7) << 5) + 16 * part + (m >> 3)))
        spectra = spectra + nn(rows[NF * part : NF * (part + 1)], place)
    trace = nt(spectra.astype(BF), inv[...])
    for p in range(POINTS):
        for (a, b), piece in zip(SPANS, keep_own(trace[NI * p : NI * (p + 1)], onset, p)):
            out[p, :, a:b] = (focus[p, :, a:b].astype(F32) + piece).astype(BF)
        out[p, :, 384:640] = focus[p, :, 384:640]


def call(kernel, outs, scratch=(), scalars=0, far=0, copies=0):
    single = not isinstance(outs, list)
    shapes = [jax.ShapeDtypeStruct(shape, dtype) for shape, dtype in ([outs] if single else outs)]

    def run(*args):
        spaces = [pltpu.SMEM] * scalars + [pltpu.HBM] * far + [pltpu.VMEM] * (len(args) - scalars - far)
        args = [
            pltpu.with_memory_space_constraint(arg, pltpu.HBM) if space is pltpu.HBM else arg
            for arg, space in zip(args, spaces)
        ]
        got = pl.pallas_call(
            kernel,
            out_shape=shapes,
            in_specs=[pl.BlockSpec(memory_space=space) for space in spaces],
            out_specs=[pl.BlockSpec(memory_space=pltpu.VMEM)] * len(shapes),
            scratch_shapes=[pltpu.VMEM(shape, dtype) for shape, dtype in scratch]
            + [pltpu.SemaphoreType.DMA((copies,))] * (copies > 0),
            compiler_params=pltpu.CompilerParams(vmem_limit_bytes=VMEM_LIMIT),
        )(*args)
        return got[0] if single else got

    return run


def exchange(values, axes):
    return lax.all_to_all(values, axes, 0, 0, tiled=True)


def shards(focus_start, onset, bins, refl_real, refl_imag):
    mats = (refl_real[0], refl_imag[0])
    where = jnp.stack([lax.axis_index(axis) for axis in ("x", "y", "c", "z")]).astype(I32)
    bins = bins.reshape(1, NF)
    onset = onset.T
    forward, wide, inverse = base_tables()
    own = (POINTS, NI, NT)

    scratch = [((1, NF), I32), ((NI, POINTS), I32), (own, BF), ((NF, 2 * NT), BF), ((POINTS * NI, NT), F32)]
    run = call(start_kernel, ((NA, 8, LANES), BF), scratch, far=4, copies=4)
    got = exchange(run(bins, onset, focus_start, wide), ("y", "c"))
    send = call(middle_kernel, ((NX, NZ, POINTS + 8, LANES), BF), [((8 * NA, LANES), F32)])(got)
    outs = [((KEPT, LANES), BF), ((CUT, 2 * NA), BF), ((CUT, LANES), BF), ((2 * NG, CUT), BF), ((2 * NX, CUT), BF)]
    outs += [((2, 2 * NG, 2 * NA), BF), ((2, 2 * NX, LANES), BF), ((BLOCK, COLS), BF), ((BLOCK, COLS), BF)]
    scratch = [((1, NF), I32), ((2 * NF, NT), BF), ((KEPT, LANES), BF)]
    run = call(tables_kernel, outs, scratch, scalars=1, far=5, copies=5)
    inv, own_inv, turned_inv, fwd, own_fwd, fixed, own_fixed, *mats = run(where, bins, forward, inverse, *mats)
    got = exchange(send.reshape(NX * NZ, POINTS + 8, LANES), ("x", "z"))
    outs = [((NY, NC, 32, LANES), BF), ((2 * POINTS, COLS), BF), ((POINTS, BLOCK), I32)]
    scratch = [((NX * NZ * (POINTS + 8), LANES), F32)]
    send, first, marks = call(first_conv_kernel, outs, scratch, scalars=1)(where, got, *mats)
    for step in range(ITERS):
        got = exchange(send.reshape(NA, 32, LANES), ("y", "c"))
        scratch = [((NA * 32, LANES), F32), ((NG * 32, LANES), F32)]
        tables = (own_inv, fwd, fixed, marks)
        if step == ITERS - 1:
            scratch = scratch + [((NG * 32, LANES), F32)]
            send = call(last_time_kernel, ((NG, 64, LANES), BF), scratch, scalars=1)(where, got, *tables)
            got = exchange(send, ("x", "c"))
            focus_minus = call(minus_kernel, (own, BF))(got, inv, onset)
            break
        send = call(time_kernel, ((NG, 32, LANES), BF), scratch, scalars=1)(where, got, *tables)
        got = exchange(send, ("x", "c"))
        send = call(corr_kernel, ((NX * NZ, 16, LANES), BF), [((NX * NZ * 16, LANES), F32)])(got, *mats)
        got = exchange(send, ("x", "z"))
        send = call(sum_kernel, ((NY, NX * 16, LANES), BF))(got)
        got = lax.all_gather(exchange(send, "y"), "c")
        scratch = [((NF * 16, LANES), F32), ((NX * 16, LANES), F32)]
        run = call(time_copies_kernel, ((NX, NZ, 16, LANES), BF), scratch, scalars=1)
        send = run(where, got, turned_inv, own_fwd, own_fixed, marks)
        got = exchange(send.reshape(NX * NZ, 16, LANES), ("x", "z"))
        scratch = [((NX * NZ * 16, LANES), F32), ((2 * POINTS, COLS), F32)]
        send = call(next_conv_kernel, ((NY, NC, 32, LANES), BF), scratch)(got, first, *mats)
    send = call(last_corr_kernel, ((NX, NZ, POINTS, LANES), BF))(got, *mats)
    got = exchange(send.reshape(NX * NZ, POINTS, LANES), ("x", "z")).reshape(NX, NZ, POINTS, LANES)
    send = call(last_sum_kernel, ((NA, 8, LANES), BF))(got)
    got = exchange(send, ("y", "c"))
    focus_plus = call(plus_kernel, (own, BF))(got, inv, onset, focus_start)
    return (focus_plus, focus_minus)


def solution(mesh):
    fine = Mesh(mesh.devices.reshape(NX, NY, NC, NZ), ("x", "y", "c", "z"))
    receivers = ("z", "x", "y", "c")
    slabs = ("x", "y", "c")
    return jax.shard_map(
        shards,
        mesh=fine,
        in_specs=(
            P(None, receivers, None),
            P(None, receivers),
            P(),
            P(slabs, "z", None),
            P(slabs, "z", None),
        ),
        out_specs=(P(None, receivers, None), P(None, receivers, None)),
        check_vma=False,
    )
```

```python
import math

import jax
import jax.numpy as jnp
import numpy as np
from jax import lax
from jax.experimental import pallas as pl
from jax.experimental.pallas import tpu as pltpu
from jax.sharding import Mesh
from jax.sharding import PartitionSpec as P

FLO = 8
ITERS = 2
NX, NY, NC, NZ = 4, 8, 2, 8
NA, NG, NI = NY * NC, NX * NC, 4
NF, POINTS, NT = 64, 16, 1024
BLOCK, COLS = 256, 2048
LANES = 128
SPANS = ((128, 384), (640, 896), (0, 128), (896, 1024))
CUT = 512
KEPT = 768
ONSET_MID = 256
BF, F32, I32 = jnp.bfloat16, jnp.float32, jnp.int32
VMEM_LIMIT = 8 * 1024 * 1024


def base_tables():
    phase = (np.arange(NT)[None, :] * (FLO + np.arange(NF))[:, None]) % NT
    angle = phase.astype(np.float32) * np.float32(2.0 * math.pi / NT)
    rows = np.concatenate([np.cos(angle), -np.sin(angle)], axis=0)
    forward = (rows * np.float32(1.0 / math.sqrt(NT))).astype(BF)
    inverse = (rows * np.float32(math.sqrt(2.0 / NF))).astype(BF)
    inverse = np.concatenate([inverse[:, a:b] for a, b in SPANS], axis=1)
    wide = np.concatenate([forward[:NF], forward[NF:]], axis=1)
    return forward, wide, np.ascontiguousarray(inverse.T)


def iota(shape, dim):
    return lax.broadcasted_iota(I32, shape, dim)


def grid(rows, cols):
    return iota((rows, cols), 0), iota((rows, cols), 1)


def hot(mask):
    return jnp.where(mask, jnp.float32(1), jnp.float32(0)).astype(BF)


def nn(a, b):
    return lax.dot_general(a, b, (((1,), (0,)), ((), ())), preferred_element_type=F32)


def nt(a, b):
    return lax.dot_general(a, b, (((1,), (1,)), ((), ())), preferred_element_type=F32)


def two_terms(value):
    high = value.astype(BF)
    return high, (value - high.astype(F32)).astype(BF)


def slab_of_bin(bins):
    row, _ = grid(NF, NF)
    return hot(row == bins)


def fetch(pairs, sems):
    copies = [pltpu.make_async_copy(src, dst, sems.at[n]) for n, (src, dst) in enumerate(pairs)]
    for copy in copies:
        copy.start()
    return copies


def start_kernel(bins_in, onset_in, focus_in, base_in, out, bins, onset, focus, base, flat, sems):
    copies = fetch([(bins_in, bins), (onset_in, onset), (focus_in, focus), (base_in, base)], sems)
    copies[0].wait()
    m, j = grid(8 * NA, NF)
    place = hot(((m & 7) < NX) & (j == ((m & 7) << 4) + (m >> 3)))
    order = nt(place, slab_of_bin(bins[...])).astype(BF)
    copies[1].wait()
    p, lane = grid(POINTS, LANES)
    spread = hot((((lane >> 2) & 15) == p) & ((lane >> 6) == (p >> 3)))
    marks = nn((onset[...] - ONSET_MID).astype(F32).astype(BF), spread)
    i, lane = grid(NI, LANES)
    marks = jnp.where((lane & 3) == i, marks, 0.0).sum(axis=0, keepdims=True)
    copies[2].wait()
    for p in range(POINTS):
        flat[NI * p : NI * (p + 1), :] = focus[p].astype(F32)
    rows = flat[...].astype(BF)
    none = jnp.zeros_like(rows)
    copies[3].wait()
    spec = nt(base[:, :NT], jnp.concatenate([rows, none], axis=0))
    spec = spec + nt(base[:, NT:], jnp.concatenate([none, rows], axis=0))
    sent = nn(order, spec.astype(BF))
    sent = jnp.where((iota((8 * NA, LANES), 0) & 7) == NX, marks, sent)
    out[...] = sent.reshape(NA, 8, LANES).astype(BF)


def tables_kernel(
    where, bins_in, onset_in, forward_in, inverse_in, re_in, im_in,
    inv, own_inv, fwd, fixed, own_fixed, own_marks, re, im,
    bins, onset, forward, inverse, sems,
):
    pairs = [(bins_in, bins), (onset_in, onset), (forward_in, forward), (inverse_in, inverse), (re_in, re), (im_in, im)]
    copies = fetch(pairs, sems)
    for copy in copies[:4]:
        copy.wait()
    holds = slab_of_bin(bins[...])
    j, k = grid(NF, LANES)
    order = nn(holds, hot(j == ((k >> 5) << 4) + (k & 15)))
    part = (k >> 4) & 1
    order = jnp.concatenate([jnp.where(part == 0, order, 0.0), jnp.where(part == 1, order, 0.0)], axis=0)
    table = nn(inverse[...], order.astype(BF)).astype(BF)
    inv[...] = table
    k, n = grid(LANES, 2 * NA)
    mine = hot(k == 2 * NA * where[0] + n)
    own_inv[...] = nn(table[:CUT], mine).astype(BF)
    m, j = grid(2 * NG, NF)
    slabs = nt(hot(j == (((m & 7) >> 1) << 4) + (where[1] << 1) + (m & 1)), holds)
    pick = jnp.concatenate([jnp.where(m < NG, slabs, 0.0), jnp.where(m < NG, 0.0, slabs)], axis=1)
    picked = nn(pick.astype(BF), forward[...]).astype(BF)
    picked = jnp.concatenate([picked[:, a:b] for a, b in SPANS], axis=1)
    fwd[...] = picked[:, :CUT]
    for n, term in enumerate(two_terms(nn(picked[:, CUT:], table[CUT:]))):
        fixed[n] = term
        own_fixed[n] = nn(term, mine).astype(BF)
    m, p = grid(POINTS * NI, POINTS)
    marks = nt(hot((m >> 2) == p), (onset[...] - ONSET_MID).astype(F32).astype(BF))
    m, i = grid(POINTS * NI, NI)
    marks = jnp.where((m & 3) == i, marks, 0.0).sum(axis=1, keepdims=True)
    own_marks[...] = jnp.broadcast_to(marks, (POINTS * NI, LANES)).astype(I32) + ONSET_MID
    copies[4].wait()
    copies[5].wait()


def middle_kernel(got, _, out, rows):
    rows[...] = got[...].astype(F32).reshape(8 * NA, LANES)
    line = jnp.concatenate([rows[pl.ds(e, NA, stride=8), :] for e in range(NX + 1)], axis=1).astype(BF)
    m, a = grid(NA * NI, NA)
    spread = nn(hot((m >> 2) == a), line)
    m, lane = grid(NA * NI, LANES)
    stacked = []
    for e in range(NX + 1):
        piece = spread[:, LANES * e : LANES * (e + 1)]
        for part in range(2):
            fits = ((lane & 3) == (m & 3)) & ((lane >> 6) == part)
            stacked.append(jnp.where(fits, piece, 0.0))
    stacked = jnp.concatenate(stacked, axis=0).astype(BF)
    p, lane = grid(POINTS, LANES)
    turned = nt(hot(((lane >> 2) & 15) == p), stacked)
    marks = turned[:8, LANES * NX :] + turned[8:, LANES * NX :]
    for x in range(NX):
        message = jnp.concatenate([turned[:, LANES * x : LANES * (x + 1)], marks], axis=0).astype(BF)
        for z in range(NZ):
            out[x, z] = message


def swap(a, b):
    low = iota(a.shape, 1) < LANES // 2
    return (
        jnp.where(low, a, pltpu.roll(b, LANES // 2, 1)),
        jnp.where(low, pltpu.roll(a, LANES // 2, 1), b),
    )


def convolve(src, mat_re, mat_im, out):
    a = nt(src, mat_re[...])
    b = nt(src, mat_im[...])
    parts = (a[:POINTS] - b[POINTS:], a[POINTS:] + b[:POINTS])
    for c in range(NC):
        at = slice(8 * c, 8 * (c + 1))
        slabs = [part[at, LANES * half : LANES * (half + 1)] for part in parts for half in range(2)]
        message = jnp.concatenate(slabs, axis=0).astype(BF)
        for y in range(NY):
            out[y, c] = message


def first_conv_kernel(where, got, mat_re, mat_im, out, src, marks, rows):
    height = POINTS + 8
    rows[...] = got[...].astype(F32).reshape(NX * NZ * height, LANES)
    for z in range(NZ):
        for half in range(2):
            a = rows[pl.ds((2 * half * NZ + z) * height, POINTS), :]
            b = rows[pl.ds(((2 * half + 1) * NZ + z) * height, POINTS), :]
            at = LANES * (2 * z + half)
            re, im = swap(a, b)
            src[:POINTS, at : at + LANES] = re.astype(BF)
            src[POINTS:, at : at + LANES] = im.astype(BF)
    for half in range(2):
        at = (2 * half * NZ + where[3]) * height + POINTS
        a = rows[pl.ds(pl.multiple_of(at, 8), 8), :]
        b = rows[pl.ds(pl.multiple_of(at + NZ * height, 8), 8), :]
        for h, block in enumerate(swap(a, b)):
            marks[8 * h : 8 * (h + 1), LANES * half : LANES * (half + 1)] = block.astype(I32) + ONSET_MID
    convolve(src[...], mat_re, mat_im, out)


def next_conv_kernel(got, first, mat_re, mat_im, out, rows, more):
    rows[...] = got[...].astype(F32).reshape(NG * NZ * 8, LANES)
    for z in range(NZ):
        for p in range(2):
            for part in range(2):
                for half in range(2):
                    slab = rows[pl.ds(8 * z + 4 * p + 2 * part + half, NG, stride=8 * NZ), :]
                    more[pl.ds(2 * POINTS * (2 * z + half) + POINTS * part + p, NG, stride=2), :] = slab
    blocks = [more[2 * POINTS * n : 2 * POINTS * (n + 1), :] for n in range(COLS // LANES)]
    src = (first[...].astype(F32) + jnp.concatenate(blocks, axis=1)).astype(BF)
    convolve(src, mat_re, mat_im, out)


def window(spectra, marks, inv, fwd, fixed):
    t = iota((BLOCK, 1), 0)
    front = jnp.where(t + SPANS[0][0] < marks, nn(inv[:BLOCK], spectra), 0.0).astype(BF)
    back = jnp.where(t + SPANS[1][0] >= NT - marks, nn(inv[BLOCK:CUT], spectra), 0.0).astype(BF)
    spec = nn(fwd[:, :BLOCK], front) + nn(fwd[:, BLOCK:], back)
    return spec + nn(fixed[0], spectra) + nn(fixed[1], spectra)


def points_window(marks, first, count, every, inv, fwd, fixed):
    mark = jnp.concatenate([marks[pl.ds(first + p, 1), :] for p in range(count)], axis=1)
    spec = window(jnp.concatenate(every, axis=1), mark, inv, fwd, fixed)
    return [spec[:, BLOCK * p : BLOCK * (p + 1)] for p in range(count)]


def window_slabs(where, got, inv, fwd, fixed, marks, rows, turn):
    rows[...] = got[...].astype(F32).reshape(NA * 32, LANES)
    every = []
    for p in range(8):
        parts = []
        for part in range(2):
            halves = [rows[pl.ds(16 * part + 8 * half + p, NA, stride=32), :] for half in range(2)]
            parts.append(jnp.concatenate(halves, axis=1))
        every.append(jnp.concatenate(parts, axis=0).astype(BF))
    for p, spec in enumerate(points_window(marks, 8 * where[2], 8, every, inv, fwd, fixed)):
        for part in range(2):
            for half in range(2):
                at = 16 * part + 8 * half + p
                slab = spec[NG * part : NG * (part + 1), LANES * half : LANES * (half + 1)]
                turn[pl.ds(at, NG, stride=32), :] = slab
    return every, turn[...].reshape(NG, 32, LANES)


def time_kernel(where, got, inv, fwd, fixed, marks, out, rows, turn):
    out[...] = window_slabs(where, got, inv, fwd, fixed, marks, rows, turn)[1].astype(BF)


def last_time_kernel(where, got, inv, fwd, fixed, marks, out, rows, turn, tail):
    every, message = window_slabs(where, got, inv, fwd, fixed, marks, rows, turn)
    m, r = grid(NG * NI, BLOCK)
    own = hot(r == ((m >> 3) << 6) + (where[1] << 3) + (((m >> 2) & 1) << 2) + (m & 3))
    taken = [nt(own, spectra) for spectra in every]
    taken = jnp.concatenate(taken, axis=0).astype(BF)
    n, k = grid(2 * NA, LANES)
    taken = nn(taken, hot(k == 2 * NA * where[0] + n))
    for p in range(8):
        for g in range(NG):
            at = NG * NI * p + NI * g
            tail[32 * g + NI * p : 32 * g + NI * (p + 1), :] = taken[at : at + NI]
    own = tail[...].reshape(NG, 32, LANES)
    out[...] = jnp.concatenate([message, own], axis=1).astype(BF)


def time_copies_kernel(where, got, inv, fwd, fixed, marks, out, rows, turn):
    rows[...] = got[...].astype(F32).reshape(NF * 8, LANES)
    every = []
    for p in range(2):
        parts = []
        for x in range(NX):
            for part in range(2):
                at = [8 * x + 4 * p + 2 * part + half for half in range(2)]
                halves = [rows[pl.ds(n, NA, stride=8 * NX), :] for n in at]
                parts.append(jnp.concatenate(halves, axis=1))
        every.append(jnp.concatenate(parts, axis=0).astype(BF))
    first = 4 * where[0] + 2 * where[2]
    for p, spec in enumerate(points_window(marks, first, 2, every, inv, fwd, fixed)):
        for part in range(2):
            for half in range(2):
                slab = spec[NG * part : NG * (part + 1), LANES * half : LANES * (half + 1)]
                turn[pl.ds(4 * p + 2 * part + half, NG, stride=8), :] = slab
    message = turn[...].reshape(NG, 8, LANES).astype(BF)
    for z in range(NZ):
        out[:, z] = message


def correlate(got, mat_re, mat_im):
    parts = []
    for part in range(2):
        halves = []
        for half in range(2):
            at = 8 * (2 * part + half)
            both = [sum(got[NC * x + c].astype(F32)[at : at + 8] for x in range(NX)) for c in range(NC)]
            halves.append(jnp.concatenate(both, axis=0))
        parts.append(jnp.concatenate(halves, axis=1))
    straight = jnp.concatenate(parts, axis=0).astype(BF)
    turned = jnp.concatenate([parts[1], -parts[0]], axis=0).astype(BF)
    for z in range(NZ):
        at = slice(BLOCK * z, BLOCK * (z + 1))
        yield z, nn(straight, mat_re[:, at]) + nn(turned, mat_im[:, at])


def corr_kernel(got, mat_re, mat_im, out, turn):
    for z, block in correlate(got, mat_re, mat_im):
        for x in range(NX):
            for part in range(2):
                for half in range(2):
                    at = (x * NZ + z) * 16 + 2 * part + half
                    row = POINTS * part + 4 * x
                    turn[pl.ds(at, 4, stride=4), :] = block[row : row + 4, LANES * half : LANES * (half + 1)]
    out[...] = turn[...].reshape(NX * NZ, 16, LANES).astype(BF)


def last_corr_kernel(got, mat_re, mat_im, out):
    for z, block in correlate(got, mat_re, mat_im):
        for half in range(2):
            at = slice(LANES * half, LANES * (half + 1))
            a, b = swap(block[:POINTS, at], block[POINTS:, at])
            out[2 * half, z] = a.astype(BF)
            out[2 * half + 1, z] = b.astype(BF)


def sum_kernel(got, out):
    total = got[...].astype(F32).reshape(NX, NZ, 16, LANES).sum(axis=1)
    for c in range(NC):
        message = total[:, 8 * c : 8 * (c + 1)].reshape(NX * 8, LANES).astype(BF)
        for y in range(NY):
            out[y, c] = message


def last_sum_kernel(got, out):
    total = got[...].astype(F32).sum(axis=1).astype(BF)
    total = jnp.concatenate([total[x] for x in range(NX)], axis=1)
    m, p = grid(LANES, POINTS)
    turned = nn(hot(((m >> 2) & 15) == p), total)
    m, n = grid(LANES, NX * LANES)
    turned = jnp.where(((n & 3) == (m & 3)) & (((n >> 6) & 1) == (m >> 6)), turned, 0.0).astype(BF)
    sent = nt(hot(((m & 7) == (n >> 7)) & ((m >> 3) == ((n >> 2) & 15))), turned)
    out[...] = sent.reshape(NA, 8, LANES).astype(BF)


def keep_own(spectra, inv, marks):
    trace = nt(spectra, inv)
    t = iota((POINTS * NI, LANES), 1)
    pieces = [trace[:, LANES * n : LANES * (n + 1)] for n in range(KEPT // LANES)]
    none = jnp.zeros_like(pieces[0])
    front = [jnp.where(t + SPANS[0][0] + LANES * n < marks, pieces[n], 0.0) for n in range(2)]
    back = [jnp.where(t + SPANS[1][0] + LANES * n >= NT - marks, pieces[2 + n], 0.0) for n in range(2)]
    return jnp.concatenate([pieces[4], *front, none, none, *back, pieces[5]], axis=1)


def minus_kernel(got, inv, marks, out):
    own = [sum(got[NC * x + c].astype(F32)[32:] for x in range(NX)) for c in range(NC)]
    own = jnp.concatenate(own, axis=0).astype(BF)
    trace = keep_own(own, inv[...], marks[...])
    for p in range(POINTS):
        out[p] = trace[NI * p : NI * (p + 1)].astype(BF)


def plus_kernel(got, inv, marks, focus, out):
    rows = got[...].astype(F32).reshape(8 * NA, LANES).T.astype(BF)
    m, k = grid(8 * NA, LANES)
    spectra = jnp.zeros((POINTS * NI, LANES), F32)
    for part in range(2):
        place = hot(((m & 7) < NX) & (k == ((m & 7) << 5) + 16 * part + (m >> 3)))
        spectra = spectra + nn(rows[NF * part : NF * (part + 1)], place)
    trace = keep_own(spectra.astype(BF), inv[...], marks[...])
    for p in range(POINTS):
        out[p] = (focus[p].astype(F32) + trace[NI * p : NI * (p + 1)]).astype(BF)


def call(kernel, outs, scratch=(), scalars=0, far=0, copies=0):
    single = not isinstance(outs, list)
    shapes = [jax.ShapeDtypeStruct(shape, dtype) for shape, dtype in ([outs] if single else outs)]

    def run(*args):
        spaces = [pltpu.SMEM] * scalars + [pltpu.HBM] * far + [pltpu.VMEM] * (len(args) - scalars - far)
        args = [
            pltpu.with_memory_space_constraint(arg, pltpu.HBM) if space is pltpu.HBM else arg
            for arg, space in zip(args, spaces)
        ]
        got = pl.pallas_call(
            kernel,
            out_shape=shapes,
            in_specs=[pl.BlockSpec(memory_space=space) for space in spaces],
            out_specs=[pl.BlockSpec(memory_space=pltpu.VMEM)] * len(shapes),
            scratch_shapes=[pltpu.VMEM(shape, dtype) for shape, dtype in scratch]
            + [pltpu.SemaphoreType.DMA((copies,))] * (copies > 0),
            compiler_params=pltpu.CompilerParams(vmem_limit_bytes=VMEM_LIMIT),
        )(*args)
        return got[0] if single else got

    return run


def exchange(values, axes):
    return lax.all_to_all(values, axes, 0, 0, tiled=True)


def shards(focus_start, onset, bins, refl_real, refl_imag):
    mats = (refl_real[0], refl_imag[0])
    where = jnp.stack([lax.axis_index(axis) for axis in ("x", "y", "c", "z")]).astype(I32)
    bins = bins.reshape(1, NF)
    onset = onset.T
    forward, wide, inverse = base_tables()
    own = (POINTS, NI, NT)

    scratch = [((1, NF), I32), ((NI, POINTS), I32), (own, BF), ((NF, 2 * NT), BF), ((POINTS * NI, NT), F32)]
    run = call(start_kernel, ((NA, 8, LANES), BF), scratch, far=4, copies=4)
    got = exchange(run(bins, onset, focus_start, wide), ("y", "c"))
    outs = [((KEPT, LANES), BF), ((CUT, 2 * NA), BF), ((2 * NG, CUT), BF), ((2, 2 * NG, LANES), BF), ((2, 2 * NG, 2 * NA), BF)]
    outs += [((POINTS * NI, LANES), I32), ((BLOCK, COLS), BF), ((BLOCK, COLS), BF)]
    scratch = [((1, NF), I32), ((NI, POINTS), I32), ((2 * NF, NT), BF), ((KEPT, LANES), BF)]
    run = call(tables_kernel, outs, scratch, scalars=1, far=6, copies=6)
    inv, own_inv, fwd, fixed, own_fixed, own_marks, *mats = run(where, bins, onset, forward, inverse, *mats)
    send = call(middle_kernel, ((NX, NZ, POINTS + 8, LANES), BF), [((8 * NA, LANES), F32)])(got, fwd)
    got = exchange(send.reshape(NX * NZ, POINTS + 8, LANES), ("x", "z"))
    outs = [((NY, NC, 32, LANES), BF), ((2 * POINTS, COLS), BF), ((POINTS, BLOCK), I32)]
    scratch = [((NX * NZ * (POINTS + 8), LANES), F32)]
    send, first, marks = call(first_conv_kernel, outs, scratch, scalars=1)(where, got, *mats)
    for step in range(ITERS):
        got = exchange(send.reshape(NA, 32, LANES), ("y", "c"))
        scratch = [((NA * 32, LANES), F32), ((NG * 32, LANES), F32)]
        tables = (own_inv, fwd, own_fixed, marks)
        if step == ITERS - 1:
            scratch = scratch + [((NG * 32, LANES), F32)]
            send = call(last_time_kernel, ((NG, 64, LANES), BF), scratch, scalars=1)(where, got, *tables)
            got = exchange(send, ("x", "c"))
            focus_minus = call(minus_kernel, (own, BF))(got, inv, own_marks)
            break
        send = call(time_kernel, ((NG, 32, LANES), BF), scratch, scalars=1)(where, got, *tables)
        got = exchange(send, ("x", "c"))
        send = call(corr_kernel, ((NX * NZ, 16, LANES), BF), [((NX * NZ * 16, LANES), F32)])(got, *mats)
        got = exchange(send, ("x", "z"))
        send = call(sum_kernel, ((NY, NC, NX * 8, LANES), BF))(got)
        got = exchange(send.reshape(NA, NX * 8, LANES), ("y", "c"))
        scratch = [((NF * 8, LANES), F32), ((NG * 8, LANES), F32)]
        run = call(time_copies_kernel, ((NG, NZ, 8, LANES), BF), scratch, scalars=1)
        send = run(where, got, inv, fwd, fixed, marks)
        got = exchange(send.reshape(NG * NZ, 8, LANES), ("x", "c", "z"))
        scratch = [((NG * NZ * 8, LANES), F32), ((2 * POINTS * COLS // LANES, LANES), F32)]
        send = call(next_conv_kernel, ((NY, NC, 32, LANES), BF), scratch)(got, first, *mats)
    send = call(last_corr_kernel, ((NX, NZ, POINTS, LANES), BF))(got, *mats)
    got = exchange(send.reshape(NX * NZ, POINTS, LANES), ("x", "z")).reshape(NX, NZ, POINTS, LANES)
    send = call(last_sum_kernel, ((NA, 8, LANES), BF))(got)
    got = exchange(send, ("y", "c"))
    focus_plus = call(plus_kernel, (own, BF))(got, inv, own_marks, focus_start)
    return (focus_plus, focus_minus)


def solution(mesh):
    fine = Mesh(mesh.devices.reshape(NX, NY, NC, NZ), ("x", "y", "c", "z"))
    receivers = ("z", "x", "y", "c")
    slabs = ("x", "y", "c")
    return jax.shard_map(
        shards,
        mesh=fine,
        in_specs=(
            P(None, receivers, None),
            P(None, receivers),
            P(),
            P(slabs, "z", None),
            P(slabs, "z", None),
        ),
        out_specs=(P(None, receivers, None), P(None, receivers, None)),
        check_vma=False,
    )
```

```python
import math

import jax
import jax.numpy as jnp
import numpy as np
from jax import lax
from jax.experimental import pallas as pl
from jax.experimental.pallas import tpu as pltpu
from jax.sharding import Mesh
from jax.sharding import PartitionSpec as P

FLO = 8
ITERS = 2
NX, NY, NC, NZ = 4, 8, 2, 8
NA, NG, NI = NY * NC, NX * NC, 4
NF, POINTS, NT = 64, 16, 1024
BLOCK, COLS = 256, 2048
LANES = 128
SPANS = ((128, 384), (640, 896), (0, 128), (896, 1024))
CUT = 512
KEPT = 768
TIMES = CUT + 2 * 2 * NG
ONSET_MID = 256
BF, F32, I32 = jnp.bfloat16, jnp.float32, jnp.int32
VMEM_LIMIT = 8 * 1024 * 1024


def base_tables():
    phase = (np.arange(NT)[None, :] * (FLO + np.arange(NF))[:, None]) % NT
    angle = phase.astype(np.float32) * np.float32(2.0 * math.pi / NT)
    rows = np.concatenate([np.cos(angle), -np.sin(angle)], axis=0)
    forward = (rows * np.float32(1.0 / math.sqrt(NT))).astype(BF)
    inverse = (rows * np.float32(math.sqrt(2.0 / NF))).astype(BF)
    inverse = np.concatenate([inverse[:, a:b] for a, b in SPANS], axis=1)
    wide = np.concatenate([forward[:NF], forward[NF:]], axis=1)
    return forward, wide, np.ascontiguousarray(inverse.T)


def iota(shape, dim):
    return lax.broadcasted_iota(I32, shape, dim)


def grid(rows, cols):
    return iota((rows, cols), 0), iota((rows, cols), 1)


def hot(mask):
    return jnp.where(mask, jnp.float32(1), jnp.float32(0)).astype(BF)


def nn(a, b):
    return lax.dot_general(a, b, (((1,), (0,)), ((), ())), preferred_element_type=F32)


def nt(a, b):
    return lax.dot_general(a, b, (((1,), (1,)), ((), ())), preferred_element_type=F32)


def two_terms(value):
    high = value.astype(BF)
    return high, (value - high.astype(F32)).astype(BF)


def slab_of_bin(bins):
    row, _ = grid(NF, NF)
    return hot(row == bins)


def fetch(pairs, sems):
    copies = [pltpu.make_async_copy(src, dst, sems.at[n]) for n, (src, dst) in enumerate(pairs)]
    for copy in copies:
        copy.start()
    return copies


def start_kernel(bins_in, onset_in, focus_in, base_in, out, bins, onset, focus, base, flat, sems):
    copies = fetch([(bins_in, bins), (onset_in, onset), (focus_in, focus), (base_in, base)], sems)
    copies[0].wait()
    m, j = grid(8 * NA, NF)
    place = hot(((m & 7) < NX) & (j == ((m & 7) << 4) + (m >> 3)))
    order = nt(place, slab_of_bin(bins[...])).astype(BF)
    copies[1].wait()
    p, lane = grid(POINTS, LANES)
    spread = hot((((lane >> 2) & 15) == p) & ((lane >> 6) == (p >> 3)))
    marks = nn((onset[...] - ONSET_MID).astype(F32).astype(BF), spread)
    i, lane = grid(NI, LANES)
    marks = jnp.where((lane & 3) == i, marks, 0.0).sum(axis=0, keepdims=True)
    copies[2].wait()
    for p in range(POINTS):
        flat[NI * p : NI * (p + 1), :] = focus[p].astype(F32)
    rows = flat[...].astype(BF)
    none = jnp.zeros_like(rows)
    copies[3].wait()
    spec = nt(base[:, :NT], jnp.concatenate([rows, none], axis=0))
    spec = spec + nt(base[:, NT:], jnp.concatenate([none, rows], axis=0))
    sent = nn(order, spec.astype(BF))
    sent = jnp.where((iota((8 * NA, LANES), 0) & 7) == NX, marks, sent)
    out[...] = sent.reshape(NA, 8, LANES).astype(BF)


def tables_kernel(
    where, bins_in, onset_in, forward_in, inverse_in, re_in, im_in,
    inv, own_inv, fwd, own_marks, re, im,
    bins, onset, forward, inverse, sems,
):
    pairs = [(bins_in, bins), (onset_in, onset), (forward_in, forward), (inverse_in, inverse), (re_in, re), (im_in, im)]
    copies = fetch(pairs, sems)
    for copy in copies[:4]:
        copy.wait()
    held = bins[...].astype(F32).astype(BF)
    j, k = grid(NF, LANES)
    arrival = ((k >> 5) << 4) + (k & 15)
    at_k = nn(held, hot(j == arrival))
    j, n = grid(NF, 2 * NA)
    at_own = nn(held, hot(j == (where[0] << 4) + (n & 15)))
    row, k = grid(LANES, LANES)
    order = hot(((row >> 6) == ((k >> 4) & 1)) & ((row & 63).astype(F32) == at_k))
    row, n = grid(LANES, 2 * NA)
    own_order = hot(((row >> 6) == (n >> 4)) & ((row & 63).astype(F32) == at_own))
    base = inverse[...]
    table = nn(base, order).astype(BF)
    own_table = nn(base, own_order).astype(BF)
    m, j = grid(2 * NG, NF)
    slabs = nt(hot(j == (((m & 7) >> 1) << 4) + (where[1] << 1) + (m & 1)), slab_of_bin(bins[...]))
    pick = jnp.concatenate([jnp.where(m < NG, slabs, 0.0), jnp.where(m < NG, 0.0, slabs)], axis=1).astype(BF)
    for n, (a, b) in enumerate(SPANS[:2]):
        fwd[:, BLOCK * n : BLOCK * (n + 1)] = nn(pick, forward[:, a:b]).astype(BF)
    picked = [nn(pick, forward[:, a:b]).astype(BF) for a, b in SPANS[2:]]
    picked = jnp.concatenate(picked, axis=1)
    for out, part in ((inv, table), (own_inv, own_table)):
        out[:CUT] = part[:CUT]
        out[CUT:TIMES] = jnp.concatenate(two_terms(nn(picked, part[CUT:])), axis=0)
    inv[TIMES:] = table[CUT:]
    m, p = grid(POINTS * NI, POINTS)
    marks = nt(hot((m >> 2) == p), (onset[...] - ONSET_MID).astype(F32).astype(BF))
    m, i = grid(POINTS * NI, NI)
    marks = jnp.where((m & 3) == i, marks, 0.0).sum(axis=1, keepdims=True)
    own_marks[...] = jnp.broadcast_to(marks, (POINTS * NI, LANES)).astype(I32) + ONSET_MID
    for copy in copies[4:]:
        copy.wait()


def middle_kernel(got, _, out, rows):
    rows[...] = got[...].astype(F32).reshape(8 * NA, LANES)
    line = jnp.concatenate([rows[pl.ds(e, NA, stride=8), :] for e in range(NX + 1)], axis=1).astype(BF)
    m, a = grid(NA * NI, NA)
    spread = nn(hot((m >> 2) == a), line)
    m, lane = grid(NA * NI, LANES)
    stacked = []
    for e in range(NX + 1):
        piece = spread[:, LANES * e : LANES * (e + 1)]
        for part in range(2):
            fits = ((lane & 3) == (m & 3)) & ((lane >> 6) == part)
            stacked.append(jnp.where(fits, piece, 0.0))
    stacked = jnp.concatenate(stacked, axis=0).astype(BF)
    p, lane = grid(POINTS, LANES)
    turned = nt(hot(((lane >> 2) & 15) == p), stacked)
    marks = turned[:8, LANES * NX :] + turned[8:, LANES * NX :]
    for x in range(NX):
        message = jnp.concatenate([turned[:, LANES * x : LANES * (x + 1)], marks], axis=0).astype(BF)
        for z in range(NZ):
            out[x, z] = message


def swap(a, b):
    low = iota(a.shape, 1) < LANES // 2
    return (
        jnp.where(low, a, pltpu.roll(b, LANES // 2, 1)),
        jnp.where(low, pltpu.roll(a, LANES // 2, 1), b),
    )


def convolve(src, mat_re, mat_im, out):
    a = nt(src, mat_re[...])
    b = nt(src, mat_im[...])
    parts = (a[:POINTS] - b[POINTS:], a[POINTS:] + b[:POINTS])
    for c in range(NC):
        at = slice(8 * c, 8 * (c + 1))
        slabs = [part[at, LANES * half : LANES * (half + 1)] for part in parts for half in range(2)]
        message = jnp.concatenate(slabs, axis=0).astype(BF)
        for y in range(NY):
            out[y, c] = message


def first_conv_kernel(where, got, mat_re, mat_im, out, src, marks, rows):
    height = POINTS + 8
    rows[...] = got[...].astype(F32).reshape(NX * NZ * height, LANES)
    for z in range(NZ):
        for half in range(2):
            a = rows[pl.ds((2 * half * NZ + z) * height, POINTS), :]
            b = rows[pl.ds(((2 * half + 1) * NZ + z) * height, POINTS), :]
            at = LANES * (2 * z + half)
            re, im = swap(a, b)
            src[:POINTS, at : at + LANES] = re.astype(BF)
            src[POINTS:, at : at + LANES] = im.astype(BF)
    for half in range(2):
        at = (2 * half * NZ + where[3]) * height + POINTS
        a = rows[pl.ds(pl.multiple_of(at, 8), 8), :]
        b = rows[pl.ds(pl.multiple_of(at + NZ * height, 8), 8), :]
        for h, block in enumerate(swap(a, b)):
            marks[8 * h : 8 * (h + 1), LANES * half : LANES * (half + 1)] = block.astype(I32) + ONSET_MID
    convolve(src[...], mat_re, mat_im, out)


def next_conv_kernel(got, first, mat_re, mat_im, out, rows, more):
    rows[...] = got[...].astype(F32).reshape(NG * NZ * 8, LANES)
    for z in range(NZ):
        for p in range(2):
            for part in range(2):
                for half in range(2):
                    slab = rows[pl.ds(8 * z + 4 * p + 2 * part + half, NG, stride=8 * NZ), :]
                    more[pl.ds(2 * POINTS * (2 * z + half) + POINTS * part + p, NG, stride=2), :] = slab
    blocks = [more[2 * POINTS * n : 2 * POINTS * (n + 1), :] for n in range(COLS // LANES)]
    src = (first[...].astype(F32) + jnp.concatenate(blocks, axis=1)).astype(BF)
    convolve(src, mat_re, mat_im, out)


def window(spectra, marks, inv, fwd):
    t = iota((BLOCK, 1), 0)
    front = jnp.where(t + SPANS[0][0] < marks, nn(inv[:BLOCK], spectra), 0.0).astype(BF)
    rest = nn(inv[BLOCK:TIMES], spectra)
    back = jnp.where(t + SPANS[1][0] >= NT - marks, rest[:BLOCK], 0.0).astype(BF)
    fixed = rest[BLOCK : BLOCK + 2 * NG] + rest[BLOCK + 2 * NG :]
    return nn(fwd[:, :BLOCK], front) + nn(fwd[:, BLOCK:], back) + fixed


def points_window(marks, first, count, every, inv, fwd):
    mark = jnp.concatenate([marks[pl.ds(first + p, 1), :] for p in range(count)], axis=1)
    spec = window(jnp.concatenate(every, axis=1), mark, inv, fwd)
    return [spec[:, BLOCK * p : BLOCK * (p + 1)] for p in range(count)]


def window_slabs(where, got, inv, fwd, marks, rows, turn):
    rows[...] = got[...].astype(F32).reshape(NA * 32, LANES)
    every = []
    for p in range(8):
        parts = []
        for part in range(2):
            halves = [rows[pl.ds(16 * part + 8 * half + p, NA, stride=32), :] for half in range(2)]
            parts.append(jnp.concatenate(halves, axis=1))
        every.append(jnp.concatenate(parts, axis=0).astype(BF))
    for p, spec in enumerate(points_window(marks, 8 * where[2], 8, every, inv, fwd)):
        for part in range(2):
            for half in range(2):
                at = 16 * part + 8 * half + p
                slab = spec[NG * part : NG * (part + 1), LANES * half : LANES * (half + 1)]
                turn[pl.ds(at, NG, stride=32), :] = slab
    return every, turn[...].reshape(NG, 32, LANES)


def time_kernel(where, got, inv, fwd, marks, out, rows, turn):
    out[...] = window_slabs(where, got, inv, fwd, marks, rows, turn)[1].astype(BF)


def last_time_kernel(where, got, inv, fwd, marks, out, rows, turn, tail):
    every, message = window_slabs(where, got, inv, fwd, marks, rows, turn)
    m, r = grid(NG * NI, BLOCK)
    own = hot(r == ((m >> 3) << 6) + (where[1] << 3) + (((m >> 2) & 1) << 2) + (m & 3))
    for h in range(2):
        taken = nt(own, jnp.concatenate(every[4 * h : 4 * (h + 1)], axis=0))
        for g in range(NG):
            tail[8 * g + NI * h : 8 * g + NI * (h + 1), :] = taken[NI * g : NI * (g + 1)]
    out[...] = jnp.concatenate([message, tail[...].reshape(NG, 8, LANES)], axis=1).astype(BF)


def time_copies_kernel(where, got, inv, fwd, marks, out, rows, turn):
    rows[...] = got[...].astype(F32).reshape(NF * 8, LANES)
    every = []
    for p in range(2):
        parts = []
        for x in range(NX):
            for part in range(2):
                at = [8 * x + 4 * p + 2 * part + half for half in range(2)]
                halves = [rows[pl.ds(n, NA, stride=8 * NX), :] for n in at]
                parts.append(jnp.concatenate(halves, axis=1))
        every.append(jnp.concatenate(parts, axis=0).astype(BF))
    first = 4 * where[0] + 2 * where[2]
    for p, spec in enumerate(points_window(marks, first, 2, every, inv, fwd)):
        for part in range(2):
            for half in range(2):
                slab = spec[NG * part : NG * (part + 1), LANES * half : LANES * (half + 1)]
                turn[pl.ds(4 * p + 2 * part + half, NG, stride=8), :] = slab
    message = turn[...].reshape(NG, 8, LANES).astype(BF)
    for z in range(NZ):
        out[:, z] = message


def correlate(got, mat_re, mat_im):
    parts = []
    for part in range(2):
        halves = []
        for half in range(2):
            at = 8 * (2 * part + half)
            both = [sum(got[NC * x + c].astype(F32)[at : at + 8] for x in range(NX)) for c in range(NC)]
            halves.append(jnp.concatenate(both, axis=0))
        parts.append(jnp.concatenate(halves, axis=1))
    straight = jnp.concatenate(parts, axis=0).astype(BF)
    turned = jnp.concatenate([parts[1], -parts[0]], axis=0).astype(BF)
    for z in range(NZ):
        at = slice(BLOCK * z, BLOCK * (z + 1))
        yield z, nn(straight, mat_re[:, at]) + nn(turned, mat_im[:, at])


def corr_kernel(got, mat_re, mat_im, out, turn):
    for z, block in correlate(got, mat_re, mat_im):
        for x in range(NX):
            for part in range(2):
                for half in range(2):
                    at = (x * NZ + z) * 16 + 2 * part + half
                    row = POINTS * part + 4 * x
                    turn[pl.ds(at, 4, stride=4), :] = block[row : row + 4, LANES * half : LANES * (half + 1)]
    out[...] = turn[...].reshape(NX * NZ, 16, LANES).astype(BF)


def last_corr_kernel(got, mat_re, mat_im, out):
    for z, block in correlate(got, mat_re, mat_im):
        for half in range(2):
            at = slice(LANES * half, LANES * (half + 1))
            a, b = swap(block[:POINTS, at], block[POINTS:, at])
            out[2 * half, z] = a.astype(BF)
            out[2 * half + 1, z] = b.astype(BF)


def sum_kernel(got, out):
    total = got[...].astype(F32).reshape(NX, NZ, 16, LANES).sum(axis=1)
    for c in range(NC):
        message = total[:, 8 * c : 8 * (c + 1)].reshape(NX * 8, LANES).astype(BF)
        for y in range(NY):
            out[y, c] = message


def last_sum_kernel(got, out):
    total = got[...].astype(F32).sum(axis=1).astype(BF)
    total = jnp.concatenate([total[x] for x in range(NX)], axis=1)
    m, p = grid(LANES, POINTS)
    turned = nn(hot(((m >> 2) & 15) == p), total)
    m, n = grid(LANES, NX * LANES)
    turned = jnp.where(((n & 3) == (m & 3)) & (((n >> 6) & 1) == (m >> 6)), turned, 0.0).astype(BF)
    sent = nt(hot(((m & 7) == (n >> 7)) & ((m >> 3) == ((n >> 2) & 15))), turned)
    out[...] = sent.reshape(NA, 8, LANES).astype(BF)


def keep_own(spectra, inv, marks):
    t = iota((POINTS * NI, LANES), 1)
    trace = [nt(spectra, inv[a:b]) for a, b in ((0, CUT), (TIMES, TIMES + KEPT - CUT))]
    trace = jnp.concatenate(trace, axis=1)
    pieces = [trace[:, LANES * n : LANES * (n + 1)] for n in range(KEPT // LANES)]
    none = jnp.zeros_like(pieces[0])
    front = [jnp.where(t + SPANS[0][0] + LANES * n < marks, pieces[n], 0.0) for n in range(2)]
    back = [jnp.where(t + SPANS[1][0] + LANES * n >= NT - marks, pieces[2 + n], 0.0) for n in range(2)]
    return jnp.concatenate([pieces[4], *front, none, none, *back, pieces[5]], axis=1)


def last_kernel(got, tail, inv, marks, focus, plus_out, minus_out, plus, minus, spectra, sems):
    rows = got[...].astype(F32).reshape(8 * NA, LANES).T.astype(BF)
    m, k = grid(8 * NA, LANES)
    own = jnp.zeros((POINTS * NI, LANES), F32)
    for part in range(2):
        place = hot(((m & 7) < NX) & (k == ((m & 7) << 5) + 16 * part + (m >> 3)))
        own = own + nn(rows[NF * part : NF * (part + 1)], place)
    trace = keep_own(own.astype(BF), inv[...], marks[...])
    for p in range(POINTS):
        plus[p] = (focus[p].astype(F32) + trace[NI * p : NI * (p + 1)]).astype(BF)
    first = pltpu.make_async_copy(plus, plus_out, sems.at[0])
    first.start()
    own = [jnp.concatenate([tail[NC * x + c].astype(F32)[32:] for c in range(NC)], axis=0) for x in range(NX)]
    own = jnp.concatenate(own, axis=1).astype(BF)
    n, k = grid(NX * LANES, LANES)
    same = (n >> 7) * 32 + (n & 31) == k
    own = [nn(own, hot(same & (((n >> 5) & 3) == p))) for p in range(4)]
    for p in range(POINTS):
        spectra[NI * p : NI * (p + 1), :] = own[p & 3][NI * (p >> 2) : NI * ((p >> 2) + 1)]
    trace = keep_own(spectra[...].astype(BF), inv[...], marks[...])
    for p in range(POINTS):
        minus[p] = trace[NI * p : NI * (p + 1)].astype(BF)
    second = pltpu.make_async_copy(minus, minus_out, sems.at[1])
    second.start()
    first.wait()
    second.wait()


def call(kernel, outs, scratch=(), scalars=0, far=0, copies=0, far_outs=0):
    single = not isinstance(outs, list)
    shapes = [jax.ShapeDtypeStruct(shape, dtype) for shape, dtype in ([outs] if single else outs)]

    def run(*args):
        out_spaces = [pltpu.VMEM] * (len(shapes) - far_outs) + [pltpu.HBM] * far_outs
        spaces = [pltpu.SMEM] * scalars + [pltpu.HBM] * far + [pltpu.VMEM] * (len(args) - scalars - far)
        args = [
            pltpu.with_memory_space_constraint(arg, pltpu.HBM) if space is pltpu.HBM else arg
            for arg, space in zip(args, spaces)
        ]
        got = pl.pallas_call(
            kernel,
            out_shape=shapes,
            in_specs=[pl.BlockSpec(memory_space=space) for space in spaces],
            out_specs=[pl.BlockSpec(memory_space=space) for space in out_spaces],
            scratch_shapes=[pltpu.VMEM(shape, dtype) for shape, dtype in scratch]
            + [pltpu.SemaphoreType.DMA((copies,))] * (copies > 0),
            compiler_params=pltpu.CompilerParams(vmem_limit_bytes=VMEM_LIMIT),
        )(*args)
        return got[0] if single else got

    return run


def exchange(values, axes):
    return lax.all_to_all(values, axes, 0, 0, tiled=True)


def shards(focus_start, onset, bins, refl_real, refl_imag):
    mats = (refl_real[0], refl_imag[0])
    where = jnp.stack([lax.axis_index(axis) for axis in ("x", "y", "c", "z")]).astype(I32)
    bins = bins.reshape(1, NF)
    onset = onset.T
    forward, wide, inverse = base_tables()
    own = (POINTS, NI, NT)

    scratch = [((1, NF), I32), ((NI, POINTS), I32), (own, BF), ((NF, 2 * NT), BF), ((POINTS * NI, NT), F32)]
    run = call(start_kernel, ((NA, 8, LANES), BF), scratch, far=4, copies=4)
    got = exchange(run(bins, onset, focus_start, wide), ("y", "c"))
    outs = [((TIMES + KEPT - CUT, LANES), BF), ((TIMES, 2 * NA), BF), ((2 * NG, CUT), BF)]
    outs += [((POINTS * NI, LANES), I32), ((BLOCK, COLS), BF), ((BLOCK, COLS), BF)]
    scratch = [((1, NF), I32), ((NI, POINTS), I32), ((2 * NF, NT), BF), ((KEPT, LANES), BF)]
    run = call(tables_kernel, outs, scratch, scalars=1, far=6, copies=6)
    inv, own_inv, fwd, own_marks, *mats = run(where, bins, onset, forward, inverse, *mats)
    send = call(middle_kernel, ((NX, NZ, POINTS + 8, LANES), BF), [((8 * NA, LANES), F32)])(got, fwd)
    got = exchange(send.reshape(NX * NZ, POINTS + 8, LANES), ("x", "z"))
    outs = [((NY, NC, 32, LANES), BF), ((2 * POINTS, COLS), BF), ((POINTS, BLOCK), I32)]
    scratch = [((NX * NZ * (POINTS + 8), LANES), F32)]
    send, first, marks = call(first_conv_kernel, outs, scratch, scalars=1)(where, got, *mats)
    for step in range(ITERS):
        got = exchange(send.reshape(NA, 32, LANES), ("y", "c"))
        scratch = [((NA * 32, LANES), F32), ((NG * 32, LANES), F32)]
        tables = (own_inv, fwd, marks)
        if step == ITERS - 1:
            scratch = scratch + [((NG * 8, LANES), F32)]
            send = call(last_time_kernel, ((NG, 40, LANES), BF), scratch, scalars=1)(where, got, *tables)
            got = exchange(send, ("x", "c"))
            break
        send = call(time_kernel, ((NG, 32, LANES), BF), scratch, scalars=1)(where, got, *tables)
        got = exchange(send, ("x", "c"))
        send = call(corr_kernel, ((NX * NZ, 16, LANES), BF), [((NX * NZ * 16, LANES), F32)])(got, *mats)
        got = exchange(send, ("x", "z"))
        send = call(sum_kernel, ((NY, NC, NX * 8, LANES), BF))(got)
        got = exchange(send.reshape(NA, NX * 8, LANES), ("y", "c"))
        scratch = [((NF * 8, LANES), F32), ((NG * 8, LANES), F32)]
        run = call(time_copies_kernel, ((NG, NZ, 8, LANES), BF), scratch, scalars=1)
        send = run(where, got, inv, fwd, marks)
        got = exchange(send.reshape(NG * NZ, 8, LANES), ("x", "c", "z"))
        scratch = [((NG * NZ * 8, LANES), F32), ((2 * POINTS * COLS // LANES, LANES), F32)]
        send = call(next_conv_kernel, ((NY, NC, 32, LANES), BF), scratch)(got, first, *mats)
    tail = got
    send = call(last_corr_kernel, ((NX, NZ, POINTS, LANES), BF))(got, *mats)
    got = exchange(send.reshape(NX * NZ, POINTS, LANES), ("x", "z")).reshape(NX, NZ, POINTS, LANES)
    send = call(last_sum_kernel, ((NA, 8, LANES), BF))(got)
    got = exchange(send, ("y", "c"))
    scratch = [(own, BF), (own, BF), ((POINTS * NI, LANES), F32)]
    run = call(last_kernel, [(own, BF), (own, BF)], scratch, copies=2, far_outs=2)
    focus_plus, focus_minus = run(got, tail, inv, own_marks, focus_start)
    return (focus_plus, focus_minus)


def solution(mesh):
    fine = Mesh(mesh.devices.reshape(NX, NY, NC, NZ), ("x", "y", "c", "z"))
    receivers = ("z", "x", "y", "c")
    slabs = ("x", "y", "c")
    return jax.shard_map(
        shards,
        mesh=fine,
        in_specs=(
            P(None, receivers, None),
            P(None, receivers),
            P(),
            P(slabs, "z", None),
            P(slabs, "z", None),
        ),
        out_specs=(P(None, receivers, None), P(None, receivers, None)),
        check_vma=False,
    )
```

```python
import math

import jax
import jax.numpy as jnp
import numpy as np
from jax import lax
from jax.experimental import pallas as pl
from jax.experimental.pallas import tpu as pltpu
from jax.sharding import Mesh
from jax.sharding import PartitionSpec as P

FLO = 8
ITERS = 2
NX, NY, NC, NZ = 4, 8, 2, 8
NW = 2
NA, NG, NI = NY * NC, NX * NC, 4
NU = NG * NW
NF, POINTS, NT = 64, 16, 1024
BLOCK, COLS = 256, 2048
LANES = 128
SPANS = ((128, 384), (640, 896), (0, 128), (896, 1024))
CUT = 512
KEPT = 768
TIMES = CUT + 2 * 2 * NG
OWN_TIMES = CUT + 2 * 2 * NU
ONSET_MID = 256
BF, F32, I32 = jnp.bfloat16, jnp.float32, jnp.int32
VMEM_LIMIT = 8 * 1024 * 1024


def base_tables():
    phase = (np.arange(NT)[None, :] * (FLO + np.arange(NF))[:, None]) % NT
    angle = phase.astype(np.float32) * np.float32(2.0 * math.pi / NT)
    rows = np.concatenate([np.cos(angle), -np.sin(angle)], axis=0)
    forward = (rows * np.float32(1.0 / math.sqrt(NT))).astype(BF)
    inverse = (rows * np.float32(math.sqrt(2.0 / NF))).astype(BF)
    inverse = np.concatenate([inverse[:, a:b] for a, b in SPANS], axis=1)
    wide = np.concatenate([forward[:NF], forward[NF:]], axis=1)
    return forward, wide, np.ascontiguousarray(inverse.T)


def iota(shape, dim):
    return lax.broadcasted_iota(I32, shape, dim)


def grid(rows, cols):
    return iota((rows, cols), 0), iota((rows, cols), 1)


def hot(mask):
    return jnp.where(mask, jnp.float32(1), jnp.float32(0)).astype(BF)


def nn(a, b):
    return lax.dot_general(a, b, (((1,), (0,)), ((), ())), preferred_element_type=F32)


def nt(a, b):
    return lax.dot_general(a, b, (((1,), (1,)), ((), ())), preferred_element_type=F32)


def two_terms(value):
    high = value.astype(BF)
    return high, (value - high.astype(F32)).astype(BF)


def slab_of_bin(bins):
    row, _ = grid(NF, NF)
    return hot(row == bins)


def fetch(pairs, sems):
    copies = [pltpu.make_async_copy(src, dst, sems.at[n]) for n, (src, dst) in enumerate(pairs)]
    for copy in copies:
        copy.start()
    return copies


def start_kernel(bins_in, onset_in, focus_in, base_in, out, bins, onset, focus, base, flat, sems):
    copies = fetch([(bins_in, bins), (onset_in, onset), (focus_in, focus), (base_in, base)], sems)
    copies[0].wait()
    m, j = grid(8 * NA, NF)
    place = hot(((m & 7) < NX) & (j == ((m & 7) << 4) + (m >> 3)))
    order = nt(place, slab_of_bin(bins[...])).astype(BF)
    copies[1].wait()
    p, lane = grid(POINTS, LANES)
    spread = hot((((lane >> 2) & 15) == p) & ((lane >> 6) == (p >> 3)))
    marks = nn((onset[...] - ONSET_MID).astype(F32).astype(BF), spread)
    i, lane = grid(NI, LANES)
    marks = jnp.where((lane & 3) == i, marks, 0.0).sum(axis=0, keepdims=True)
    copies[2].wait()
    for p in range(POINTS):
        flat[NI * p : NI * (p + 1), :] = focus[p].astype(F32)
    rows = flat[...].astype(BF)
    none = jnp.zeros_like(rows)
    copies[3].wait()
    spec = nt(base[:, :NT], jnp.concatenate([rows, none], axis=0))
    spec = spec + nt(base[:, NT:], jnp.concatenate([none, rows], axis=0))
    sent = nn(order, spec.astype(BF))
    sent = jnp.where((iota((8 * NA, LANES), 0) & 7) == NX, marks, sent)
    out[...] = sent.reshape(NA, 8, LANES).astype(BF)


def tables_kernel(
    where, bins_in, onset_in, forward_in, inverse_in, re_in, im_in,
    place, inv, own_inv, fwd, own_fwd, own_marks, re, im,
    bins, onset, forward, inverse, sems,
):
    pairs = [(bins_in, bins), (onset_in, onset), (forward_in, forward), (inverse_in, inverse), (re_in, re), (im_in, im)]
    copies = fetch(pairs, sems)
    for copy in copies[:4]:
        copy.wait()
    row, _ = grid(8, LANES)
    value = jnp.zeros((8, LANES), I32)
    for n in range(4):
        value = jnp.where(row == n, where[n], value)
    place[...] = value
    held = bins[...].astype(F32).astype(BF)
    j, k = grid(NF, LANES)
    arrival = ((k >> 5) << 4) + (k & 15)
    at_k = nn(held, hot(j == arrival))
    j, n = grid(NF, 2 * NA)
    at_own = nn(held, hot(j == (where[0] << 4) + (n & 15)))
    row, k = grid(LANES, LANES)
    order = hot(((row >> 6) == ((k >> 4) & 1)) & ((row & 63).astype(F32) == at_k))
    row, n = grid(LANES, 2 * NA)
    own_order = hot(((row >> 6) == (n >> 4)) & ((row & 63).astype(F32) == at_own))
    base = inverse[...]
    table = nn(base, order).astype(BF)
    own_table = nn(base, own_order).astype(BF)
    holds = slab_of_bin(bins[...])
    m, j = grid(2 * NG, NF)
    slabs = hot(j == (((m & 7) >> 1) << 4) + (where[1] << 1) + (m & 1))
    m, j = grid(2 * NU, NF)
    own_slabs = hot(j == (((m & 15) >> 2) << 4) + ((where[1] >> 1) << 2) + ((m & 1) << 1) + ((m >> 1) & 1))
    inv[TIMES:] = table[CUT:]
    for to_inv, to_fwd, part, rows in ((inv, fwd, table, slabs), (own_inv, own_fwd, own_table, own_slabs)):
        count = rows.shape[0] // 2
        rows = nt(rows, holds)
        first = iota(rows.shape, 0) < count
        pick = jnp.concatenate([jnp.where(first, rows, 0.0), jnp.where(first, 0.0, rows)], axis=1).astype(BF)
        for n, (a, b) in enumerate(SPANS[:2]):
            to_fwd[:, BLOCK * n : BLOCK * (n + 1)] = nn(pick, forward[:, a:b]).astype(BF)
        picked = jnp.concatenate([nn(pick, forward[:, a:b]).astype(BF) for a, b in SPANS[2:]], axis=1)
        to_inv[:CUT] = part[:CUT]
        to_inv[CUT : CUT + 4 * count] = jnp.concatenate(two_terms(nn(picked, part[CUT:])), axis=0)
    m, p = grid(POINTS * NI, POINTS)
    marks = nt(hot((m >> 2) == p), (onset[...] - ONSET_MID).astype(F32).astype(BF))
    m, i = grid(POINTS * NI, NI)
    marks = jnp.where((m & 3) == i, marks, 0.0).sum(axis=1, keepdims=True)
    own_marks[...] = jnp.broadcast_to(marks, (POINTS * NI, LANES)).astype(I32) + ONSET_MID
    for copy in copies[4:]:
        copy.wait()


def middle_kernel(got, _, out, rows):
    rows[...] = got[...].astype(F32).reshape(8 * NA, LANES)
    line = jnp.concatenate([rows[pl.ds(e, NA, stride=8), :] for e in range(NX + 1)], axis=1).astype(BF)
    m, a = grid(NA * NI, NA)
    spread = nn(hot((m >> 2) == a), line)
    m, lane = grid(NA * NI, LANES)
    stacked = []
    for e in range(NX + 1):
        piece = spread[:, LANES * e : LANES * (e + 1)]
        for part in range(2):
            fits = ((lane & 3) == (m & 3)) & ((lane >> 6) == part)
            stacked.append(jnp.where(fits, piece, 0.0))
    stacked = jnp.concatenate(stacked, axis=0).astype(BF)
    p, lane = grid(POINTS, LANES)
    turned = nt(hot(((lane >> 2) & 15) == p), stacked)
    marks = turned[:8, LANES * NX :] + turned[8:, LANES * NX :]
    for x in range(NX):
        message = jnp.concatenate([turned[:, LANES * x : LANES * (x + 1)], marks], axis=0).astype(BF)
        for z in range(NZ):
            out[x, z] = message


def swap(a, b):
    low = iota(a.shape, 1) < LANES // 2
    return (
        jnp.where(low, a, pltpu.roll(b, LANES // 2, 1)),
        jnp.where(low, pltpu.roll(a, LANES // 2, 1), b),
    )


def convolve(src, mat_re, mat_im, out):
    a = nt(src, mat_re[...])
    b = nt(src, mat_im[...])
    parts = (a[:POINTS] - b[POINTS:], a[POINTS:] + b[:POINTS])
    for c in range(NC):
        at = slice(8 * c, 8 * (c + 1))
        for w in range(NW):
            slabs = [part[at, LANES * w : LANES * (w + 1)] for part in parts]
            message = jnp.concatenate(slabs, axis=0).astype(BF)
            for v in range(NY // NW):
                out[NW * v + w, c] = message


def first_conv_kernel(place, got, mat_re, mat_im, out, src, own_marks, marks, rows):
    height = POINTS + 8
    rows[...] = got[...].astype(F32).reshape(NX * NZ * height, LANES)
    for z in range(NZ):
        for half in range(2):
            a = rows[pl.ds((2 * half * NZ + z) * height, POINTS), :]
            b = rows[pl.ds(((2 * half + 1) * NZ + z) * height, POINTS), :]
            at = LANES * (2 * z + half)
            re, im = swap(a, b)
            src[:POINTS, at : at + LANES] = re.astype(BF)
            src[POINTS:, at : at + LANES] = im.astype(BF)
    x, y, c, z = (place[n : n + 1, :] for n in range(4))
    mine = (y & 1) + 2 * c
    own = jnp.zeros((8, LANES), F32)
    picked = []
    p, _ = grid(POINTS, LANES)
    for half in range(2):
        a = b = jnp.zeros((8, LANES), F32)
        for n in range(NZ):
            at = (2 * half * NZ + n) * height + POINTS
            a = jnp.where(z == n, rows[at : at + 8, :], a)
            b = jnp.where(z == n, rows[at + NZ * height : at + NZ * height + 8, :], b)
        blocks = swap(a, b)
        for h in range(2):
            own = jnp.where(mine == half + 2 * h, blocks[h], own)
        blocks = jnp.concatenate(blocks, axis=0)
        for n in range(2):
            row = jnp.where(p == 4 * x + 2 * c + n, blocks, 0.0).sum(axis=0, keepdims=True)
            marks[2 * n + half : 2 * n + half + 1, :] = row.astype(I32) + ONSET_MID
    own_marks[...] = own.astype(I32) + ONSET_MID
    convolve(src[...], mat_re, mat_im, out)


def next_conv_kernel(got, first, mat_re, mat_im, out, rows, more):
    rows[...] = got[...].astype(F32).reshape(NG * NZ * 8, LANES)
    for z in range(NZ):
        for p in range(2):
            for part in range(2):
                for half in range(2):
                    slab = rows[pl.ds(8 * z + 4 * p + 2 * part + half, NG, stride=8 * NZ), :]
                    more[pl.ds(2 * POINTS * (2 * z + half) + POINTS * part + p, NG, stride=2), :] = slab
    blocks = [more[2 * POINTS * n : 2 * POINTS * (n + 1), :] for n in range(COLS // LANES)]
    src = (first[...].astype(F32) + jnp.concatenate(blocks, axis=1)).astype(BF)
    convolve(src, mat_re, mat_im, out)


def window(spectra, marks, inv, fwd):
    t = iota((BLOCK, 1), 0)
    count = fwd.shape[0]
    front = jnp.where(t + SPANS[0][0] < marks, nn(inv[:BLOCK], spectra), 0.0).astype(BF)
    rest = nn(inv[BLOCK : CUT + 2 * count], spectra)
    back = jnp.where(t + SPANS[1][0] >= NT - marks, rest[:BLOCK], 0.0).astype(BF)
    fixed = rest[BLOCK : BLOCK + count] + rest[BLOCK + count :]
    return nn(fwd[:, :BLOCK], front) + nn(fwd[:, BLOCK:], back) + fixed


def window_slabs(got, inv, fwd, marks, rows, turn):
    rows[...] = got[...].astype(F32).reshape(NA * 16, LANES)
    every = []
    for p in range(8):
        parts = [rows[pl.ds(8 * part + p, NA, stride=16), :] for part in range(2)]
        every.append(jnp.concatenate(parts, axis=0).astype(BF))
    mark = [marks[p : p + 1, :] for p in range(8)]
    spec = window(jnp.concatenate(every, axis=1), jnp.concatenate(mark, axis=1), inv, fwd)
    for p in range(8):
        for part in range(2):
            slab = spec[NU * part : NU * (part + 1), LANES * p : LANES * (p + 1)]
            turn[pl.ds(8 * part + p, NU, stride=16), :] = slab
    return every, turn[...].reshape(NU, 16, LANES)


def time_kernel(got, inv, fwd, marks, out, rows, turn):
    out[...] = window_slabs(got, inv, fwd, marks, rows, turn)[1].astype(BF)


def last_time_kernel(got, inv, fwd, marks, place, out, rows, turn, tail):
    every, message = window_slabs(got, inv, fwd, marks, rows, turn)
    m, r = grid(NU * NI, LANES)
    y = place[1:2, :]
    w = y & 1
    y = (y & 6) + ((m >> 2) & 1)
    own = ((m >> 4) << 6) + (y << 3) + (((m >> 3) & 1) << 2) + (m & 3)
    own = hot(r + LANES * w == own)
    for h in range(2):
        taken = nt(own, jnp.concatenate(every[4 * h : 4 * (h + 1)], axis=0))
        for u in range(NU):
            tail[8 * u + NI * h : 8 * u + NI * (h + 1), :] = taken[NI * u : NI * (u + 1)]
    out[...] = jnp.concatenate([message, tail[...].reshape(NU, 8, LANES)], axis=1).astype(BF)


def time_copies_kernel(got, inv, fwd, marks, out, rows, turn):
    rows[...] = got[...].astype(F32).reshape(NF * 8, LANES)
    every = []
    for p in range(2):
        parts = []
        for x in range(NX):
            for part in range(2):
                at = [8 * x + 4 * p + 2 * part + half for half in range(2)]
                halves = [rows[pl.ds(n, NA, stride=8 * NX), :] for n in at]
                parts.append(jnp.concatenate(halves, axis=1))
        every.append(jnp.concatenate(parts, axis=0).astype(BF))
    mark = [marks[n : n + 1, :] for n in range(4)]
    spectra = window(jnp.concatenate(every, axis=1), jnp.concatenate(mark, axis=1), inv, fwd)
    for p in range(2):
        spec = spectra[:, BLOCK * p : BLOCK * (p + 1)]
        for part in range(2):
            for half in range(2):
                slab = spec[NG * part : NG * (part + 1), LANES * half : LANES * (half + 1)]
                turn[pl.ds(4 * p + 2 * part + half, NG, stride=8), :] = slab
    message = turn[...].reshape(NG, 8, LANES).astype(BF)
    for z in range(NZ):
        out[:, z] = message


def correlate(got, mat_re, mat_im):
    parts = []
    for part in range(2):
        halves = []
        for half in range(2):
            at = 8 * part
            both = [sum(got[4 * x + 2 * c + half].astype(F32)[at : at + 8] for x in range(NX)) for c in range(NC)]
            halves.append(jnp.concatenate(both, axis=0))
        parts.append(jnp.concatenate(halves, axis=1))
    straight = jnp.concatenate(parts, axis=0).astype(BF)
    turned = jnp.concatenate([parts[1], -parts[0]], axis=0).astype(BF)
    for z in range(NZ):
        at = slice(BLOCK * z, BLOCK * (z + 1))
        yield z, nn(straight, mat_re[:, at]) + nn(turned, mat_im[:, at])


def corr_kernel(got, mat_re, mat_im, out, turn):
    for z, block in correlate(got, mat_re, mat_im):
        for x in range(NX):
            for part in range(2):
                for half in range(2):
                    at = (x * NZ + z) * 16 + 2 * part + half
                    row = POINTS * part + 4 * x
                    turn[pl.ds(at, 4, stride=4), :] = block[row : row + 4, LANES * half : LANES * (half + 1)]
    out[...] = turn[...].reshape(NX * NZ, 16, LANES).astype(BF)


def last_corr_kernel(got, mat_re, mat_im, out):
    for z, block in correlate(got, mat_re, mat_im):
        for half in range(2):
            at = slice(LANES * half, LANES * (half + 1))
            a, b = swap(block[:POINTS, at], block[POINTS:, at])
            out[2 * half, z] = a.astype(BF)
            out[2 * half + 1, z] = b.astype(BF)


def sum_kernel(got, out):
    total = got[...].astype(F32).reshape(NX, NZ, 16, LANES).sum(axis=1)
    for c in range(NC):
        message = total[:, 8 * c : 8 * (c + 1)].reshape(NX * 8, LANES).astype(BF)
        for y in range(NY):
            out[y, c] = message


def last_sum_kernel(got, out):
    total = got[...].astype(F32).sum(axis=1).astype(BF)
    total = jnp.concatenate([total[x] for x in range(NX)], axis=1)
    m, p = grid(LANES, POINTS)
    turned = nn(hot(((m >> 2) & 15) == p), total)
    m, n = grid(LANES, NX * LANES)
    turned = jnp.where(((n & 3) == (m & 3)) & (((n >> 6) & 1) == (m >> 6)), turned, 0.0).astype(BF)
    sent = nt(hot(((m & 7) == (n >> 7)) & ((m >> 3) == ((n >> 2) & 15))), turned)
    out[...] = sent.reshape(NA, 8, LANES).astype(BF)


def keep_own(spectra, inv, marks):
    t = iota((POINTS * NI, LANES), 1)
    trace = [nt(spectra, inv[a:b]) for a, b in ((0, CUT), (TIMES, TIMES + KEPT - CUT))]
    trace = jnp.concatenate(trace, axis=1)
    pieces = [trace[:, LANES * n : LANES * (n + 1)] for n in range(KEPT // LANES)]
    none = jnp.zeros_like(pieces[0])
    front = [jnp.where(t + SPANS[0][0] + LANES * n < marks, pieces[n], 0.0) for n in range(2)]
    back = [jnp.where(t + SPANS[1][0] + LANES * n >= NT - marks, pieces[2 + n], 0.0) for n in range(2)]
    return jnp.concatenate([pieces[4], *front, none, none, *back, pieces[5]], axis=1)


def last_kernel(got, tail, inv, marks, focus, plus_out, minus_out, plus, minus, spectra, sems):
    rows = got[...].astype(F32).reshape(8 * NA, LANES).T.astype(BF)
    m, k = grid(8 * NA, LANES)
    own = jnp.zeros((POINTS * NI, LANES), F32)
    for part in range(2):
        place = hot(((m & 7) < NX) & (k == ((m & 7) << 5) + 16 * part + (m >> 3)))
        own = own + nn(rows[NF * part : NF * (part + 1)], place)
    trace = keep_own(own.astype(BF), inv[...], marks[...])
    for p in range(POINTS):
        plus[p] = (focus[p].astype(F32) + trace[NI * p : NI * (p + 1)]).astype(BF)
    first = pltpu.make_async_copy(plus, plus_out, sems.at[0])
    first.start()
    own = []
    for x in range(NX):
        both = [sum(tail[4 * x + 2 * c + w].astype(F32)[16:] for w in range(NW)) for c in range(NC)]
        own.append(jnp.concatenate(both, axis=0))
    own = jnp.concatenate(own, axis=1).astype(BF)
    n, k = grid(NX * LANES, LANES)
    same = (n >> 7) * 32 + (n & 31) == k
    own = [nn(own, hot(same & (((n >> 5) & 3) == p))) for p in range(4)]
    for p in range(POINTS):
        spectra[NI * p : NI * (p + 1), :] = own[p & 3][NI * (p >> 2) : NI * ((p >> 2) + 1)]
    trace = keep_own(spectra[...].astype(BF), inv[...], marks[...])
    for p in range(POINTS):
        minus[p] = trace[NI * p : NI * (p + 1)].astype(BF)
    second = pltpu.make_async_copy(minus, minus_out, sems.at[1])
    second.start()
    first.wait()
    second.wait()


def call(kernel, outs, scratch=(), scalars=0, far=0, copies=0, far_outs=0):
    single = not isinstance(outs, list)
    shapes = [jax.ShapeDtypeStruct(shape, dtype) for shape, dtype in ([outs] if single else outs)]

    def run(*args):
        out_spaces = [pltpu.VMEM] * (len(shapes) - far_outs) + [pltpu.HBM] * far_outs
        spaces = [pltpu.SMEM] * scalars + [pltpu.HBM] * far + [pltpu.VMEM] * (len(args) - scalars - far)
        args = [
            pltpu.with_memory_space_constraint(arg, pltpu.HBM) if space is pltpu.HBM else arg
            for arg, space in zip(args, spaces)
        ]
        got = pl.pallas_call(
            kernel,
            out_shape=shapes,
            in_specs=[pl.BlockSpec(memory_space=space) for space in spaces],
            out_specs=[pl.BlockSpec(memory_space=space) for space in out_spaces],
            scratch_shapes=[pltpu.VMEM(shape, dtype) for shape, dtype in scratch]
            + [pltpu.SemaphoreType.DMA((copies,))] * (copies > 0),
            compiler_params=pltpu.CompilerParams(vmem_limit_bytes=VMEM_LIMIT),
        )(*args)
        return got[0] if single else got

    return run


def exchange(values, axes):
    return lax.all_to_all(values, axes, 0, 0, tiled=True)


def shards(focus_start, onset, bins, refl_real, refl_imag):
    mats = (refl_real[0], refl_imag[0])
    where = jnp.stack([lax.axis_index(axis) for axis in ("x", ("v", "w"), "c", "z")]).astype(I32)
    bins = bins.reshape(1, NF)
    onset = onset.T
    forward, wide, inverse = base_tables()
    own = (POINTS, NI, NT)

    scratch = [((1, NF), I32), ((NI, POINTS), I32), (own, BF), ((NF, 2 * NT), BF), ((POINTS * NI, NT), F32)]
    run = call(start_kernel, ((NA, 8, LANES), BF), scratch, far=4, copies=4)
    got = exchange(run(bins, onset, focus_start, wide), ("v", "w", "c"))
    outs = [((8, LANES), I32), ((TIMES + KEPT - CUT, LANES), BF), ((OWN_TIMES, 2 * NA), BF), ((2 * NG, CUT), BF), ((2 * NU, CUT), BF)]
    outs += [((POINTS * NI, LANES), I32), ((BLOCK, COLS), BF), ((BLOCK, COLS), BF)]
    scratch = [((1, NF), I32), ((NI, POINTS), I32), ((2 * NF, NT), BF), ((KEPT, LANES), BF)]
    run = call(tables_kernel, outs, scratch, scalars=1, far=6, copies=6)
    place, inv, own_inv, fwd, own_fwd, kept, *mats = run(where, bins, onset, forward, inverse, *mats)
    send = call(middle_kernel, ((NX, NZ, POINTS + 8, LANES), BF), [((8 * NA, LANES), F32)])(got, fwd)
    got = exchange(send.reshape(NX * NZ, POINTS + 8, LANES), ("x", "z"))
    outs = [((NY, NC, 16, LANES), BF), ((2 * POINTS, COLS), BF), ((8, LANES), I32), ((4, LANES), I32)]
    scratch = [((NX * NZ * (POINTS + 8), LANES), F32)]
    send, first, own_marks, marks = call(first_conv_kernel, outs, scratch)(place, got, *mats)
    for step in range(ITERS):
        got = exchange(send.reshape(NA, 16, LANES), ("v", "w", "c"))
        scratch = [((NA * 16, LANES), F32), ((NU * 16, LANES), F32)]
        tables = (own_inv, own_fwd, own_marks)
        if step == ITERS - 1:
            scratch = scratch + [((NU * 8, LANES), F32)]
            send = call(last_time_kernel, ((NU, 24, LANES), BF), scratch)(got, *tables, place)
            got = exchange(send, ("x", "c", "w"))
            break
        send = call(time_kernel, ((NU, 16, LANES), BF), scratch)(got, *tables)
        got = exchange(send, ("x", "c", "w"))
        send = call(corr_kernel, ((NX * NZ, 16, LANES), BF), [((NX * NZ * 16, LANES), F32)])(got, *mats)
        got = exchange(send, ("x", "z"))
        send = call(sum_kernel, ((NY, NC, NX * 8, LANES), BF))(got)
        got = exchange(send.reshape(NA, NX * 8, LANES), ("v", "w", "c"))
        scratch = [((NF * 8, LANES), F32), ((NG * 8, LANES), F32)]
        send = call(time_copies_kernel, ((NG, NZ, 8, LANES), BF), scratch)(got, inv, fwd, marks)
        got = exchange(send.reshape(NG * NZ, 8, LANES), ("x", "c", "z"))
        scratch = [((NG * NZ * 8, LANES), F32), ((2 * POINTS * COLS // LANES, LANES), F32)]
        send = call(next_conv_kernel, ((NY, NC, 16, LANES), BF), scratch)(got, first, *mats)
    tail = got
    send = call(last_corr_kernel, ((NX, NZ, POINTS, LANES), BF))(got, *mats)
    got = exchange(send.reshape(NX * NZ, POINTS, LANES), ("x", "z")).reshape(NX, NZ, POINTS, LANES)
    send = call(last_sum_kernel, ((NA, 8, LANES), BF))(got)
    got = exchange(send, ("v", "w", "c"))
    scratch = [(own, BF), (own, BF), ((POINTS * NI, LANES), F32)]
    run = call(last_kernel, [(own, BF), (own, BF)], scratch, copies=2, far_outs=2)
    focus_plus, focus_minus = run(got, tail, inv, kept, focus_start)
    return (focus_plus, focus_minus)


def solution(mesh):
    fine = Mesh(mesh.devices.reshape(NX, NY // NW, NW, NC, NZ), ("x", "v", "w", "c", "z"))
    receivers = ("z", "x", "v", "w", "c")
    slabs = ("x", "v", "w", "c")
    return jax.shard_map(
        shards,
        mesh=fine,
        in_specs=(
            P(None, receivers, None),
            P(None, receivers),
            P(),
            P(slabs, "z", None),
            P(slabs, "z", None),
        ),
        out_specs=(P(None, receivers, None), P(None, receivers, None)),
        check_vma=False,
    )
```

```python
import math

import jax
import jax.numpy as jnp
import numpy as np
from jax import lax
from jax.experimental import pallas as pl
from jax.experimental.pallas import tpu as pltpu
from jax.sharding import Mesh
from jax.sharding import PartitionSpec as P

FLO = 8
ITERS = 2
NX, NY, NC, NZ = 4, 8, 2, 8
NW = 2
NA, NG, NI = NY * NC, NX * NC, 4
NU = NG * NW
NF, POINTS, NT = 64, 16, 1024
BLOCK, COLS = 256, 2048
LANES = 128
SPANS = ((128, 384), (640, 896), (0, 128), (896, 1024))
CUT = 512
KEPT = 768
TIMES = CUT + 2 * 2 * NG
OWN_TIMES = CUT + 2 * 2 * NU
ONSET_MID = 256
BF, F32, I32 = jnp.bfloat16, jnp.float32, jnp.int32
VMEM_LIMIT = 8 * 1024 * 1024


def base_tables():
    phase = (np.arange(NT)[None, :] * (FLO + np.arange(NF))[:, None]) % NT
    angle = phase.astype(np.float32) * np.float32(2.0 * math.pi / NT)
    rows = np.concatenate([np.cos(angle), -np.sin(angle)], axis=0)
    forward = (rows * np.float32(1.0 / math.sqrt(NT))).astype(BF)
    inverse = (rows * np.float32(math.sqrt(2.0 / NF))).astype(BF)
    inverse = np.concatenate([inverse[:, a:b] for a, b in SPANS], axis=1)
    wide = np.concatenate([forward[:NF], forward[NF:]], axis=1)
    return forward, wide, np.ascontiguousarray(inverse.T)


def iota(shape, dim):
    return lax.broadcasted_iota(I32, shape, dim)


def grid(rows, cols):
    return iota((rows, cols), 0), iota((rows, cols), 1)


def hot(mask):
    return jnp.where(mask, jnp.float32(1), jnp.float32(0)).astype(BF)


def nn(a, b):
    return lax.dot_general(a, b, (((1,), (0,)), ((), ())), preferred_element_type=F32)


def nt(a, b):
    return lax.dot_general(a, b, (((1,), (1,)), ((), ())), preferred_element_type=F32)


def two_terms(value):
    high = value.astype(BF)
    return high, (value - high.astype(F32)).astype(BF)


def slab_of_bin(bins):
    row, _ = grid(NF, NF)
    return hot(row == bins)


def fetch(pairs, sems):
    copies = [pltpu.make_async_copy(src, dst, sems.at[n]) for n, (src, dst) in enumerate(pairs)]
    for copy in copies:
        copy.start()
    return copies


def start_kernel(bins_in, onset_in, focus_in, base_in, out, bins, onset, focus, base, flat, sems):
    copies = fetch([(bins_in, bins), (onset_in, onset), (focus_in, focus), (base_in, base)], sems)
    copies[0].wait()
    m, j = grid(8 * NA, NF)
    place = hot(((m & 7) < NX) & (j == ((m & 7) << 4) + (m >> 3)))
    order = nt(place, slab_of_bin(bins[...])).astype(BF)
    copies[1].wait()
    p, lane = grid(POINTS, LANES)
    spread = hot((((lane >> 2) & 15) == p) & ((lane >> 6) == (p >> 3)))
    marks = nn((onset[...] - ONSET_MID).astype(F32).astype(BF), spread)
    i, lane = grid(NI, LANES)
    marks = jnp.where((lane & 3) == i, marks, 0.0).sum(axis=0, keepdims=True)
    copies[2].wait()
    for p in range(POINTS):
        flat[NI * p : NI * (p + 1), :] = focus[p].astype(F32)
    rows = flat[: POINTS * NI, :].astype(BF)
    none = jnp.zeros_like(rows)
    copies[3].wait()
    spec = nt(base[:, :NT], jnp.concatenate([rows, none], axis=0))
    spec = spec + nt(base[:, NT:], jnp.concatenate([none, rows], axis=0))
    sent = nn(order, spec.astype(BF))
    sent = jnp.where((iota((8 * NA, LANES), 0) & 7) == NX, marks, sent)
    out[...] = sent.reshape(NA, 8, LANES).astype(BF)


def tables_kernel(
    where, bins_in, onset_in, forward_in, inverse_in, re_in, im_in,
    place, inv, own_inv, fwd, own_fwd, own_marks, re, im,
    bins, onset, forward, inverse, sems,
):
    pairs = [(bins_in, bins), (onset_in, onset), (forward_in, forward), (inverse_in, inverse), (re_in, re), (im_in, im)]
    copies = fetch(pairs, sems)
    for copy in copies[:4]:
        copy.wait()
    row, _ = grid(8, LANES)
    value = jnp.zeros((8, LANES), I32)
    for n in range(4):
        value = jnp.where(row == n, where[n], value)
    place[...] = value
    held = bins[...].astype(F32).astype(BF)
    j, k = grid(NF, LANES)
    arrival = ((k >> 5) << 4) + (k & 15)
    at_k = nn(held, hot(j == arrival))
    j, n = grid(NF, 2 * NA)
    at_own = nn(held, hot(j == (where[0] << 4) + (n & 15)))
    row, k = grid(LANES, LANES)
    order = hot(((row >> 6) == ((k >> 4) & 1)) & ((row & 63).astype(F32) == at_k))
    row, n = grid(LANES, 2 * NA)
    own_order = hot(((row >> 6) == (n >> 4)) & ((row & 63).astype(F32) == at_own))
    base = inverse[...]
    table = nn(base, order).astype(BF)
    own_table = nn(base, own_order).astype(BF)
    holds = slab_of_bin(bins[...])
    m, j = grid(2 * NG, NF)
    slabs = hot(j == (((m & 7) >> 1) << 4) + (where[1] << 1) + (m & 1))
    m, j = grid(2 * NU, NF)
    own_slabs = hot(j == (((m & 15) >> 2) << 4) + ((where[1] >> 1) << 2) + ((m & 1) << 1) + ((m >> 1) & 1))
    inv[TIMES:] = table[CUT:]
    for to_inv, to_fwd, part, rows in ((inv, fwd, table, slabs), (own_inv, own_fwd, own_table, own_slabs)):
        count = rows.shape[0] // 2
        rows = nt(rows, holds)
        first = iota(rows.shape, 0) < count
        pick = jnp.concatenate([jnp.where(first, rows, 0.0), jnp.where(first, 0.0, rows)], axis=1).astype(BF)
        for n, (a, b) in enumerate(SPANS[:2]):
            to_fwd[:, BLOCK * n : BLOCK * (n + 1)] = nn(pick, forward[:, a:b]).astype(BF)
        picked = jnp.concatenate([nn(pick, forward[:, a:b]).astype(BF) for a, b in SPANS[2:]], axis=1)
        to_inv[:CUT] = part[:CUT]
        to_inv[CUT : CUT + 4 * count] = jnp.concatenate(two_terms(nn(picked, part[CUT:])), axis=0)
    m, p = grid(POINTS * NI, POINTS)
    marks = nt(hot((m >> 2) == p), (onset[...] - ONSET_MID).astype(F32).astype(BF))
    m, i = grid(POINTS * NI, NI)
    marks = jnp.where((m & 3) == i, marks, 0.0).sum(axis=1, keepdims=True)
    own_marks[...] = jnp.broadcast_to(marks, (POINTS * NI, LANES)).astype(I32) + ONSET_MID
    for copy in copies[4:]:
        copy.wait()


def middle_kernel(got, _, out, rows):
    rows[: 8 * NA, :] = got[...].astype(F32).reshape(8 * NA, LANES)
    line = jnp.concatenate([rows[pl.ds(e, NA, stride=8), :] for e in range(NX + 1)], axis=1).astype(BF)
    m, a = grid(NA * NI, NA)
    spread = nn(hot((m >> 2) == a), line)
    m, lane = grid(NA * NI, LANES)
    stacked = []
    for e in range(NX + 1):
        piece = spread[:, LANES * e : LANES * (e + 1)]
        for part in range(2):
            fits = ((lane & 3) == (m & 3)) & ((lane >> 6) == part)
            stacked.append(jnp.where(fits, piece, 0.0))
    stacked = jnp.concatenate(stacked, axis=0).astype(BF)
    p, lane = grid(POINTS, LANES)
    turned = nt(hot(((lane >> 2) & 15) == p), stacked)
    marks = turned[:8, LANES * NX :] + turned[8:, LANES * NX :]
    for x in range(NX):
        message = jnp.concatenate([turned[:, LANES * x : LANES * (x + 1)], marks], axis=0).astype(BF)
        for z in range(NZ):
            out[x, z] = message


def swap(a, b):
    low = iota(a.shape, 1) < LANES // 2
    return (
        jnp.where(low, a, pltpu.roll(b, LANES // 2, 1)),
        jnp.where(low, pltpu.roll(a, LANES // 2, 1), b),
    )


def convolve(src, mat_re, mat_im, out):
    a = nt(src, mat_re[...])
    b = nt(src, mat_im[...])
    parts = (a[:POINTS] - b[POINTS:], a[POINTS:] + b[:POINTS])
    for c in range(NC):
        at = slice(8 * c, 8 * (c + 1))
        for w in range(NW):
            slabs = [part[at, LANES * w : LANES * (w + 1)] for part in parts]
            message = jnp.concatenate(slabs, axis=0).astype(BF)
            for v in range(NY // NW):
                out[NW * v + w, c] = message


def first_conv_kernel(place, got, mat_re, mat_im, out, src, own_marks, marks, rows):
    height = POINTS + 8
    rows[...] = got[...].astype(F32).reshape(NX * NZ * height, LANES)
    for z in range(NZ):
        for half in range(2):
            a = rows[pl.ds((2 * half * NZ + z) * height, POINTS), :]
            b = rows[pl.ds(((2 * half + 1) * NZ + z) * height, POINTS), :]
            at = LANES * (2 * z + half)
            re, im = swap(a, b)
            src[:POINTS, at : at + LANES] = re.astype(BF)
            src[POINTS:, at : at + LANES] = im.astype(BF)
    x, y, c, z = (place[n : n + 1, :] for n in range(4))
    mine = (y & 1) + 2 * c
    own = jnp.zeros((8, LANES), F32)
    line, _ = grid(8, LANES)
    few = jnp.zeros((8, LANES), F32)
    p, _ = grid(POINTS, LANES)
    for half in range(2):
        a = b = jnp.zeros((8, LANES), F32)
        for n in range(NZ):
            at = (2 * half * NZ + n) * height + POINTS
            a = jnp.where(z == n, rows[at : at + 8, :], a)
            b = jnp.where(z == n, rows[at + NZ * height : at + NZ * height + 8, :], b)
        blocks = swap(a, b)
        for h in range(2):
            own = jnp.where(mine == half + 2 * h, blocks[h], own)
        blocks = jnp.concatenate(blocks, axis=0)
        for n in range(2):
            row = jnp.where(p == 4 * x + 2 * c + n, blocks, 0.0).sum(axis=0, keepdims=True)
            few = jnp.where(line == 2 * n + half, row, few)
    marks[...] = few.astype(I32) + ONSET_MID
    own_marks[...] = own.astype(I32) + ONSET_MID
    convolve(src[...], mat_re, mat_im, out)


def next_conv_kernel(got, first, mat_re, mat_im, out, rows, more):
    rows[: NG * NZ * 8, :] = got[...].astype(F32).reshape(NG * NZ * 8, LANES)
    for z in range(NZ):
        for p in range(2):
            for part in range(2):
                for half in range(2):
                    slab = rows[pl.ds(8 * z + 4 * p + 2 * part + half, NG, stride=8 * NZ), :]
                    more[pl.ds(2 * POINTS * (2 * z + half) + POINTS * part + p, NG, stride=2), :] = slab
    blocks = [more[2 * POINTS * n : 2 * POINTS * (n + 1), :] for n in range(COLS // LANES)]
    src = (first[...].astype(F32) + jnp.concatenate(blocks, axis=1)).astype(BF)
    convolve(src, mat_re, mat_im, out)


def window(spectra, marks, inv, fwd):
    t = iota((BLOCK, 1), 0)
    count = fwd.shape[0]
    front = jnp.where(t + SPANS[0][0] < marks, nn(inv[:BLOCK], spectra), 0.0).astype(BF)
    rest = nn(inv[BLOCK : CUT + 2 * count], spectra)
    back = jnp.where(t + SPANS[1][0] >= NT - marks, rest[:BLOCK], 0.0).astype(BF)
    fixed = rest[BLOCK : BLOCK + count] + rest[BLOCK + count :]
    return nn(fwd[:, :BLOCK], front) + nn(fwd[:, BLOCK:], back) + fixed


def window_slabs(got, inv, fwd, marks, rows, turn):
    rows[: NA * 16, :] = got[...].astype(F32).reshape(NA * 16, LANES)
    every = []
    for p in range(8):
        parts = [rows[pl.ds(8 * part + p, NA, stride=16), :] for part in range(2)]
        every.append(jnp.concatenate(parts, axis=0).astype(BF))
    mark = [marks[p : p + 1, :] for p in range(8)]
    spec = window(jnp.concatenate(every, axis=1), jnp.concatenate(mark, axis=1), inv, fwd)
    for p in range(8):
        for part in range(2):
            slab = spec[NU * part : NU * (part + 1), LANES * p : LANES * (p + 1)]
            turn[pl.ds(8 * part + p, NU, stride=16), :] = slab
    return every, turn[: NU * 16, :].reshape(NU, 16, LANES)


def time_kernel(got, inv, fwd, marks, out, rows, turn):
    out[...] = window_slabs(got, inv, fwd, marks, rows, turn)[1].astype(BF)


def last_time_kernel(got, inv, fwd, marks, place, out, rows, turn, tail):
    every, message = window_slabs(got, inv, fwd, marks, rows, turn)
    m, r = grid(NU * NI, LANES)
    y = place[1:2, :]
    w = y & 1
    y = (y & 6) + ((m >> 2) & 1)
    own = ((m >> 4) << 6) + (y << 3) + (((m >> 3) & 1) << 2) + (m & 3)
    own = hot(r + LANES * w == own)
    for h in range(2):
        taken = nt(own, jnp.concatenate(every[4 * h : 4 * (h + 1)], axis=0))
        for u in range(NU):
            tail[8 * u + NI * h : 8 * u + NI * (h + 1), :] = taken[NI * u : NI * (u + 1)]
    out[...] = jnp.concatenate([message, tail[: NU * 8, :].reshape(NU, 8, LANES)], axis=1).astype(BF)


def time_copies_kernel(got, inv, fwd, marks, out, rows, turn):
    rows[: NF * 8, :] = got[...].astype(F32).reshape(NF * 8, LANES)
    every = []
    for p in range(2):
        parts = []
        for x in range(NX):
            for part in range(2):
                at = [8 * x + 4 * p + 2 * part + half for half in range(2)]
                halves = [rows[pl.ds(n, NA, stride=8 * NX), :] for n in at]
                parts.append(jnp.concatenate(halves, axis=1))
        every.append(jnp.concatenate(parts, axis=0).astype(BF))
    mark = [marks[n : n + 1, :] for n in range(4)]
    spectra = window(jnp.concatenate(every, axis=1), jnp.concatenate(mark, axis=1), inv, fwd)
    for p in range(2):
        spec = spectra[:, BLOCK * p : BLOCK * (p + 1)]
        for part in range(2):
            for half in range(2):
                slab = spec[NG * part : NG * (part + 1), LANES * half : LANES * (half + 1)]
                turn[pl.ds(4 * p + 2 * part + half, NG, stride=8), :] = slab
    message = turn[: NG * 8, :].reshape(NG, 8, LANES).astype(BF)
    for z in range(NZ):
        out[:, z] = message


def correlate(got, mat_re, mat_im):
    parts = []
    for part in range(2):
        halves = []
        for half in range(2):
            at = 8 * part
            both = [sum(got[4 * x + 2 * c + half].astype(F32)[at : at + 8] for x in range(NX)) for c in range(NC)]
            halves.append(jnp.concatenate(both, axis=0))
        parts.append(jnp.concatenate(halves, axis=1))
    straight = jnp.concatenate(parts, axis=0).astype(BF)
    turned = jnp.concatenate([parts[1], -parts[0]], axis=0).astype(BF)
    for z in range(NZ):
        at = slice(BLOCK * z, BLOCK * (z + 1))
        yield z, nn(straight, mat_re[:, at]) + nn(turned, mat_im[:, at])


def corr_kernel(got, mat_re, mat_im, out, turn):
    for z, block in correlate(got, mat_re, mat_im):
        for x in range(NX):
            for part in range(2):
                for half in range(2):
                    at = (x * NZ + z) * 16 + 2 * part + half
                    row = POINTS * part + 4 * x
                    turn[pl.ds(at, 4, stride=4), :] = block[row : row + 4, LANES * half : LANES * (half + 1)]
    out[...] = turn[: NX * NZ * 16, :].reshape(NX * NZ, 16, LANES).astype(BF)


def last_corr_kernel(got, mat_re, mat_im, out):
    for z, block in correlate(got, mat_re, mat_im):
        for half in range(2):
            at = slice(LANES * half, LANES * (half + 1))
            a, b = swap(block[:POINTS, at], block[POINTS:, at])
            out[2 * half, z] = a.astype(BF)
            out[2 * half + 1, z] = b.astype(BF)


def sum_kernel(got, out):
    total = got[...].astype(F32).reshape(NX, NZ, 16, LANES).sum(axis=1)
    for c in range(NC):
        message = total[:, 8 * c : 8 * (c + 1)].reshape(NX * 8, LANES).astype(BF)
        for y in range(NY):
            out[y, c] = message


def last_sum_kernel(got, out):
    total = got[...].astype(F32).sum(axis=1).astype(BF)
    total = jnp.concatenate([total[x] for x in range(NX)], axis=1)
    m, p = grid(LANES, POINTS)
    turned = nn(hot(((m >> 2) & 15) == p), total)
    m, n = grid(LANES, NX * LANES)
    turned = jnp.where(((n & 3) == (m & 3)) & (((n >> 6) & 1) == (m >> 6)), turned, 0.0).astype(BF)
    sent = nt(hot(((m & 7) == (n >> 7)) & ((m >> 3) == ((n >> 2) & 15))), turned)
    out[...] = sent.reshape(NA, 8, LANES).astype(BF)


def keep_own(spectra, inv, marks):
    t = iota((spectra.shape[0], LANES), 1)
    trace = [nt(spectra, inv[a:b]) for a, b in ((0, CUT), (TIMES, TIMES + KEPT - CUT))]
    trace = jnp.concatenate(trace, axis=1)
    pieces = [trace[:, LANES * n : LANES * (n + 1)] for n in range(KEPT // LANES)]
    none = jnp.zeros_like(pieces[0])
    front = [jnp.where(t + SPANS[0][0] + LANES * n < marks, pieces[n], 0.0) for n in range(2)]
    back = [jnp.where(t + SPANS[1][0] + LANES * n >= NT - marks, pieces[2 + n], 0.0) for n in range(2)]
    return jnp.concatenate([pieces[4], *front, none, none, *back, pieces[5]], axis=1)


def last_kernel(got, tail, inv, marks, focus, plus_out, minus_out, plus, minus, spectra, sems):
    own = []
    for x in range(NX):
        both = [sum(tail[4 * x + 2 * c + w].astype(F32)[16:] for w in range(NW)) for c in range(NC)]
        own.append(jnp.concatenate(both, axis=0))
    own = jnp.concatenate(own, axis=1).astype(BF)
    n, k = grid(NX * LANES, LANES)
    same = (n >> 7) * 32 + (n & 31) == k
    own = [nn(own, hot(same & (((n >> 5) & 3) == p))) for p in range(4)]
    for p in range(POINTS):
        spectra[NI * p : NI * (p + 1), :] = own[p & 3][NI * (p >> 2) : NI * ((p >> 2) + 1)]
    rows = got[...].astype(F32).reshape(8 * NA, LANES).T.astype(BF)
    m, k = grid(8 * NA, LANES)
    own = jnp.zeros((POINTS * NI, LANES), F32)
    for part in range(2):
        place = hot(((m & 7) < NX) & (k == ((m & 7) << 5) + 16 * part + (m >> 3)))
        own = own + nn(rows[NF * part : NF * (part + 1)], place)
    own = jnp.concatenate([own, spectra[: POINTS * NI, :]], axis=0).astype(BF)
    trace = keep_own(own, inv[...], jnp.concatenate([marks[...], marks[...]], axis=0))
    for p in range(POINTS):
        plus[p] = (focus[p].astype(F32) + trace[NI * p : NI * (p + 1)]).astype(BF)
    copies = [pltpu.make_async_copy(plus, plus_out, sems.at[0])]
    copies[0].start()
    for p in range(POINTS):
        at = NI * (POINTS + p)
        minus[p] = trace[at : at + NI].astype(BF)
    copies.append(pltpu.make_async_copy(minus, minus_out, sems.at[1]))
    copies[1].start()
    for copy in copies:
        copy.wait()


def call(kernel, outs, scratch=(), scalars=0, far=0, copies=0, far_outs=0):
    single = not isinstance(outs, list)
    shapes = [jax.ShapeDtypeStruct(shape, dtype) for shape, dtype in ([outs] if single else outs)]

    def run(*args):
        out_spaces = [pltpu.VMEM] * (len(shapes) - far_outs) + [pltpu.HBM] * far_outs
        spaces = [pltpu.SMEM] * scalars + [pltpu.HBM] * far + [pltpu.VMEM] * (len(args) - scalars - far)
        args = [
            pltpu.with_memory_space_constraint(arg, pltpu.HBM) if space is pltpu.HBM else arg
            for arg, space in zip(args, spaces)
        ]
        got = pl.pallas_call(
            kernel,
            out_shape=shapes,
            in_specs=[pl.BlockSpec(memory_space=space) for space in spaces],
            out_specs=[pl.BlockSpec(memory_space=space) for space in out_spaces],
            scratch_shapes=[pltpu.VMEM(shape, dtype) for shape, dtype in scratch]
            + [pltpu.SemaphoreType.DMA((copies,))] * (copies > 0),
            compiler_params=pltpu.CompilerParams(vmem_limit_bytes=VMEM_LIMIT),
        )(*args)
        return got[0] if single else got

    return run


def exchange(values, axes):
    return lax.all_to_all(values, axes, 0, 0, tiled=True)


def shards(focus_start, onset, bins, refl_real, refl_imag):
    mats = (refl_real[0], refl_imag[0])
    where = jnp.stack([lax.axis_index(axis) for axis in ("x", ("v", "w"), "c", "z")]).astype(I32)
    bins = bins.reshape(1, NF)
    onset = onset.T
    forward, wide, inverse = base_tables()
    own = (POINTS, NI, NT)

    scratch = [((1, NF), I32), ((NI, POINTS), I32), (own, BF), ((NF, 2 * NT), BF), ((POINTS * NI + 8, NT), F32)]
    run = call(start_kernel, ((NA, 8, LANES), BF), scratch, far=4, copies=4)
    got = exchange(run(bins, onset, focus_start, wide), ("v", "w", "c"))
    outs = [((8, LANES), I32), ((TIMES + KEPT - CUT, LANES), BF), ((OWN_TIMES, 2 * NA), BF), ((2 * NG, CUT), BF), ((2 * NU, CUT), BF)]
    outs += [((POINTS * NI, LANES), I32), ((BLOCK, COLS), BF), ((BLOCK, COLS), BF)]
    scratch = [((1, NF), I32), ((NI, POINTS), I32), ((2 * NF, NT), BF), ((KEPT, LANES), BF)]
    run = call(tables_kernel, outs, scratch, scalars=1, far=6, copies=6)
    place, inv, own_inv, fwd, own_fwd, kept, *mats = run(where, bins, onset, forward, inverse, *mats)
    send = call(middle_kernel, ((NX, NZ, POINTS + 8, LANES), BF), [((8 * NA + 8, LANES), F32)])(got, fwd)
    got = exchange(send.reshape(NX * NZ, POINTS + 8, LANES), ("x", "z"))
    outs = [((NY, NC, 16, LANES), BF), ((2 * POINTS, COLS), BF), ((8, LANES), I32), ((8, LANES), I32)]
    scratch = [((NX * NZ * (POINTS + 8), LANES), F32)]
    send, first, own_marks, marks = call(first_conv_kernel, outs, scratch)(place, got, *mats)
    for step in range(ITERS):
        got = exchange(send.reshape(NA, 16, LANES), ("v", "w", "c"))
        scratch = [((NA * 16 + 16, LANES), F32), ((NU * 16 + 16, LANES), F32)]
        tables = (own_inv, own_fwd, own_marks)
        if step == ITERS - 1:
            scratch = scratch + [((NU * 8 + 8, LANES), F32)]
            send = call(last_time_kernel, ((NU, 24, LANES), BF), scratch)(got, *tables, place)
            got = exchange(send, ("x", "c", "w"))
            break
        send = call(time_kernel, ((NU, 16, LANES), BF), scratch)(got, *tables)
        got = exchange(send, ("x", "c", "w"))
        send = call(corr_kernel, ((NX * NZ, 16, LANES), BF), [((NX * NZ * 16 + 32, LANES), F32)])(got, *mats)
        got = exchange(send, ("x", "z"))
        send = call(sum_kernel, ((NY, NC, NX * 8, LANES), BF))(got)
        got = exchange(send.reshape(NA, NX * 8, LANES), ("v", "w", "c"))
        scratch = [((NF * 8 + 32, LANES), F32), ((NG * 8 + 8, LANES), F32)]
        send = call(time_copies_kernel, ((NG, NZ, 8, LANES), BF), scratch)(got, inv, fwd, marks)
        got = exchange(send.reshape(NG * NZ, 8, LANES), ("x", "c", "z"))
        scratch = [((NG * NZ * 8 + 64, LANES), F32), ((2 * POINTS * COLS // LANES + 16, LANES), F32)]
        send = call(next_conv_kernel, ((NY, NC, 16, LANES), BF), scratch)(got, first, *mats)
    tail = got
    send = call(last_corr_kernel, ((NX, NZ, POINTS, LANES), BF))(got, *mats)
    got = exchange(send.reshape(NX * NZ, POINTS, LANES), ("x", "z")).reshape(NX, NZ, POINTS, LANES)
    send = call(last_sum_kernel, ((NA, 8, LANES), BF))(got)
    got = exchange(send, ("v", "w", "c"))
    scratch = [(own, BF), (own, BF), ((POINTS * NI + 8, LANES), F32)]
    run = call(last_kernel, [(own, BF), (own, BF)], scratch, copies=2, far_outs=2)
    focus_plus, focus_minus = run(got, tail, inv, kept, focus_start)
    return (focus_plus, focus_minus)


def solution(mesh):
    fine = Mesh(mesh.devices.reshape(NX, NY // NW, NW, NC, NZ), ("x", "v", "w", "c", "z"))
    receivers = ("z", "x", "v", "w", "c")
    slabs = ("x", "v", "w", "c")
    return jax.shard_map(
        shards,
        mesh=fine,
        in_specs=(
            P(None, receivers, None),
            P(None, receivers),
            P(),
            P(slabs, "z", None),
            P(slabs, "z", None),
        ),
        out_specs=(P(None, receivers, None), P(None, receivers, None)),
        check_vma=False,
    )
```

```python
import math

import jax
import jax.numpy as jnp
import numpy as np
from jax import lax
from jax.experimental import pallas as pl
from jax.experimental.pallas import tpu as pltpu
from jax.sharding import Mesh
from jax.sharding import PartitionSpec as P

FLO = 8
ITERS = 2
NX, NY, NC, NZ = 4, 8, 2, 8
NW = 2
NA, NG, NI = NY * NC, NX * NC, 4
NU = NG * NW
NF, POINTS, NT = 64, 16, 1024
BLOCK, COLS = 256, 2048
LANES = 128
SPANS = ((128, 384), (640, 896), (0, 128), (896, 1024))
CUT = 512
KEPT = 768
TIMES = CUT + 2 * 2 * NG
OWN_TIMES = CUT + 2 * 2 * NU
ONSET_MID = 256
BF, F32, I32 = jnp.bfloat16, jnp.float32, jnp.int32
VMEM_LIMIT = 8 * 1024 * 1024


def base_tables():
    phase = (np.arange(NT)[None, :] * (FLO + np.arange(NF))[:, None]) % NT
    angle = phase.astype(np.float32) * np.float32(2.0 * math.pi / NT)
    rows = np.concatenate([np.cos(angle), -np.sin(angle)], axis=0)
    forward = (rows * np.float32(1.0 / math.sqrt(NT))).astype(BF)
    inverse = (rows * np.float32(math.sqrt(2.0 / NF))).astype(BF)
    inverse = np.concatenate([inverse[:, a:b] for a, b in SPANS], axis=1)
    wide = np.concatenate([forward[:NF], forward[NF:]], axis=1)
    return forward, wide, np.ascontiguousarray(inverse.T)


def iota(shape, dim):
    return lax.broadcasted_iota(I32, shape, dim)


def grid(rows, cols):
    return iota((rows, cols), 0), iota((rows, cols), 1)


def hot(mask):
    return jnp.where(mask, jnp.float32(1), jnp.float32(0)).astype(BF)


def nn(a, b):
    return lax.dot_general(a, b, (((1,), (0,)), ((), ())), preferred_element_type=F32)


def nt(a, b):
    return lax.dot_general(a, b, (((1,), (1,)), ((), ())), preferred_element_type=F32)


def two_terms(value):
    high = value.astype(BF)
    return high, (value - high.astype(F32)).astype(BF)


def slab_of_bin(bins):
    row, _ = grid(NF, NF)
    return hot(row == bins)


def fetch(pairs, sems):
    copies = [pltpu.make_async_copy(src, dst, sems.at[n]) for n, (src, dst) in enumerate(pairs)]
    for copy in copies:
        copy.start()
    return copies


def start_kernel(bins_in, onset_in, focus_in, base_in, out, bins, onset, focus, base, flat, sems):
    copies = fetch([(bins_in, bins), (onset_in, onset), (focus_in, focus), (base_in, base)], sems)
    copies[0].wait()
    m, j = grid(8 * NA, NF)
    place = hot(((m & 7) < NX) & (j == ((m & 7) << 4) + (m >> 3)))
    order = nt(place, slab_of_bin(bins[...])).astype(BF)
    copies[1].wait()
    p, lane = grid(POINTS, LANES)
    spread = hot((((lane >> 2) & 15) == p) & ((lane >> 6) == (p >> 3)))
    marks = nn((onset[...] - ONSET_MID).astype(F32).astype(BF), spread)
    i, lane = grid(NI, LANES)
    marks = jnp.where((lane & 3) == i, marks, 0.0).sum(axis=0, keepdims=True)
    copies[2].wait()
    for p in range(POINTS):
        flat[NI * p : NI * (p + 1), :] = focus[p].astype(F32)
    rows = flat[: POINTS * NI, :].astype(BF)
    none = jnp.zeros_like(rows)
    copies[3].wait()
    spec = nt(base[:, :NT], jnp.concatenate([rows, none], axis=0))
    spec = spec + nt(base[:, NT:], jnp.concatenate([none, rows], axis=0))
    sent = nn(order, spec.astype(BF))
    sent = jnp.where((iota((8 * NA, LANES), 0) & 7) == NX, marks, sent)
    out[...] = sent.reshape(NA, 8, LANES).astype(BF)


def tables_kernel(
    where, bins_in, onset_in, forward_in, inverse_in, re_in, im_in,
    place, inv, own_inv, fwd, own_fwd, own_marks, re, im,
    bins, onset, forward, inverse, sems,
):
    pairs = [(bins_in, bins), (onset_in, onset), (forward_in, forward), (inverse_in, inverse), (re_in, re), (im_in, im)]
    copies = fetch(pairs, sems)
    for copy in copies[:4]:
        copy.wait()
    row, _ = grid(8, LANES)
    value = jnp.zeros((8, LANES), I32)
    for n in range(4):
        value = jnp.where(row == n, where[n], value)
    place[...] = value
    held = bins[...].astype(F32).astype(BF)
    j, k = grid(NF, LANES)
    arrival = ((k >> 5) << 4) + (k & 15)
    at_k = nn(held, hot(j == arrival))
    j, n = grid(NF, 2 * NA)
    at_own = nn(held, hot(j == (where[0] << 4) + (n & 15)))
    row, k = grid(LANES, LANES)
    order = hot(((row >> 6) == ((k >> 4) & 1)) & ((row & 63).astype(F32) == at_k))
    row, n = grid(LANES, 2 * NA)
    own_order = hot(((row >> 6) == (n >> 4)) & ((row & 63).astype(F32) == at_own))
    base = inverse[...]
    table = nn(base, order).astype(BF)
    own_table = nn(base, own_order).astype(BF)
    holds = slab_of_bin(bins[...])
    m, j = grid(2 * NG, NF)
    slabs = hot(j == (((m & 7) >> 1) << 4) + (where[1] << 1) + (m & 1))
    m, j = grid(2 * NU, NF)
    own_slabs = hot(j == (((m & 15) >> 2) << 4) + ((where[1] >> 1) << 2) + ((m & 1) << 1) + ((m >> 1) & 1))
    inv[TIMES:] = table[CUT:]
    for to_inv, to_fwd, part, rows in ((inv, fwd, table, slabs), (own_inv, own_fwd, own_table, own_slabs)):
        count = rows.shape[0] // 2
        rows = nt(rows, holds)
        first = iota(rows.shape, 0) < count
        pick = jnp.concatenate([jnp.where(first, rows, 0.0), jnp.where(first, 0.0, rows)], axis=1).astype(BF)
        for n, (a, b) in enumerate(SPANS[:2]):
            to_fwd[:, BLOCK * n : BLOCK * (n + 1)] = nn(pick, forward[:, a:b]).astype(BF)
        picked = jnp.concatenate([nn(pick, forward[:, a:b]).astype(BF) for a, b in SPANS[2:]], axis=1)
        to_inv[:CUT] = part[:CUT]
        to_inv[CUT : CUT + 4 * count] = jnp.concatenate(two_terms(nn(picked, part[CUT:])), axis=0)
    m, p = grid(POINTS * NI, POINTS)
    marks = nt(hot((m >> 2) == p), (onset[...] - ONSET_MID).astype(F32).astype(BF))
    m, i = grid(POINTS * NI, NI)
    marks = jnp.where((m & 3) == i, marks, 0.0).sum(axis=1, keepdims=True)
    own_marks[...] = jnp.broadcast_to(marks, (POINTS * NI, LANES)).astype(I32) + ONSET_MID
    for copy in copies[4:]:
        copy.wait()


def middle_kernel(got, _, out, rows):
    rows[: 8 * NA, :] = got[...].astype(F32).reshape(8 * NA, LANES)
    line = jnp.concatenate([rows[pl.ds(e, NA, stride=8), :] for e in range(NX + 1)], axis=1).astype(BF)
    m, a = grid(NA * NI, NA)
    spread = nn(hot((m >> 2) == a), line)
    m, lane = grid(NA * NI, LANES)
    stacked = []
    for e in range(NX + 1):
        piece = spread[:, LANES * e : LANES * (e + 1)]
        for part in range(2):
            fits = ((lane & 3) == (m & 3)) & ((lane >> 6) == part)
            stacked.append(jnp.where(fits, piece, 0.0))
    stacked = jnp.concatenate(stacked, axis=0).astype(BF)
    p, lane = grid(POINTS, LANES)
    turned = nt(hot(((lane >> 2) & 15) == p), stacked)
    marks = turned[:8, LANES * NX :] + turned[8:, LANES * NX :]
    for x in range(NX):
        message = jnp.concatenate([turned[:, LANES * x : LANES * (x + 1)], marks], axis=0).astype(BF)
        for z in range(NZ):
            out[x, z] = message


def swap(a, b):
    low = iota(a.shape, 1) < LANES // 2
    return (
        jnp.where(low, a, pltpu.roll(b, LANES // 2, 1)),
        jnp.where(low, pltpu.roll(a, LANES // 2, 1), b),
    )


def convolve(src, mat_re, mat_im, out):
    a = nt(src, mat_re[...])
    b = nt(src, mat_im[...])
    parts = (a[:POINTS] - b[POINTS:], a[POINTS:] + b[:POINTS])
    for c in range(NC):
        at = slice(8 * c, 8 * (c + 1))
        for w in range(NW):
            slabs = [part[at, LANES * w : LANES * (w + 1)] for part in parts]
            message = jnp.concatenate(slabs, axis=0).astype(BF)
            for v in range(NY // NW):
                out[NW * v + w, c] = message


def first_conv_kernel(place, got, mat_re, mat_im, out, src, own_marks, marks, rows):
    height = POINTS + 8
    rows[...] = got[...].astype(F32).reshape(NX * NZ * height, LANES)
    for z in range(NZ):
        for half in range(2):
            a = rows[pl.ds((2 * half * NZ + z) * height, POINTS), :]
            b = rows[pl.ds(((2 * half + 1) * NZ + z) * height, POINTS), :]
            at = LANES * (2 * z + half)
            re, im = swap(a, b)
            src[:POINTS, at : at + LANES] = re.astype(BF)
            src[POINTS:, at : at + LANES] = im.astype(BF)
    x, y, c, z = (place[n : n + 1, :] for n in range(4))
    mine = (y & 1) + 2 * c
    own = jnp.zeros((8, LANES), F32)
    line, _ = grid(8, LANES)
    few = jnp.zeros((8, LANES), F32)
    p, _ = grid(POINTS, LANES)
    for half in range(2):
        a = b = jnp.zeros((8, LANES), F32)
        for n in range(NZ):
            at = (2 * half * NZ + n) * height + POINTS
            a = jnp.where(z == n, rows[at : at + 8, :], a)
            b = jnp.where(z == n, rows[at + NZ * height : at + NZ * height + 8, :], b)
        blocks = swap(a, b)
        for h in range(2):
            own = jnp.where(mine == half + 2 * h, blocks[h], own)
        blocks = jnp.concatenate(blocks, axis=0)
        for n in range(2):
            row = jnp.where(p == 4 * x + 2 * c + n, blocks, 0.0).sum(axis=0, keepdims=True)
            few = jnp.where(line == 2 * n + half, row, few)
    marks[...] = few.astype(I32) + ONSET_MID
    own_marks[...] = own.astype(I32) + ONSET_MID
    convolve(src[...], mat_re, mat_im, out)


def next_conv_kernel(got, first, mat_re, mat_im, out, rows, more):
    rows[: NG * NZ * 8, :] = got[...].astype(F32).reshape(NG * NZ * 8, LANES)
    for z in range(NZ):
        for p in range(2):
            for part in range(2):
                for half in range(2):
                    slab = rows[pl.ds(8 * z + 4 * p + 2 * part + half, NG, stride=8 * NZ), :]
                    more[pl.ds(2 * POINTS * (2 * z + half) + POINTS * part + p, NG, stride=2), :] = slab
    blocks = [more[2 * POINTS * n : 2 * POINTS * (n + 1), :] for n in range(COLS // LANES)]
    src = (first[...].astype(F32) + jnp.concatenate(blocks, axis=1)).astype(BF)
    convolve(src, mat_re, mat_im, out)


def window(spectra, marks, inv, fwd):
    t = iota((BLOCK, 1), 0)
    count = fwd.shape[0]
    front = jnp.where(t + SPANS[0][0] < marks, nn(inv[:BLOCK], spectra), 0.0).astype(BF)
    rest = nn(inv[BLOCK : CUT + 2 * count], spectra)
    back = jnp.where(t + SPANS[1][0] >= NT - marks, rest[:BLOCK], 0.0).astype(BF)
    fixed = rest[BLOCK : BLOCK + count] + rest[BLOCK + count :]
    return nn(fwd[:, :BLOCK], front) + nn(fwd[:, BLOCK:], back) + fixed


def window_slabs(got, inv, fwd, marks, rows, turn):
    rows[: NA * 16, :] = got[...].astype(F32).reshape(NA * 16, LANES)
    every = []
    for p in range(8):
        parts = [rows[pl.ds(8 * part + p, NA, stride=16), :] for part in range(2)]
        every.append(jnp.concatenate(parts, axis=0).astype(BF))
    mark = [marks[p : p + 1, :] for p in range(8)]
    spec = window(jnp.concatenate(every, axis=1), jnp.concatenate(mark, axis=1), inv, fwd)
    for p in range(8):
        for part in range(2):
            slab = spec[NU * part : NU * (part + 1), LANES * p : LANES * (p + 1)]
            turn[pl.ds(8 * part + p, NU, stride=16), :] = slab
    return every, turn[: NU * 16, :].reshape(NU, 16, LANES)


def time_kernel(got, inv, fwd, marks, out, rows, turn):
    out[...] = window_slabs(got, inv, fwd, marks, rows, turn)[1].astype(BF)


def last_time_kernel(got, inv, fwd, marks, place, out, rows, turn, tail):
    every, message = window_slabs(got, inv, fwd, marks, rows, turn)
    m, r = grid(NU * NI, LANES)
    y = place[1:2, :]
    w = y & 1
    y = (y & 6) + ((m >> 2) & 1)
    own = ((m >> 4) << 6) + (y << 3) + (((m >> 3) & 1) << 2) + (m & 3)
    own = hot(r + LANES * w == own)
    for h in range(2):
        taken = nt(own, jnp.concatenate(every[4 * h : 4 * (h + 1)], axis=0))
        for u in range(NU):
            tail[8 * u + NI * h : 8 * u + NI * (h + 1), :] = taken[NI * u : NI * (u + 1)]
    out[...] = jnp.concatenate([message, tail[: NU * 8, :].reshape(NU, 8, LANES)], axis=1).astype(BF)


def time_copies_kernel(got, inv, fwd, marks, out, rows, turn):
    rows[: NF * 8, :] = got[...].astype(F32).reshape(NF * 8, LANES)
    every = []
    for p in range(2):
        parts = []
        for x in range(NX):
            for part in range(2):
                at = [8 * x + 4 * p + 2 * part + half for half in range(2)]
                halves = [rows[pl.ds(n, NA, stride=8 * NX), :] for n in at]
                parts.append(jnp.concatenate(halves, axis=1))
        every.append(jnp.concatenate(parts, axis=0).astype(BF))
    mark = [marks[n : n + 1, :] for n in range(4)]
    spectra = window(jnp.concatenate(every, axis=1), jnp.concatenate(mark, axis=1), inv, fwd)
    for p in range(2):
        spec = spectra[:, BLOCK * p : BLOCK * (p + 1)]
        for part in range(2):
            for half in range(2):
                slab = spec[NG * part : NG * (part + 1), LANES * half : LANES * (half + 1)]
                turn[pl.ds(4 * p + 2 * part + half, NG, stride=8), :] = slab
    message = turn[: NG * 8, :].reshape(NG, 8, LANES).astype(BF)
    for z in range(NZ):
        out[:, z] = message


def correlate(got, mat_re, mat_im):
    parts = []
    for part in range(2):
        halves = []
        for half in range(2):
            at = 8 * part
            both = [sum(got[4 * x + 2 * c + half].astype(F32)[at : at + 8] for x in range(NX)) for c in range(NC)]
            halves.append(jnp.concatenate(both, axis=0))
        parts.append(jnp.concatenate(halves, axis=1))
    straight = jnp.concatenate(parts, axis=0).astype(BF)
    turned = jnp.concatenate([parts[1], -parts[0]], axis=0).astype(BF)
    for z in range(NZ):
        at = slice(BLOCK * z, BLOCK * (z + 1))
        yield z, nn(straight, mat_re[:, at]) + nn(turned, mat_im[:, at])


def corr_kernel(got, mat_re, mat_im, out, turn):
    for z, block in correlate(got, mat_re, mat_im):
        for x in range(NX):
            for part in range(2):
                for half in range(2):
                    at = (x * NZ + z) * 16 + 2 * part + half
                    row = POINTS * part + 4 * x
                    turn[pl.ds(at, 4, stride=4), :] = block[row : row + 4, LANES * half : LANES * (half + 1)]
    out[...] = turn[: NX * NZ * 16, :].reshape(NX * NZ, 16, LANES).astype(BF)


def last_corr_kernel(got, mat_re, mat_im, out):
    for z, block in correlate(got, mat_re, mat_im):
        for half in range(2):
            at = slice(LANES * half, LANES * (half + 1))
            a, b = swap(block[:POINTS, at], block[POINTS:, at])
            out[2 * half, z] = a.astype(BF)
            out[2 * half + 1, z] = b.astype(BF)


def sum_kernel(got, out):
    total = got[...].astype(F32).reshape(NX, NZ, 16, LANES).sum(axis=1)
    for c in range(NC):
        message = total[:, 8 * c : 8 * (c + 1)].reshape(NX * 8, LANES).astype(BF)
        for y in range(NY):
            out[y, c] = message


def last_sum_kernel(got, out):
    total = got[...].astype(F32).sum(axis=1).astype(BF)
    total = jnp.concatenate([total[x] for x in range(NX)], axis=1)
    m, p = grid(LANES, POINTS)
    turned = nn(hot(((m >> 2) & 15) == p), total)
    m, n = grid(LANES, NX * LANES)
    turned = jnp.where(((n & 3) == (m & 3)) & (((n >> 6) & 1) == (m >> 6)), turned, 0.0).astype(BF)
    sent = nt(hot(((m & 7) == (n >> 7)) & ((m >> 3) == ((n >> 2) & 15))), turned)
    out[...] = sent.reshape(NA, 8, LANES).astype(BF)


def keep_own(spectra, inv, marks):
    t = iota((POINTS * NI, LANES), 1)
    trace = [nt(spectra, inv[a:b]) for a, b in ((0, CUT), (TIMES, TIMES + KEPT - CUT))]
    trace = jnp.concatenate(trace, axis=1)
    pieces = [trace[:, LANES * n : LANES * (n + 1)] for n in range(KEPT // LANES)]
    none = jnp.zeros_like(pieces[0])
    front = [jnp.where(t + SPANS[0][0] + LANES * n < marks, pieces[n], 0.0) for n in range(2)]
    back = [jnp.where(t + SPANS[1][0] + LANES * n >= NT - marks, pieces[2 + n], 0.0) for n in range(2)]
    return jnp.concatenate([pieces[4], *front, none, none, *back, pieces[5]], axis=1)


def last_kernel(got, tail, inv, marks, focus, plus_out, minus_out, plus, minus, spectra, sems):
    rows = got[...].astype(F32).reshape(8 * NA, LANES).T.astype(BF)
    m, k = grid(8 * NA, LANES)
    own = jnp.zeros((POINTS * NI, LANES), F32)
    for part in range(2):
        place = hot(((m & 7) < NX) & (k == ((m & 7) << 5) + 16 * part + (m >> 3)))
        own = own + nn(rows[NF * part : NF * (part + 1)], place)
    trace = keep_own(own.astype(BF), inv[...], marks[...])
    for p in range(POINTS):
        plus[p] = (focus[p].astype(F32) + trace[NI * p : NI * (p + 1)]).astype(BF)
    first = pltpu.make_async_copy(plus, plus_out, sems.at[0])
    first.start()
    own = []
    for x in range(NX):
        both = [sum(tail[4 * x + 2 * c + w].astype(F32)[16:] for w in range(NW)) for c in range(NC)]
        own.append(jnp.concatenate(both, axis=0))
    own = jnp.concatenate(own, axis=1).astype(BF)
    n, k = grid(NX * LANES, LANES)
    same = (n >> 7) * 32 + (n & 31) == k
    own = [nn(own, hot(same & (((n >> 5) & 3) == p))) for p in range(4)]
    for p in range(POINTS):
        spectra[NI * p : NI * (p + 1), :] = own[p & 3][NI * (p >> 2) : NI * ((p >> 2) + 1)]
    trace = keep_own(spectra[: POINTS * NI, :].astype(BF), inv[...], marks[...])
    for p in range(POINTS):
        minus[p] = trace[NI * p : NI * (p + 1)].astype(BF)
    second = pltpu.make_async_copy(minus, minus_out, sems.at[1])
    second.start()
    first.wait()
    second.wait()


def call(kernel, outs, scratch=(), scalars=0, far=0, copies=0, far_outs=0):
    single = not isinstance(outs, list)
    shapes = [jax.ShapeDtypeStruct(shape, dtype) for shape, dtype in ([outs] if single else outs)]

    def run(*args):
        out_spaces = [pltpu.VMEM] * (len(shapes) - far_outs) + [pltpu.HBM] * far_outs
        spaces = [pltpu.SMEM] * scalars + [pltpu.HBM] * far + [pltpu.VMEM] * (len(args) - scalars - far)
        args = [
            pltpu.with_memory_space_constraint(arg, pltpu.HBM) if space is pltpu.HBM else arg
            for arg, space in zip(args, spaces)
        ]
        got = pl.pallas_call(
            kernel,
            out_shape=shapes,
            in_specs=[pl.BlockSpec(memory_space=space) for space in spaces],
            out_specs=[pl.BlockSpec(memory_space=space) for space in out_spaces],
            scratch_shapes=[pltpu.VMEM(shape, dtype) for shape, dtype in scratch]
            + [pltpu.SemaphoreType.DMA((copies,))] * (copies > 0),
            compiler_params=pltpu.CompilerParams(vmem_limit_bytes=VMEM_LIMIT),
        )(*args)
        return got[0] if single else got

    return run


def exchange(values, axes):
    return lax.all_to_all(values, axes, 0, 0, tiled=True)


def shards(focus_start, onset, bins, refl_real, refl_imag):
    mats = (refl_real[0], refl_imag[0])
    where = jnp.stack([lax.axis_index(axis) for axis in ("x", ("v", "w"), "c", "z")]).astype(I32)
    bins = bins.reshape(1, NF)
    onset = onset.T
    forward, wide, inverse = base_tables()
    own = (POINTS, NI, NT)

    scratch = [((1, NF), I32), ((NI, POINTS), I32), (own, BF), ((NF, 2 * NT), BF), ((POINTS * NI + 8, NT), F32)]
    run = call(start_kernel, ((NA, 8, LANES), BF), scratch, far=4, copies=4)
    got = exchange(run(bins, onset, focus_start, wide), ("v", "w", "c"))
    outs = [((8, LANES), I32), ((TIMES + KEPT - CUT, LANES), BF), ((OWN_TIMES, 2 * NA), BF), ((2 * NG, CUT), BF), ((2 * NU, CUT), BF)]
    outs += [((POINTS * NI, LANES), I32), ((BLOCK, COLS), BF), ((BLOCK, COLS), BF)]
    scratch = [((1, NF), I32), ((NI, POINTS), I32), ((2 * NF, NT), BF), ((KEPT, LANES), BF)]
    run = call(tables_kernel, outs, scratch, scalars=1, far=6, copies=6)
    place, inv, own_inv, fwd, own_fwd, kept, *mats = run(where, bins, onset, forward, inverse, *mats)
    send = call(middle_kernel, ((NX, NZ, POINTS + 8, LANES), BF), [((8 * NA + 8, LANES), F32)])(got, fwd)
    got = exchange(send.reshape(NX * NZ, POINTS + 8, LANES), ("x", "z"))
    outs = [((NY, NC, 16, LANES), BF), ((2 * POINTS, COLS), BF), ((8, LANES), I32), ((8, LANES), I32)]
    scratch = [((NX * NZ * (POINTS + 8), LANES), F32)]
    send, first, own_marks, marks = call(first_conv_kernel, outs, scratch)(place, got, *mats)
    for step in range(ITERS):
        got = exchange(send.reshape(NA, 16, LANES), ("v", "w", "c"))
        scratch = [((NA * 16 + 16, LANES), F32), ((NU * 16 + 16, LANES), F32)]
        tables = (own_inv, own_fwd, own_marks)
        if step == ITERS - 1:
            scratch = scratch + [((NU * 8 + 8, LANES), F32)]
            send = call(last_time_kernel, ((NU, 24, LANES), BF), scratch)(got, *tables, place)
            got = exchange(send, ("x", "c", "w"))
            break
        send = call(time_kernel, ((NU, 16, LANES), BF), scratch)(got, *tables)
        got = exchange(send, ("x", "c", "w"))
        send = call(corr_kernel, ((NX * NZ, 16, LANES), BF), [((NX * NZ * 16 + 32, LANES), F32)])(got, *mats)
        got = exchange(send, ("x", "z"))
        send = call(sum_kernel, ((NY, NC, NX * 8, LANES), BF))(got)
        got = exchange(send.reshape(NA, NX * 8, LANES), ("v", "w", "c"))
        scratch = [((NF * 8 + 32, LANES), F32), ((NG * 8 + 8, LANES), F32)]
        send = call(time_copies_kernel, ((NG, NZ, 8, LANES), BF), scratch)(got, inv, fwd, marks)
        got = exchange(send.reshape(NG * NZ, 8, LANES), ("x", "c", "z"))
        scratch = [((NG * NZ * 8 + 64, LANES), F32), ((2 * POINTS * COLS // LANES + 16, LANES), F32)]
        send = call(next_conv_kernel, ((NY, NC, 16, LANES), BF), scratch)(got, first, *mats)
    tail = got
    send = call(last_corr_kernel, ((NX, NZ, POINTS, LANES), BF))(got, *mats)
    got = exchange(send.reshape(NX * NZ, POINTS, LANES), ("x", "z")).reshape(NX, NZ, POINTS, LANES)
    send = call(last_sum_kernel, ((NA, 8, LANES), BF))(got)
    got = exchange(send, ("v", "w", "c"))
    scratch = [(own, BF), (own, BF), ((POINTS * NI + 8, LANES), F32)]
    run = call(last_kernel, [(own, BF), (own, BF)], scratch, copies=2, far_outs=2)
    focus_plus, focus_minus = run(got, tail, inv, kept, focus_start)
    return (focus_plus, focus_minus)


def solution(mesh):
    fine = Mesh(mesh.devices.reshape(NX, NY // NW, NW, NC, NZ), ("x", "v", "w", "c", "z"))
    receivers = ("z", "x", "v", "w", "c")
    slabs = ("x", "v", "w", "c")
    return jax.shard_map(
        shards,
        mesh=fine,
        in_specs=(
            P(None, receivers, None),
            P(None, receivers),
            P(),
            P(slabs, "z", None),
            P(slabs, "z", None),
        ),
        out_specs=(P(None, receivers, None), P(None, receivers, None)),
        check_vma=False,
    )
```

```python
import math

import jax
import jax.numpy as jnp
import numpy as np
from jax import lax
from jax.experimental import pallas as pl
from jax.experimental.pallas import tpu as pltpu
from jax.sharding import Mesh
from jax.sharding import PartitionSpec as P

FLO = 8
ITERS = 2
NX, NY, NC, NZ = 4, 8, 2, 8
NW = 2
NA, NG, NI = NY * NC, NX * NC, 4
NU = NG * NW
NF, POINTS, NT = 64, 16, 1024
BLOCK, COLS = 256, 2048
LANES = 128
SPANS = ((128, 384), (640, 896), (0, 128), (896, 1024))
CUT = 512
KEPT = 768
TIMES = CUT + 2 * 2 * NG
OWN_TIMES = CUT + 2 * 2 * NU
ONSET_MID = 256
BF, F32, I32 = jnp.bfloat16, jnp.float32, jnp.int32
VMEM_LIMIT = 8 * 1024 * 1024


def base_tables():
    phase = (np.arange(NT)[None, :] * (FLO + np.arange(NF))[:, None]) % NT
    angle = phase.astype(np.float32) * np.float32(2.0 * math.pi / NT)
    rows = np.concatenate([np.cos(angle), -np.sin(angle)], axis=0)
    forward = (rows * np.float32(1.0 / math.sqrt(NT))).astype(BF)
    inverse = (rows * np.float32(math.sqrt(2.0 / NF))).astype(BF)
    inverse = np.concatenate([inverse[:, a:b] for a, b in SPANS], axis=1)
    wide = np.concatenate([forward[:NF], forward[NF:]], axis=1)
    return forward, wide, np.ascontiguousarray(inverse.T)


def iota(shape, dim):
    return lax.broadcasted_iota(I32, shape, dim)


def grid(rows, cols):
    return iota((rows, cols), 0), iota((rows, cols), 1)


def hot(mask):
    return jnp.where(mask, jnp.float32(1), jnp.float32(0)).astype(BF)


def nn(a, b):
    return lax.dot_general(a, b, (((1,), (0,)), ((), ())), preferred_element_type=F32)


def nt(a, b):
    return lax.dot_general(a, b, (((1,), (1,)), ((), ())), preferred_element_type=F32)


def two_terms(value):
    high = value.astype(BF)
    return high, (value - high.astype(F32)).astype(BF)


def slab_of_bin(bins):
    row, _ = grid(NF, NF)
    return hot(row == bins)


def fetch(pairs, sems):
    copies = [pltpu.make_async_copy(src, dst, sems.at[n]) for n, (src, dst) in enumerate(pairs)]
    for copy in copies:
        copy.start()
    return copies


def start_kernel(bins_in, onset_in, focus_in, base_in, out, bins, onset, focus, base, flat, sems):
    copies = fetch([(bins_in, bins), (onset_in, onset), (focus_in, focus), (base_in, base)], sems)
    copies[0].wait()
    m, j = grid(8 * NA, NF)
    place = hot(((m & 7) < NX) & (j == ((m & 7) << 4) + (m >> 3)))
    order = nt(place, slab_of_bin(bins[...])).astype(BF)
    copies[1].wait()
    p, lane = grid(POINTS, LANES)
    spread = hot((((lane >> 2) & 15) == p) & ((lane >> 6) == (p >> 3)))
    marks = nn((onset[...] - ONSET_MID).astype(F32).astype(BF), spread)
    i, lane = grid(NI, LANES)
    marks = jnp.where((lane & 3) == i, marks, 0.0).sum(axis=0, keepdims=True)
    copies[2].wait()
    for p in range(POINTS):
        flat[NI * p : NI * (p + 1), :] = focus[p].astype(F32)
    rows = flat[: POINTS * NI, :].astype(BF)
    none = jnp.zeros_like(rows)
    copies[3].wait()
    spec = nt(base[:, :NT], jnp.concatenate([rows, none], axis=0))
    spec = spec + nt(base[:, NT:], jnp.concatenate([none, rows], axis=0))
    sent = nn(order, spec.astype(BF))
    sent = jnp.where((iota((8 * NA, LANES), 0) & 7) == NX, marks, sent)
    out[...] = sent.reshape(NA, 8, LANES).astype(BF)


def tables_kernel(
    where, bins_in, onset_in, forward_in, inverse_in, re_in, im_in,
    place, inv, own_inv, fwd, own_fwd, own_marks, re, im,
    bins, onset, forward, inverse, sems,
):
    pairs = [(bins_in, bins), (onset_in, onset), (forward_in, forward), (inverse_in, inverse), (re_in, re), (im_in, im)]
    copies = fetch(pairs, sems)
    for copy in copies[:4]:
        copy.wait()
    row, _ = grid(8, LANES)
    value = jnp.zeros((8, LANES), I32)
    for n in range(4):
        value = jnp.where(row == n, where[n], value)
    place[...] = value
    held = bins[...].astype(F32).astype(BF)
    j, k = grid(NF, LANES)
    arrival = ((k >> 5) << 4) + (k & 15)
    at_k = nn(held, hot(j == arrival))
    j, n = grid(NF, 2 * NA)
    at_own = nn(held, hot(j == (where[0] << 4) + (n & 15)))
    row, k = grid(LANES, LANES)
    order = hot(((row >> 6) == ((k >> 4) & 1)) & ((row & 63).astype(F32) == at_k))
    row, n = grid(LANES, 2 * NA)
    own_order = hot(((row >> 6) == (n >> 4)) & ((row & 63).astype(F32) == at_own))
    base = inverse[...]
    table = nn(base, order).astype(BF)
    own_table = nn(base, own_order).astype(BF)
    holds = slab_of_bin(bins[...])
    m, j = grid(2 * NG, NF)
    slabs = hot(j == (((m & 7) >> 1) << 4) + (where[1] << 1) + (m & 1))
    m, j = grid(2 * NU, NF)
    own_slabs = hot(j == (((m & 15) >> 2) << 4) + ((where[1] >> 1) << 2) + ((m & 1) << 1) + ((m >> 1) & 1))
    inv[TIMES:] = table[CUT:]
    for to_inv, to_fwd, part, rows in ((inv, fwd, table, slabs), (own_inv, own_fwd, own_table, own_slabs)):
        count = rows.shape[0] // 2
        rows = nt(rows, holds)
        first = iota(rows.shape, 0) < count
        pick = jnp.concatenate([jnp.where(first, rows, 0.0), jnp.where(first, 0.0, rows)], axis=1).astype(BF)
        for n, (a, b) in enumerate(SPANS[:2]):
            to_fwd[:, BLOCK * n : BLOCK * (n + 1)] = nn(pick, forward[:, a:b]).astype(BF)
        picked = jnp.concatenate([nn(pick, forward[:, a:b]).astype(BF) for a, b in SPANS[2:]], axis=1)
        to_inv[:CUT] = part[:CUT]
        to_inv[CUT : CUT + 4 * count] = jnp.concatenate(two_terms(nn(picked, part[CUT:])), axis=0)
    m, p = grid(POINTS * NI, POINTS)
    marks = nt(hot((m >> 2) == p), (onset[...] - ONSET_MID).astype(F32).astype(BF))
    m, i = grid(POINTS * NI, NI)
    marks = jnp.where((m & 3) == i, marks, 0.0).sum(axis=1, keepdims=True)
    own_marks[...] = jnp.broadcast_to(marks, (POINTS * NI, LANES)).astype(I32) + ONSET_MID
    for copy in copies[4:]:
        copy.wait()


def middle_kernel(got, _, out, rows):
    rows[: 8 * NA, :] = got[...].astype(F32).reshape(8 * NA, LANES)
    line = jnp.concatenate([rows[pl.ds(e, NA, stride=8), :] for e in range(NX + 1)], axis=1).astype(BF)
    m, a = grid(NA * NI, NA)
    spread = nn(hot((m >> 2) == a), line)
    m, lane = grid(NA * NI, LANES)
    stacked = []
    for e in range(NX + 1):
        piece = spread[:, LANES * e : LANES * (e + 1)]
        for part in range(2):
            fits = ((lane & 3) == (m & 3)) & ((lane >> 6) == part)
            stacked.append(jnp.where(fits, piece, 0.0))
    stacked = jnp.concatenate(stacked, axis=0).astype(BF)
    p, lane = grid(POINTS, LANES)
    turned = nt(hot(((lane >> 2) & 15) == p), stacked)
    marks = turned[:8, LANES * NX :] + turned[8:, LANES * NX :]
    for x in range(NX):
        message = jnp.concatenate([turned[:, LANES * x : LANES * (x + 1)], marks], axis=0).astype(BF)
        for z in range(NZ):
            out[x, z] = message


def swap(a, b):
    low = iota(a.shape, 1) < LANES // 2
    return (
        jnp.where(low, a, pltpu.roll(b, LANES // 2, 1)),
        jnp.where(low, pltpu.roll(a, LANES // 2, 1), b),
    )


def convolve(src, mat_re, mat_im, out):
    a = nt(src, mat_re[...])
    b = nt(src, mat_im[...])
    parts = (a[:POINTS] - b[POINTS:], a[POINTS:] + b[:POINTS])
    for c in range(NC):
        at = slice(8 * c, 8 * (c + 1))
        for w in range(NW):
            slabs = [part[at, LANES * w : LANES * (w + 1)] for part in parts]
            message = jnp.concatenate(slabs, axis=0).astype(BF)
            for v in range(NY // NW):
                out[NW * v + w, c] = message


def first_conv_kernel(place, got, mat_re, mat_im, out, src, own_marks, marks, rows):
    height = POINTS + 8
    rows[...] = got[...].astype(F32).reshape(NX * NZ * height, LANES)
    for z in range(NZ):
        for half in range(2):
            a = rows[pl.ds((2 * half * NZ + z) * height, POINTS), :]
            b = rows[pl.ds(((2 * half + 1) * NZ + z) * height, POINTS), :]
            at = LANES * (2 * z + half)
            re, im = swap(a, b)
            src[:POINTS, at : at + LANES] = re.astype(BF)
            src[POINTS:, at : at + LANES] = im.astype(BF)
    x, y, c, z = (place[n : n + 1, :] for n in range(4))
    mine = (y & 1) + 2 * c
    own = jnp.zeros((8, LANES), F32)
    line, _ = grid(8, LANES)
    few = jnp.zeros((8, LANES), F32)
    p, _ = grid(POINTS, LANES)
    for half in range(2):
        a = b = jnp.zeros((8, LANES), F32)
        for n in range(NZ):
            at = (2 * half * NZ + n) * height + POINTS
            a = jnp.where(z == n, rows[at : at + 8, :], a)
            b = jnp.where(z == n, rows[at + NZ * height : at + NZ * height + 8, :], b)
        blocks = swap(a, b)
        for h in range(2):
            own = jnp.where(mine == half + 2 * h, blocks[h], own)
        blocks = jnp.concatenate(blocks, axis=0)
        for n in range(2):
            row = jnp.where(p == 4 * x + 2 * c + n, blocks, 0.0).sum(axis=0, keepdims=True)
            few = jnp.where(line == 2 * n + half, row, few)
    marks[...] = few.astype(I32) + ONSET_MID
    own_marks[...] = own.astype(I32) + ONSET_MID
    convolve(src[...], mat_re, mat_im, out)


def next_conv_kernel(got, first, mat_re, mat_im, out, rows, more):
    rows[: NG * NZ * 8, :] = got[...].astype(F32).reshape(NG * NZ * 8, LANES)
    for z in range(NZ):
        for p in range(2):
            for part in range(2):
                for half in range(2):
                    slab = rows[pl.ds(8 * z + 4 * p + 2 * part + half, NG, stride=8 * NZ), :]
                    more[pl.ds(2 * POINTS * (2 * z + half) + POINTS * part + p, NG, stride=2), :] = slab
    blocks = [more[2 * POINTS * n : 2 * POINTS * (n + 1), :] for n in range(COLS // LANES)]
    src = (first[...].astype(F32) + jnp.concatenate(blocks, axis=1)).astype(BF)
    convolve(src, mat_re, mat_im, out)


def window(spectra, marks, inv, fwd):
    t = iota((BLOCK, 1), 0)
    count = fwd.shape[0]
    front = jnp.where(t + SPANS[0][0] < marks, nn(inv[:BLOCK], spectra), 0.0).astype(BF)
    rest = nn(inv[BLOCK : CUT + 2 * count], spectra)
    back = jnp.where(t + SPANS[1][0] >= NT - marks, rest[:BLOCK], 0.0).astype(BF)
    fixed = rest[BLOCK : BLOCK + count] + rest[BLOCK + count :]
    return nn(fwd[:, :BLOCK], front) + nn(fwd[:, BLOCK:], back) + fixed


def window_slabs(got, inv, fwd, marks, rows, turn):
    rows[: NA * 16, :] = got[...].astype(F32).reshape(NA * 16, LANES)
    every = []
    for p in range(8):
        parts = [rows[pl.ds(8 * part + p, NA, stride=16), :] for part in range(2)]
        every.append(jnp.concatenate(parts, axis=0).astype(BF))
    mark = [marks[p : p + 1, :] for p in range(8)]
    spec = window(jnp.concatenate(every, axis=1), jnp.concatenate(mark, axis=1), inv, fwd)
    for p in range(8):
        for part in range(2):
            slab = spec[NU * part : NU * (part + 1), LANES * p : LANES * (p + 1)]
            turn[pl.ds(8 * part + p, NU, stride=16), :] = slab
    return every, turn[: NU * 16, :].reshape(NU, 16, LANES)


def time_kernel(got, inv, fwd, marks, out, rows, turn):
    out[...] = window_slabs(got, inv, fwd, marks, rows, turn)[1].astype(BF)


def last_time_kernel(got, inv, fwd, marks, place, out, rows, turn, tail):
    every, message = window_slabs(got, inv, fwd, marks, rows, turn)
    m, r = grid(NU * NI, LANES)
    y = place[1:2, :]
    w = y & 1
    y = (y & 6) + ((m >> 2) & 1)
    own = ((m >> 4) << 6) + (y << 3) + (((m >> 3) & 1) << 2) + (m & 3)
    own = hot(r + LANES * w == own)
    for h in range(2):
        taken = nt(own, jnp.concatenate(every[4 * h : 4 * (h + 1)], axis=0))
        for u in range(NU):
            tail[8 * u + NI * h : 8 * u + NI * (h + 1), :] = taken[NI * u : NI * (u + 1)]
    out[...] = jnp.concatenate([message, tail[: NU * 8, :].reshape(NU, 8, LANES)], axis=1).astype(BF)


def time_copies_kernel(got, inv, fwd, marks, out, rows, turn):
    rows[: NF * 8, :] = got[...].astype(F32).reshape(NF * 8, LANES)
    every = []
    for p in range(2):
        parts = []
        for x in range(NX):
            for part in range(2):
                at = [8 * x + 4 * p + 2 * part + half for half in range(2)]
                halves = [rows[pl.ds(n, NA, stride=8 * NX), :] for n in at]
                parts.append(jnp.concatenate(halves, axis=1))
        every.append(jnp.concatenate(parts, axis=0).astype(BF))
    mark = [marks[n : n + 1, :] for n in range(4)]
    spectra = window(jnp.concatenate(every, axis=1), jnp.concatenate(mark, axis=1), inv, fwd)
    for p in range(2):
        spec = spectra[:, BLOCK * p : BLOCK * (p + 1)]
        for part in range(2):
            for half in range(2):
                slab = spec[NG * part : NG * (part + 1), LANES * half : LANES * (half + 1)]
                turn[pl.ds(4 * p + 2 * part + half, NG, stride=8), :] = slab
    message = turn[: NG * 8, :].reshape(NG, 8, LANES).astype(BF)
    for z in range(NZ):
        out[:, z] = message


def correlate(got, mat_re, mat_im):
    parts = []
    for part in range(2):
        halves = []
        for half in range(2):
            at = 8 * part
            both = [sum(got[4 * x + 2 * c + half].astype(F32)[at : at + 8] for x in range(NX)) for c in range(NC)]
            halves.append(jnp.concatenate(both, axis=0))
        parts.append(jnp.concatenate(halves, axis=1))
    straight = jnp.concatenate(parts, axis=0).astype(BF)
    turned = jnp.concatenate([parts[1], -parts[0]], axis=0).astype(BF)
    for z in range(NZ):
        at = slice(BLOCK * z, BLOCK * (z + 1))
        yield z, nn(straight, mat_re[:, at]) + nn(turned, mat_im[:, at])


def corr_kernel(got, mat_re, mat_im, out, turn):
    for z, block in correlate(got, mat_re, mat_im):
        for x in range(NX):
            for part in range(2):
                for half in range(2):
                    at = (x * NZ + z) * 16 + 2 * part + half
                    row = POINTS * part + 4 * x
                    turn[pl.ds(at, 4, stride=4), :] = block[row : row + 4, LANES * half : LANES * (half + 1)]
    out[...] = turn[: NX * NZ * 16, :].reshape(NX * NZ, 16, LANES).astype(BF)


def last_corr_kernel(got, mat_re, mat_im, out):
    for z, block in correlate(got, mat_re, mat_im):
        for half in range(2):
            at = slice(LANES * half, LANES * (half + 1))
            a, b = swap(block[:POINTS, at], block[POINTS:, at])
            out[2 * half, z] = a.astype(BF)
            out[2 * half + 1, z] = b.astype(BF)


def sum_kernel(got, out):
    total = got[...].astype(F32).reshape(NX, NZ, 16, LANES).sum(axis=1)
    for c in range(NC):
        message = total[:, 8 * c : 8 * (c + 1)].reshape(NX * 8, LANES).astype(BF)
        for y in range(NY):
            out[y, c] = message


def last_sum_kernel(got, out):
    total = got[...].astype(F32).sum(axis=1).astype(BF)
    total = jnp.concatenate([total[x] for x in range(NX)], axis=1)
    m, p = grid(LANES, POINTS)
    turned = nn(hot(((m >> 2) & 15) == p), total)
    m, n = grid(LANES, NX * LANES)
    turned = jnp.where(((n & 3) == (m & 3)) & (((n >> 6) & 1) == (m >> 6)), turned, 0.0).astype(BF)
    m, n = grid(NX * NA, NX * LANES)
    sent = nt(hot(((m & 3) == (n >> 7)) & ((m >> 2) == ((n >> 2) & 15))), turned)
    for a in range(NA):
        out[a] = sent[NX * a : NX * (a + 1)].astype(BF)


def keep_own(spectra, inv, marks):
    t = iota((POINTS * NI, LANES), 1)
    trace = [nt(spectra, inv[a:b]) for a, b in ((0, CUT), (TIMES, TIMES + KEPT - CUT))]
    trace = jnp.concatenate(trace, axis=1)
    pieces = [trace[:, LANES * n : LANES * (n + 1)] for n in range(KEPT // LANES)]
    none = jnp.zeros_like(pieces[0])
    front = [jnp.where(t + SPANS[0][0] + LANES * n < marks, pieces[n], 0.0) for n in range(2)]
    back = [jnp.where(t + SPANS[1][0] + LANES * n >= NT - marks, pieces[2 + n], 0.0) for n in range(2)]
    return jnp.concatenate([pieces[4], *front, none, none, *back, pieces[5]], axis=1)


def last_kernel(got, tail, inv, marks, focus, plus_out, minus_out, plus, minus, spectra, arrived, sems):
    for a in range(NA):
        arrived[NX * a : NX * (a + 1), :] = got[a].astype(F32)
    rows = arrived[: NX * NA, :].T.astype(BF)
    m, k = grid(NX * NA, LANES)
    own = jnp.zeros((POINTS * NI, LANES), F32)
    for part in range(2):
        place = hot(k == ((m & 3) << 5) + 16 * part + (m >> 2))
        own = own + nn(rows[NF * part : NF * (part + 1)], place)
    trace = keep_own(own.astype(BF), inv[...], marks[...])
    for p in range(POINTS):
        plus[p] = (focus[p].astype(F32) + trace[NI * p : NI * (p + 1)]).astype(BF)
    first = pltpu.make_async_copy(plus, plus_out, sems.at[0])
    first.start()
    own = []
    for x in range(NX):
        both = [sum(tail[4 * x + 2 * c + w].astype(F32)[16:] for w in range(NW)) for c in range(NC)]
        own.append(jnp.concatenate(both, axis=0))
    own = jnp.concatenate(own, axis=1).astype(BF)
    n, k = grid(NX * LANES, LANES)
    same = (n >> 7) * 32 + (n & 31) == k
    own = [nn(own, hot(same & (((n >> 5) & 3) == p))) for p in range(4)]
    for p in range(POINTS):
        spectra[NI * p : NI * (p + 1), :] = own[p & 3][NI * (p >> 2) : NI * ((p >> 2) + 1)]
    trace = keep_own(spectra[: POINTS * NI, :].astype(BF), inv[...], marks[...])
    for p in range(POINTS):
        minus[p] = trace[NI * p : NI * (p + 1)].astype(BF)
    second = pltpu.make_async_copy(minus, minus_out, sems.at[1])
    second.start()
    first.wait()
    second.wait()


def call(kernel, outs, scratch=(), scalars=0, far=0, copies=0, far_outs=0):
    single = not isinstance(outs, list)
    shapes = [jax.ShapeDtypeStruct(shape, dtype) for shape, dtype in ([outs] if single else outs)]

    def run(*args):
        out_spaces = [pltpu.VMEM] * (len(shapes) - far_outs) + [pltpu.HBM] * far_outs
        spaces = [pltpu.SMEM] * scalars + [pltpu.HBM] * far + [pltpu.VMEM] * (len(args) - scalars - far)
        args = [
            pltpu.with_memory_space_constraint(arg, pltpu.HBM) if space is pltpu.HBM else arg
            for arg, space in zip(args, spaces)
        ]
        got = pl.pallas_call(
            kernel,
            out_shape=shapes,
            in_specs=[pl.BlockSpec(memory_space=space) for space in spaces],
            out_specs=[pl.BlockSpec(memory_space=space) for space in out_spaces],
            scratch_shapes=[pltpu.VMEM(shape, dtype) for shape, dtype in scratch]
            + [pltpu.SemaphoreType.DMA((copies,))] * (copies > 0),
            compiler_params=pltpu.CompilerParams(vmem_limit_bytes=VMEM_LIMIT),
        )(*args)
        return got[0] if single else got

    return run


def exchange(values, axes):
    return lax.all_to_all(values, axes, 0, 0, tiled=True)


def shards(focus_start, onset, bins, refl_real, refl_imag):
    mats = (refl_real[0], refl_imag[0])
    where = jnp.stack([lax.axis_index(axis) for axis in ("x", ("v", "w"), "c", "z")]).astype(I32)
    bins = bins.reshape(1, NF)
    onset = onset.T
    forward, wide, inverse = base_tables()
    own = (POINTS, NI, NT)

    scratch = [((1, NF), I32), ((NI, POINTS), I32), (own, BF), ((NF, 2 * NT), BF), ((POINTS * NI + 8, NT), F32)]
    run = call(start_kernel, ((NA, 8, LANES), BF), scratch, far=4, copies=4)
    got = exchange(run(bins, onset, focus_start, wide), ("v", "w", "c"))
    outs = [((8, LANES), I32), ((TIMES + KEPT - CUT, LANES), BF), ((OWN_TIMES, 2 * NA), BF), ((2 * NG, CUT), BF), ((2 * NU, CUT), BF)]
    outs += [((POINTS * NI, LANES), I32), ((BLOCK, COLS), BF), ((BLOCK, COLS), BF)]
    scratch = [((1, NF), I32), ((NI, POINTS), I32), ((2 * NF, NT), BF), ((KEPT, LANES), BF)]
    run = call(tables_kernel, outs, scratch, scalars=1, far=6, copies=6)
    place, inv, own_inv, fwd, own_fwd, kept, *mats = run(where, bins, onset, forward, inverse, *mats)
    send = call(middle_kernel, ((NX, NZ, POINTS + 8, LANES), BF), [((8 * NA + 8, LANES), F32)])(got, fwd)
    got = exchange(send.reshape(NX * NZ, POINTS + 8, LANES), ("x", "z"))
    outs = [((NY, NC, 16, LANES), BF), ((2 * POINTS, COLS), BF), ((8, LANES), I32), ((8, LANES), I32)]
    scratch = [((NX * NZ * (POINTS + 8), LANES), F32)]
    send, first, own_marks, marks = call(first_conv_kernel, outs, scratch)(place, got, *mats)
    for step in range(ITERS):
        got = exchange(send.reshape(NA, 16, LANES), ("v", "w", "c"))
        scratch = [((NA * 16 + 16, LANES), F32), ((NU * 16 + 16, LANES), F32)]
        tables = (own_inv, own_fwd, own_marks)
        if step == ITERS - 1:
            scratch = scratch + [((NU * 8 + 8, LANES), F32)]
            send = call(last_time_kernel, ((NU, 24, LANES), BF), scratch)(got, *tables, place)
            got = exchange(send, ("x", "c", "w"))
            break
        send = call(time_kernel, ((NU, 16, LANES), BF), scratch)(got, *tables)
        got = exchange(send, ("x", "c", "w"))
        send = call(corr_kernel, ((NX * NZ, 16, LANES), BF), [((NX * NZ * 16 + 32, LANES), F32)])(got, *mats)
        got = exchange(send, ("x", "z"))
        send = call(sum_kernel, ((NY, NC, NX * 8, LANES), BF))(got)
        got = exchange(send.reshape(NA, NX * 8, LANES), ("v", "w", "c"))
        scratch = [((NF * 8 + 32, LANES), F32), ((NG * 8 + 8, LANES), F32)]
        send = call(time_copies_kernel, ((NG, NZ, 8, LANES), BF), scratch)(got, inv, fwd, marks)
        got = exchange(send.reshape(NG * NZ, 8, LANES), ("x", "c", "z"))
        scratch = [((NG * NZ * 8 + 64, LANES), F32), ((2 * POINTS * COLS // LANES + 16, LANES), F32)]
        send = call(next_conv_kernel, ((NY, NC, 16, LANES), BF), scratch)(got, first, *mats)
    tail = got
    send = call(last_corr_kernel, ((NX, NZ, POINTS, LANES), BF))(got, *mats)
    got = exchange(send.reshape(NX * NZ, POINTS, LANES), ("x", "z")).reshape(NX, NZ, POINTS, LANES)
    send = call(last_sum_kernel, ((NA, NX, LANES), BF))(got)
    got = exchange(send, ("v", "w", "c"))
    scratch = [(own, BF), (own, BF), ((POINTS * NI + 8, LANES), F32), ((NX * NA + 8, LANES), F32)]
    run = call(last_kernel, [(own, BF), (own, BF)], scratch, copies=2, far_outs=2)
    focus_plus, focus_minus = run(got, tail, inv, kept, focus_start)
    return (focus_plus, focus_minus)


def solution(mesh):
    fine = Mesh(mesh.devices.reshape(NX, NY // NW, NW, NC, NZ), ("x", "v", "w", "c", "z"))
    receivers = ("z", "x", "v", "w", "c")
    slabs = ("x", "v", "w", "c")
    return jax.shard_map(
        shards,
        mesh=fine,
        in_specs=(
            P(None, receivers, None),
            P(None, receivers),
            P(),
            P(slabs, "z", None),
            P(slabs, "z", None),
        ),
        out_specs=(P(None, receivers, None), P(None, receivers, None)),
        check_vma=False,
    )
```

```python
import math

import jax
import jax.numpy as jnp
import numpy as np
from jax import lax
from jax.experimental import pallas as pl
from jax.experimental.pallas import tpu as pltpu
from jax.sharding import Mesh
from jax.sharding import PartitionSpec as P

FLO = 8
ITERS = 2
NX, NY, NC, NZ = 4, 8, 2, 8
NW = 2
NA, NG, NI = NY * NC, NX * NC, 4
NU = NG * NW
NF, POINTS, NT = 64, 16, 1024
BLOCK, COLS = 256, 2048
LANES = 128
SPANS = ((128, 384), (640, 896), (0, 128), (896, 1024))
CUT = 512
KEPT = 768
TIMES = CUT + 2 * 2 * NG
OWN_TIMES = CUT + 2 * 2 * NU
ONSET_MID = 256
BF, F32, I32 = jnp.bfloat16, jnp.float32, jnp.int32
VMEM_LIMIT = 8 * 1024 * 1024


def base_tables():
    phase = (np.arange(NT)[None, :] * (FLO + np.arange(NF))[:, None]) % NT
    angle = phase.astype(np.float32) * np.float32(2.0 * math.pi / NT)
    rows = np.concatenate([np.cos(angle), -np.sin(angle)], axis=0)
    forward = (rows * np.float32(1.0 / math.sqrt(NT))).astype(BF)
    inverse = (rows * np.float32(math.sqrt(2.0 / NF))).astype(BF)
    inverse = np.concatenate([inverse[:, a:b] for a, b in SPANS], axis=1)
    return forward, np.ascontiguousarray(inverse.T)


def iota(shape, dim):
    return lax.broadcasted_iota(I32, shape, dim)


def grid(rows, cols):
    return iota((rows, cols), 0), iota((rows, cols), 1)


def hot(mask):
    return jnp.where(mask, jnp.float32(1), jnp.float32(0)).astype(BF)


def nn(a, b):
    return lax.dot_general(a, b, (((1,), (0,)), ((), ())), preferred_element_type=F32)


def nt(a, b):
    return lax.dot_general(a, b, (((1,), (1,)), ((), ())), preferred_element_type=F32)


def two_terms(value):
    high = value.astype(BF)
    return high, (value - high.astype(F32)).astype(BF)


def slab_of_bin(bins):
    row, _ = grid(NF, NF)
    return hot(row == bins)


def fetch(pairs, sems):
    copies = [pltpu.make_async_copy(src, dst, sems.at[n]) for n, (src, dst) in enumerate(pairs)]
    for copy in copies:
        copy.start()
    return copies


def start_kernel(bins_in, onset_in, focus_in, base_in, out, bins, onset, focus, base, flat, sems):
    copies = fetch([(focus_in, focus), (base_in, base), (bins_in, bins), (onset_in, onset)], sems)
    copies[2].wait()
    m, j = grid(8 * NA, NF)
    place = hot(((m & 7) < NX) & (j == ((m & 7) << 4) + (m >> 3)))
    order = nt(place, slab_of_bin(bins[...])).astype(BF)
    copies[3].wait()
    p, lane = grid(POINTS, LANES)
    spread = hot((((lane >> 2) & 15) == p) & ((lane >> 6) == (p >> 3)))
    marks = nn((onset[...] - ONSET_MID).astype(F32).astype(BF), spread)
    i, lane = grid(NI, LANES)
    marks = jnp.where((lane & 3) == i, marks, 0.0).sum(axis=0, keepdims=True)
    copies[0].wait()
    for p in range(POINTS):
        flat[NI * p : NI * (p + 1), :] = focus[p].astype(F32)
    rows = flat[: POINTS * NI, :].astype(BF)
    copies[1].wait()
    spec = nt(base[...], rows)
    spec = jnp.concatenate([spec[:NF], spec[NF:]], axis=1)
    sent = nn(order, spec.astype(BF))
    sent = jnp.where((iota((8 * NA, LANES), 0) & 7) == NX, marks, sent)
    out[...] = sent.reshape(NA, 8, LANES).astype(BF)


def tables_kernel(
    where, bins_in, onset_in, forward_in, inverse_in, re_in, im_in,
    place, inv, own_inv, fwd, own_fwd, own_marks, re, im,
    bins, onset, forward, inverse, sems,
):
    pairs = [(bins_in, bins), (onset_in, onset), (forward_in, forward), (inverse_in, inverse), (re_in, re), (im_in, im)]
    copies = fetch(pairs, sems)
    for copy in copies[:4]:
        copy.wait()
    row, _ = grid(8, LANES)
    value = jnp.zeros((8, LANES), I32)
    for n in range(4):
        value = jnp.where(row == n, where[n], value)
    place[...] = value
    held = bins[...].astype(F32).astype(BF)
    j, k = grid(NF, LANES)
    arrival = ((k >> 5) << 4) + (k & 15)
    at_k = nn(held, hot(j == arrival))
    j, n = grid(NF, 2 * NA)
    at_own = nn(held, hot(j == (where[0] << 4) + (n & 15)))
    row, k = grid(LANES, LANES)
    order = hot(((row >> 6) == ((k >> 4) & 1)) & ((row & 63).astype(F32) == at_k))
    row, n = grid(LANES, 2 * NA)
    own_order = hot(((row >> 6) == (n >> 4)) & ((row & 63).astype(F32) == at_own))
    base = inverse[...]
    table = nn(base, order).astype(BF)
    own_table = nn(base, own_order).astype(BF)
    holds = slab_of_bin(bins[...])
    m, j = grid(2 * NG, NF)
    slabs = hot(j == (((m & 7) >> 1) << 4) + (where[1] << 1) + (m & 1))
    m, j = grid(2 * NU, NF)
    own_slabs = hot(j == (((m & 15) >> 2) << 4) + ((where[1] >> 1) << 2) + ((m & 1) << 1) + ((m >> 1) & 1))
    inv[TIMES:] = table[CUT:]
    for to_inv, to_fwd, part, rows in ((inv, fwd, table, slabs), (own_inv, own_fwd, own_table, own_slabs)):
        count = rows.shape[0] // 2
        rows = nt(rows, holds)
        first = iota(rows.shape, 0) < count
        pick = jnp.concatenate([jnp.where(first, rows, 0.0), jnp.where(first, 0.0, rows)], axis=1).astype(BF)
        for n, (a, b) in enumerate(SPANS[:2]):
            to_fwd[:, BLOCK * n : BLOCK * (n + 1)] = nn(pick, forward[:, a:b]).astype(BF)
        picked = jnp.concatenate([nn(pick, forward[:, a:b]).astype(BF) for a, b in SPANS[2:]], axis=1)
        to_inv[:CUT] = part[:CUT]
        to_inv[CUT : CUT + 4 * count] = jnp.concatenate(two_terms(nn(picked, part[CUT:])), axis=0)
    m, p = grid(POINTS * NI, POINTS)
    marks = nt(hot((m >> 2) == p), (onset[...] - ONSET_MID).astype(F32).astype(BF))
    m, i = grid(POINTS * NI, NI)
    marks = jnp.where((m & 3) == i, marks, 0.0).sum(axis=1, keepdims=True)
    own_marks[...] = jnp.broadcast_to(marks, (POINTS * NI, LANES)).astype(I32) + ONSET_MID
    for copy in copies[4:]:
        copy.wait()


def middle_kernel(got, _, out, rows):
    rows[: 8 * NA, :] = got[...].astype(F32).reshape(8 * NA, LANES)
    line = jnp.concatenate([rows[pl.ds(e, NA, stride=8), :] for e in range(NX + 1)], axis=1).astype(BF)
    m, a = grid(NA * NI, NA)
    spread = nn(hot((m >> 2) == a), line)
    m, lane = grid(NA * NI, LANES)
    stacked = []
    for e in range(NX + 1):
        piece = spread[:, LANES * e : LANES * (e + 1)]
        for part in range(2):
            fits = ((lane & 3) == (m & 3)) & ((lane >> 6) == part)
            stacked.append(jnp.where(fits, piece, 0.0))
    stacked = jnp.concatenate(stacked, axis=0).astype(BF)
    p, lane = grid(POINTS, LANES)
    turned = nt(hot(((lane >> 2) & 15) == p), stacked)
    marks = turned[:8, LANES * NX :] + turned[8:, LANES * NX :]
    for x in range(NX):
        message = jnp.concatenate([turned[:, LANES * x : LANES * (x + 1)], marks], axis=0).astype(BF)
        for z in range(NZ):
            out[x, z] = message


def swap(a, b):
    low = iota(a.shape, 1) < LANES // 2
    return (
        jnp.where(low, a, pltpu.roll(b, LANES // 2, 1)),
        jnp.where(low, pltpu.roll(a, LANES // 2, 1), b),
    )


def convolve(src, mat_re, mat_im, out):
    a = nt(src, mat_re[...])
    b = nt(src, mat_im[...])
    parts = (a[:POINTS] - b[POINTS:], a[POINTS:] + b[:POINTS])
    for c in range(NC):
        at = slice(8 * c, 8 * (c + 1))
        for w in range(NW):
            slabs = [part[at, LANES * w : LANES * (w + 1)] for part in parts]
            message = jnp.concatenate(slabs, axis=0).astype(BF)
            for v in range(NY // NW):
                out[NW * v + w, c] = message


def first_conv_kernel(place, got, mat_re, mat_im, out, src, own_marks, marks, rows):
    height = POINTS + 8
    rows[...] = got[...].astype(F32).reshape(NX * NZ * height, LANES)
    for z in range(NZ):
        for half in range(2):
            a = rows[pl.ds((2 * half * NZ + z) * height, POINTS), :]
            b = rows[pl.ds(((2 * half + 1) * NZ + z) * height, POINTS), :]
            at = LANES * (2 * z + half)
            re, im = swap(a, b)
            src[:POINTS, at : at + LANES] = re.astype(BF)
            src[POINTS:, at : at + LANES] = im.astype(BF)
    x, y, c, z = (place[n : n + 1, :] for n in range(4))
    mine = (y & 1) + 2 * c
    own = jnp.zeros((8, LANES), F32)
    line, _ = grid(8, LANES)
    few = jnp.zeros((8, LANES), F32)
    p, _ = grid(POINTS, LANES)
    for half in range(2):
        a = b = jnp.zeros((8, LANES), F32)
        for n in range(NZ):
            at = (2 * half * NZ + n) * height + POINTS
            a = jnp.where(z == n, rows[at : at + 8, :], a)
            b = jnp.where(z == n, rows[at + NZ * height : at + NZ * height + 8, :], b)
        blocks = swap(a, b)
        for h in range(2):
            own = jnp.where(mine == half + 2 * h, blocks[h], own)
        blocks = jnp.concatenate(blocks, axis=0)
        for n in range(2):
            row = jnp.where(p == 4 * x + 2 * c + n, blocks, 0.0).sum(axis=0, keepdims=True)
            few = jnp.where(line == 2 * n + half, row, few)
    marks[...] = few.astype(I32) + ONSET_MID
    own_marks[...] = own.astype(I32) + ONSET_MID
    convolve(src[...], mat_re, mat_im, out)


def next_conv_kernel(got, first, mat_re, mat_im, out, rows, more):
    rows[: NG * NZ * 8, :] = got[...].astype(F32).reshape(NG * NZ * 8, LANES)
    for z in range(NZ):
        for p in range(2):
            for part in range(2):
                for half in range(2):
                    slab = rows[pl.ds(8 * z + 4 * p + 2 * part + half, NG, stride=8 * NZ), :]
                    more[pl.ds(2 * POINTS * (2 * z + half) + POINTS * part + p, NG, stride=2), :] = slab
    blocks = [more[2 * POINTS * n : 2 * POINTS * (n + 1), :] for n in range(COLS // LANES)]
    src = (first[...].astype(F32) + jnp.concatenate(blocks, axis=1)).astype(BF)
    convolve(src, mat_re, mat_im, out)


def window(spectra, marks, inv, fwd):
    t = iota((BLOCK, 1), 0)
    count = fwd.shape[0]
    front = jnp.where(t + SPANS[0][0] < marks, nn(inv[:BLOCK], spectra), 0.0).astype(BF)
    rest = nn(inv[BLOCK : CUT + 2 * count], spectra)
    back = jnp.where(t + SPANS[1][0] >= NT - marks, rest[:BLOCK], 0.0).astype(BF)
    fixed = rest[BLOCK : BLOCK + count] + rest[BLOCK + count :]
    return nn(fwd[:, :BLOCK], front) + nn(fwd[:, BLOCK:], back) + fixed


def window_slabs(got, inv, fwd, marks, rows, turn):
    rows[: NA * 16, :] = got[...].astype(F32).reshape(NA * 16, LANES)
    every = []
    for p in range(8):
        parts = [rows[pl.ds(8 * part + p, NA, stride=16), :] for part in range(2)]
        every.append(jnp.concatenate(parts, axis=0).astype(BF))
    mark = [marks[p : p + 1, :] for p in range(8)]
    spec = window(jnp.concatenate(every, axis=1), jnp.concatenate(mark, axis=1), inv, fwd)
    for p in range(8):
        for part in range(2):
            slab = spec[NU * part : NU * (part + 1), LANES * p : LANES * (p + 1)]
            turn[pl.ds(8 * part + p, NU, stride=16), :] = slab
    return every, turn[: NU * 16, :].reshape(NU, 16, LANES)


def time_kernel(got, inv, fwd, marks, out, rows, turn):
    out[...] = window_slabs(got, inv, fwd, marks, rows, turn)[1].astype(BF)


def last_time_kernel(got, inv, fwd, marks, place, out, rows, turn, tail):
    every, message = window_slabs(got, inv, fwd, marks, rows, turn)
    m, r = grid(NU * NI, LANES)
    y = place[1:2, :]
    w = y & 1
    y = (y & 6) + ((m >> 2) & 1)
    own = ((m >> 4) << 6) + (y << 3) + (((m >> 3) & 1) << 2) + (m & 3)
    own = hot(r + LANES * w == own)
    for h in range(2):
        taken = nt(own, jnp.concatenate(every[4 * h : 4 * (h + 1)], axis=0))
        for u in range(NU):
            tail[8 * u + NI * h : 8 * u + NI * (h + 1), :] = taken[NI * u : NI * (u + 1)]
    out[...] = jnp.concatenate([message, tail[: NU * 8, :].reshape(NU, 8, LANES)], axis=1).astype(BF)


def time_copies_kernel(got, inv, fwd, marks, out, rows, turn):
    rows[: NF * 8, :] = got[...].astype(F32).reshape(NF * 8, LANES)
    every = []
    for p in range(2):
        parts = []
        for x in range(NX):
            for part in range(2):
                at = [8 * x + 4 * p + 2 * part + half for half in range(2)]
                halves = [rows[pl.ds(n, NA, stride=8 * NX), :] for n in at]
                parts.append(jnp.concatenate(halves, axis=1))
        every.append(jnp.concatenate(parts, axis=0).astype(BF))
    mark = [marks[n : n + 1, :] for n in range(4)]
    spectra = window(jnp.concatenate(every, axis=1), jnp.concatenate(mark, axis=1), inv, fwd)
    for p in range(2):
        spec = spectra[:, BLOCK * p : BLOCK * (p + 1)]
        for part in range(2):
            for half in range(2):
                slab = spec[NG * part : NG * (part + 1), LANES * half : LANES * (half + 1)]
                turn[pl.ds(4 * p + 2 * part + half, NG, stride=8), :] = slab
    message = turn[: NG * 8, :].reshape(NG, 8, LANES).astype(BF)
    for z in range(NZ):
        out[:, z] = message


def correlate(got, mat_re, mat_im):
    parts = []
    for part in range(2):
        halves = []
        for half in range(2):
            at = 8 * part
            both = [sum(got[4 * x + 2 * c + half].astype(F32)[at : at + 8] for x in range(NX)) for c in range(NC)]
            halves.append(jnp.concatenate(both, axis=0))
        parts.append(jnp.concatenate(halves, axis=1))
    straight = jnp.concatenate(parts, axis=0).astype(BF)
    turned = jnp.concatenate([parts[1], -parts[0]], axis=0).astype(BF)
    for z in range(NZ):
        at = slice(BLOCK * z, BLOCK * (z + 1))
        yield z, nn(straight, mat_re[:, at]) + nn(turned, mat_im[:, at])


def corr_kernel(got, mat_re, mat_im, out, turn):
    for z, block in correlate(got, mat_re, mat_im):
        for x in range(NX):
            for part in range(2):
                for half in range(2):
                    at = (x * NZ + z) * 16 + 2 * part + half
                    row = POINTS * part + 4 * x
                    turn[pl.ds(at, 4, stride=4), :] = block[row : row + 4, LANES * half : LANES * (half + 1)]
    out[...] = turn[: NX * NZ * 16, :].reshape(NX * NZ, 16, LANES).astype(BF)


def last_corr_kernel(got, mat_re, mat_im, out):
    for z, block in correlate(got, mat_re, mat_im):
        for half in range(2):
            at = slice(LANES * half, LANES * (half + 1))
            a, b = swap(block[:POINTS, at], block[POINTS:, at])
            out[2 * half, z] = a.astype(BF)
            out[2 * half + 1, z] = b.astype(BF)


def sum_kernel(got, out):
    total = got[...].astype(F32).reshape(NX, NZ, 16, LANES).sum(axis=1)
    for c in range(NC):
        message = total[:, 8 * c : 8 * (c + 1)].reshape(NX * 8, LANES).astype(BF)
        for y in range(NY):
            out[y, c] = message


def last_sum_kernel(got, out):
    total = got[...].astype(F32).sum(axis=1).astype(BF)
    total = jnp.concatenate([total[x] for x in range(NX)], axis=1)
    m, p = grid(LANES, POINTS)
    turned = nn(hot(((m >> 2) & 15) == p), total)
    m, n = grid(LANES, NX * LANES)
    turned = jnp.where(((n & 3) == (m & 3)) & (((n >> 6) & 1) == (m >> 6)), turned, 0.0).astype(BF)
    m, n = grid(NX * NA, NX * LANES)
    sent = nt(hot(((m & 3) == (n >> 7)) & ((m >> 2) == ((n >> 2) & 15))), turned)
    for a in range(NA):
        out[a] = sent[NX * a : NX * (a + 1)].astype(BF)


def keep_own(spectra, inv, marks):
    t = iota((POINTS * NI, LANES), 1)
    trace = [nt(spectra, inv[a:b]) for a, b in ((0, CUT), (TIMES, TIMES + KEPT - CUT))]
    trace = jnp.concatenate(trace, axis=1)
    pieces = [trace[:, LANES * n : LANES * (n + 1)] for n in range(KEPT // LANES)]
    none = jnp.zeros_like(pieces[0])
    front = [jnp.where(t + SPANS[0][0] + LANES * n < marks, pieces[n], 0.0) for n in range(2)]
    back = [jnp.where(t + SPANS[1][0] + LANES * n >= NT - marks, pieces[2 + n], 0.0) for n in range(2)]
    return jnp.concatenate([pieces[4], *front, none, none, *back, pieces[5]], axis=1)


def last_kernel(got, tail, inv, marks, focus, plus_out, minus_out, plus, minus, spectra, arrived, sems):
    for a in range(NA):
        arrived[NX * a : NX * (a + 1), :] = got[a].astype(F32)
    rows = arrived[: NX * NA, :].T.astype(BF)
    m, k = grid(NX * NA, LANES)
    own = jnp.zeros((POINTS * NI, LANES), F32)
    for part in range(2):
        place = hot(k == ((m & 3) << 5) + 16 * part + (m >> 2))
        own = own + nn(rows[NF * part : NF * (part + 1)], place)
    trace = keep_own(own.astype(BF), inv[...], marks[...])
    for p in range(POINTS):
        plus[p] = (focus[p].astype(F32) + trace[NI * p : NI * (p + 1)]).astype(BF)
    first = pltpu.make_async_copy(plus, plus_out, sems.at[0])
    first.start()
    own = []
    for x in range(NX):
        both = [sum(tail[4 * x + 2 * c + w].astype(F32)[16:] for w in range(NW)) for c in range(NC)]
        own.append(jnp.concatenate(both, axis=0))
    own = jnp.concatenate(own, axis=1).astype(BF)
    n, k = grid(NX * LANES, LANES)
    same = (n >> 7) * 32 + (n & 31) == k
    own = [nn(own, hot(same & (((n >> 5) & 3) == p))) for p in range(4)]
    for p in range(POINTS):
        spectra[NI * p : NI * (p + 1), :] = own[p & 3][NI * (p >> 2) : NI * ((p >> 2) + 1)]
    trace = keep_own(spectra[: POINTS * NI, :].astype(BF), inv[...], marks[...])
    for p in range(POINTS):
        minus[p] = trace[NI * p : NI * (p + 1)].astype(BF)
    second = pltpu.make_async_copy(minus, minus_out, sems.at[1])
    second.start()
    first.wait()
    second.wait()


def call(kernel, outs, scratch=(), scalars=0, far=0, copies=0, far_outs=0):
    single = not isinstance(outs, list)
    shapes = [jax.ShapeDtypeStruct(shape, dtype) for shape, dtype in ([outs] if single else outs)]

    def run(*args):
        out_spaces = [pltpu.VMEM] * (len(shapes) - far_outs) + [pltpu.HBM] * far_outs
        spaces = [pltpu.SMEM] * scalars + [pltpu.HBM] * far + [pltpu.VMEM] * (len(args) - scalars - far)
        args = [
            pltpu.with_memory_space_constraint(arg, pltpu.HBM) if space is pltpu.HBM else arg
            for arg, space in zip(args, spaces)
        ]
        got = pl.pallas_call(
            kernel,
            out_shape=shapes,
            in_specs=[pl.BlockSpec(memory_space=space) for space in spaces],
            out_specs=[pl.BlockSpec(memory_space=space) for space in out_spaces],
            scratch_shapes=[pltpu.VMEM(shape, dtype) for shape, dtype in scratch]
            + [pltpu.SemaphoreType.DMA((copies,))] * (copies > 0),
            compiler_params=pltpu.CompilerParams(vmem_limit_bytes=VMEM_LIMIT),
        )(*args)
        return got[0] if single else got

    return run


def exchange(values, axes):
    return lax.all_to_all(values, axes, 0, 0, tiled=True)


def shards(focus_start, onset, bins, refl_real, refl_imag):
    mats = (refl_real[0], refl_imag[0])
    where = jnp.stack([lax.axis_index(axis) for axis in ("x", ("v", "w"), "c", "z")]).astype(I32)
    bins = bins.reshape(1, NF)
    onset = onset.T
    forward, inverse = base_tables()
    own = (POINTS, NI, NT)

    scratch = [((1, NF), I32), ((NI, POINTS), I32), (own, BF), ((2 * NF, NT), BF), ((POINTS * NI + 8, NT), F32)]
    run = call(start_kernel, ((NA, 8, LANES), BF), scratch, far=4, copies=4)
    got = exchange(run(bins, onset, focus_start, forward), ("v", "w", "c"))
    outs = [((8, LANES), I32), ((TIMES + KEPT - CUT, LANES), BF), ((OWN_TIMES, 2 * NA), BF), ((2 * NG, CUT), BF), ((2 * NU, CUT), BF)]
    outs += [((POINTS * NI, LANES), I32), ((BLOCK, COLS), BF), ((BLOCK, COLS), BF)]
    scratch = [((1, NF), I32), ((NI, POINTS), I32), ((2 * NF, NT), BF), ((KEPT, LANES), BF)]
    run = call(tables_kernel, outs, scratch, scalars=1, far=6, copies=6)
    place, inv, own_inv, fwd, own_fwd, kept, *mats = run(where, bins, onset, forward, inverse, *mats)
    send = call(middle_kernel, ((NX, NZ, POINTS + 8, LANES), BF), [((8 * NA + 8, LANES), F32)])(got, fwd)
    got = exchange(send.reshape(NX * NZ, POINTS + 8, LANES), ("x", "z"))
    outs = [((NY, NC, 16, LANES), BF), ((2 * POINTS, COLS), BF), ((8, LANES), I32), ((8, LANES), I32)]
    scratch = [((NX * NZ * (POINTS + 8), LANES), F32)]
    send, first, own_marks, marks = call(first_conv_kernel, outs, scratch)(place, got, *mats)
    for step in range(ITERS):
        got = exchange(send.reshape(NA, 16, LANES), ("v", "w", "c"))
        scratch = [((NA * 16 + 16, LANES), F32), ((NU * 16 + 16, LANES), F32)]
        tables = (own_inv, own_fwd, own_marks)
        if step == ITERS - 1:
            scratch = scratch + [((NU * 8 + 8, LANES), F32)]
            send = call(last_time_kernel, ((NU, 24, LANES), BF), scratch)(got, *tables, place)
            got = exchange(send, ("x", "c", "w"))
            break
        send = call(time_kernel, ((NU, 16, LANES), BF), scratch)(got, *tables)
        got = exchange(send, ("x", "c", "w"))
        send = call(corr_kernel, ((NX * NZ, 16, LANES), BF), [((NX * NZ * 16 + 32, LANES), F32)])(got, *mats)
        got = exchange(send, ("x", "z"))
        send = call(sum_kernel, ((NY, NC, NX * 8, LANES), BF))(got)
        got = exchange(send.reshape(NA, NX * 8, LANES), ("v", "w", "c"))
        scratch = [((NF * 8 + 32, LANES), F32), ((NG * 8 + 8, LANES), F32)]
        send = call(time_copies_kernel, ((NG, NZ, 8, LANES), BF), scratch)(got, inv, fwd, marks)
        got = exchange(send.reshape(NG * NZ, 8, LANES), ("x", "c", "z"))
        scratch = [((NG * NZ * 8 + 64, LANES), F32), ((2 * POINTS * COLS // LANES + 16, LANES), F32)]
        send = call(next_conv_kernel, ((NY, NC, 16, LANES), BF), scratch)(got, first, *mats)
    tail = got
    send = call(last_corr_kernel, ((NX, NZ, POINTS, LANES), BF))(got, *mats)
    got = exchange(send.reshape(NX * NZ, POINTS, LANES), ("x", "z")).reshape(NX, NZ, POINTS, LANES)
    send = call(last_sum_kernel, ((NA, NX, LANES), BF))(got)
    got = exchange(send, ("v", "w", "c"))
    scratch = [(own, BF), (own, BF), ((POINTS * NI + 8, LANES), F32), ((NX * NA + 8, LANES), F32)]
    run = call(last_kernel, [(own, BF), (own, BF)], scratch, copies=2, far_outs=2)
    focus_plus, focus_minus = run(got, tail, inv, kept, focus_start)
    return (focus_plus, focus_minus)


def solution(mesh):
    fine = Mesh(mesh.devices.reshape(NX, NY // NW, NW, NC, NZ), ("x", "v", "w", "c", "z"))
    receivers = ("z", "x", "v", "w", "c")
    slabs = ("x", "v", "w", "c")
    return jax.shard_map(
        shards,
        mesh=fine,
        in_specs=(
            P(None, receivers, None),
            P(None, receivers),
            P(),
            P(slabs, "z", None),
            P(slabs, "z", None),
        ),
        out_specs=(P(None, receivers, None), P(None, receivers, None)),
        check_vma=False,
    )
```
